32 devices in a mesh: grp: 8 (over z, x), exp: 4 (over y, core).
Axes of the slice: x: 2, y: 2, z: 4, core: 2. Of those that a mesh axis runs over, the one named last changes fastest.
Arguments:
- tokens: bfloat16 [24576, 1536], P(('grp', 'exp')), may hold values from -6 to 6
- cotangent: bfloat16 [24576, 1536], P(('grp', 'exp')), may hold values from -6 to 6
- gate_logits: float32 [24576, 4], P(('grp', 'exp')), may hold values from -3 to 3
- routes: int32 [24576, 4], P(('grp', 'exp')), may hold values from 0 to 31, all different within a row; in each aligned block of 768 rows (0 to 767, 768 to 1535, ...) at most 112 rows name the same one
- piece_starts: int32 [32, 3], P(('grp', 'exp')), may hold values from 0 to 768, as said below
- piece_kinds: int32 [32, 3], P(('grp', 'exp')), may hold values from 0 to 1, as said below
- q_weight: bfloat16 [1536, 1536], P('grp'), may hold values from -0.15625 to 0.15625
- k_weight: bfloat16 [1536, 256], P('grp'), may hold values from -0.15625 to 0.15625
- v_weight: bfloat16 [1536, 256], P('grp'), may hold values from -0.15625 to 0.15625
- o_weight: bfloat16 [1536, 1536], P('grp'), may hold values from -1.25 to 1.25
- attn_gain: bfloat16 [1536], P('grp'), may hold values from 0.25 to 1.75
- moe_gain: bfloat16 [1536], P('grp'), may hold values from 0.25 to 1.75
- gate_weight: bfloat16 [32, 1536, 768], P('exp'), may hold values from -0.15625 to 0.15625
- up_weight: bfloat16 [32, 1536, 768], P('exp'), may hold values from -0.15625 to 0.15625
- down_weight: bfloat16 [32, 1536, 768], P('exp'), may hold values from -0.4375 to 0.4375
Outputs:
- layer_out: bfloat16 [24576, 1536], P(('grp', 'exp'))
- tokens_grad: bfloat16 [24576, 1536], P(('grp', 'exp'))
- logits_grad: float32 [24576, 4], P(('grp', 'exp'))
- q_grad: float32 [1536, 1536], P(('grp', 'exp'))
- k_grad: float32 [1536, 256], P(('grp', 'exp'))
- v_grad: float32 [1536, 256], P(('grp', 'exp'))
- o_grad: float32 [1536, 1536], P(('grp', 'exp'))
- attn_gain_grad: float32 [1536], P(('grp', 'exp'))
- moe_gain_grad: float32 [1536], P(('grp', 'exp'))
- gate_grad: float32 [32, 1536, 768], P('exp', 'grp')
- up_grad: float32 [32, 1536, 768], P('exp', 'grp')
- down_grad: float32 [32, 1536, 768], P('exp', 'grp')
The draws below stay inside these ranges and needn't reach their ends.
Inputs may be any that keep to these rules, and one draw needn't show every extreme that they name: `routes`: each token names 4 different experts. Among the 768 tokens of one sequence at most 112 assignments go to one expert, and in some sequence some expert gets exactly 112. `piece_starts`: in each sequence the pieces begin at these positions in order, the first at 0, never falling; a piece runs to the next start or to the sequence's end, and equal starts leave a piece empty. `piece_kinds`: A piece of kind 1 spans exactly 256 positions; each sequence has at least one piece of kind 0.
All inputs are finite; a program needn't handle non-finite values.
Results may differ from the reference program's by a relative error of at most 0.015.
Values may be sent and summed in bfloat16 or wider, within the bound.
A program may use at most 448 MiB of HBM per device.

```python
import math
import jax
import jax.numpy as jnp
import numpy as np
from jax import lax

D = 1536
HEADS = 12
KV_HEADS = 2
HEAD_DIM = 128
EXPERTS = 32
FF = 768
TOP = 4
TOK_DEV = 768
PIC = 256
PIECES = 3
CAP = 112
SEQS = 32
TOKENS = 24576


def piece_layout(key):
    kinds = jax.random.randint(jax.random.fold_in(key, 11), (SEQS, PIECES), 0, 2)
    forced = jax.random.randint(jax.random.fold_in(key, 12), (SEQS, 1), 0, PIECES)
    slot_ids = jnp.arange(PIECES, dtype=jnp.int32)[None, :]
    kinds = jnp.where(slot_ids == forced, 0, kinds).astype(jnp.int32)
    shares = jax.random.randint(jax.random.fold_in(key, 13), (SEQS, PIECES), 1, 64)
    text_share = jnp.where(kinds == 0, shares, 0)
    spare = TOK_DEV - PIC * jnp.sum(kinds, axis=1, keepdims=True)
    text_len = spare * text_share // jnp.sum(text_share, axis=1, keepdims=True)
    last_text = jnp.max(jnp.where(kinds == 0, slot_ids, -1), axis=1, keepdims=True)
    remain = spare - jnp.sum(text_len, axis=1, keepdims=True)
    text_len = text_len + jnp.where(slot_ids == last_text, remain, 0)
    lengths = jnp.where(kinds == 1, PIC, text_len)
    starts = jnp.cumsum(lengths, axis=1) - lengths
    return (starts.astype(jnp.int32), kinds)


def draw_piece_starts(key, part):
    layout = piece_layout(key)
    return layout[0]


def draw_piece_kinds(key, part):
    layout = piece_layout(key)
    return layout[1]


def levels(key, shape, cuts, low, high):
    gain = 1.0
    for axis_at, parts in cuts:
        heights = jax.random.uniform(jax.random.fold_in(jax.random.fold_in(key, 6), axis_at), (parts,), jnp.float32, low / len(cuts), high / len(cuts))
        gain = gain * jnp.repeat(jnp.exp(heights), shape[axis_at] // parts).reshape((-1,) + (1,) * (len(shape) - 1 - axis_at))
    return gain


def routed_block(rng, own, number, rows, count, top, limit, lean):
    ranking = jax.random.permutation(rng, count)
    heavy_load, usual = portions_of(count, rows * top, limit, lean, True), portions_of(count, rows * top, limit, lean, False)
    places = jnp.arange(count)

    def named(sizes, rotation):
        used = int((sizes > 0).sum())
        fixed = max(1, used // 4)
        shifted = fixed + (places - fixed + rotation * (used - fixed)) % max(1, count - fixed)
        return jnp.zeros((count,), jnp.int32).at[ranking[jnp.where(places < fixed, places, shifted)]].set(jnp.asarray(sizes, jnp.int32))

    sizes = jnp.where(number % 4 == 0, named(heavy_load, number // 4), named(usual, number - number // 4 - 1))
    mixed = jax.random.permutation(jax.random.fold_in(own, 3), count)
    donor, sink = mixed[0:count // 2 * 2:2], mixed[1:count // 2 * 2:2]
    slack = jnp.minimum(sizes[donor] - 1, limit - sizes[sink]) // 2
    slack = jnp.where((donor == ranking[0]) | (sink == ranking[0]) | (sizes[sink] == 0), 0, jnp.maximum(slack, 0))
    shifted = jax.random.randint(jax.random.fold_in(own, 4), (count // 2,), 0, 1 << 20) % (slack + 1)
    sizes = sizes.at[donor].add(-shifted).at[sink].add(shifted)
    members = jnp.searchsorted(jnp.cumsum(sizes), jnp.arange(rows * top), side="right").astype(jnp.int32)
    table = members.reshape(top, rows).T
    table = table[jax.random.permutation(jax.random.fold_in(own, 1), rows)]
    rotation = jax.random.randint(jax.random.fold_in(own, 2), (rows, 1), 0, top)
    return jnp.take_along_axis(table, (jnp.arange(top)[None, :] + rotation) % top, axis=1)


def portions_of(count, total, limit, skew, full):
    loads = [(1 << 20) // math.isqrt(standing ** skew) + 1 for standing in range(1, count + 1)]
    largest = limit if full else min(limit, max(-(-total // count), total * loads[0] // sum(loads)))
    least = 1 if total - largest >= count - 1 else 0
    counts, rest = [largest] + [least] * (count - 1), total - largest - least * (count - 1)
    while rest > 0:
        free = [i for i in range(1, count) if counts[i] < largest] or [i for i in range(1, count) if counts[i] < limit]
        whole, left = sum([loads[i] for i in free]), rest
        for i in free:
            addition = min(limit - counts[i], max(1, left * loads[i] // whole), rest)
            counts[i] = counts[i] + addition
            rest = rest - addition
    return np.array(counts)


def centred(key, dims, spread, bound, cuts=(), held_as=jnp.bfloat16):
    entries = jax.random.normal(key, dims, jnp.float32) * spread
    if len(cuts) > 0:
        entries = levels(key, dims, cuts, -0.22, 0.18) * entries
    return jnp.clip(entries, min=-bound, max=bound).astype(held_as)


def setup_inputs(seed: int = 0) -> dict:
    key_of = jax.random.split(jax.random.key(seed), 16)
    tokens = centred(key_of[0], (TOKENS, D), 1.0, 6.0, ((0, 32),))
    cotangent = centred(key_of[1], (TOKENS, D), 1.0, 6.0, ((0, 32),))
    gate_logits = centred(key_of[2], (TOKENS, TOP), 0.5, 3.0, ((0, 32),), jnp.float32)
    routes_keys = jax.random.split(jax.random.fold_in(key_of[3], 1), TOKENS // TOK_DEV)
    routes_turns = jax.random.permutation(jax.random.fold_in(key_of[3], 3), TOKENS // TOK_DEV)
    routes = jax.vmap(lambda own, number: routed_block(jax.random.fold_in(key_of[3], 2), own, number, TOK_DEV, EXPERTS, TOP, CAP, 1))(routes_keys, routes_turns).reshape((TOKENS, TOP))
    piece_starts = draw_piece_starts(jax.random.fold_in(key_of[15], 71), 0)
    piece_kinds = draw_piece_kinds(jax.random.fold_in(key_of[15], 71), 0)
    q_weight = centred(key_of[6], (D, HEADS * HEAD_DIM), D ** -0.5, 0.15625, ((0, 8),))
    k_weight = centred(key_of[7], (D, KV_HEADS * HEAD_DIM), D ** -0.5, 0.15625, ((0, 8),))
    v_weight = centred(key_of[8], (D, KV_HEADS * HEAD_DIM), D ** -0.5, 0.15625, ((0, 8),))
    o_weight = centred(key_of[9], (HEADS * HEAD_DIM, D), (D // 64) ** -0.5, 1.25, ((0, 8),))
    attn_gain = jnp.clip(1.0 + 0.15 * jax.random.normal(key_of[10], (D,), jnp.float32), 0.25, 1.75).astype(jnp.bfloat16)
    moe_gain = jnp.clip(1.0 + 0.15 * jax.random.normal(key_of[11], (D,), jnp.float32), 0.25, 1.75).astype(jnp.bfloat16)
    gate_weight = centred(key_of[12], (EXPERTS, D, FF), D ** -0.5, 0.15625, ((0, 4),))
    up_weight = centred(key_of[13], (EXPERTS, D, FF), D ** -0.5, 0.15625, ((0, 4),))
    down_weight = centred(key_of[14], (EXPERTS, D, FF), (FF // 4) ** -0.5, 0.4375, ((0, 4),))
    return {"tokens": tokens, "cotangent": cotangent, "gate_logits": gate_logits, "routes": routes, "piece_starts": piece_starts, "piece_kinds": piece_kinds, "q_weight": q_weight, "k_weight": k_weight, "v_weight": v_weight, "o_weight": o_weight, "attn_gain": attn_gain, "moe_gain": moe_gain, "gate_weight": gate_weight, "up_weight": up_weight, "down_weight": down_weight}


@jax.custom_vjp
def low(v):
    return lax.optimization_barrier(v.astype(jnp.bfloat16)).astype(jnp.float32)

@jax.custom_vjp
def low_back(v):
    return v

def low_keep(v):
    return (low(v), None)

def low_pass(kept, grad):
    return (grad,)

def back_keep(v):
    return (v, None)

def back_low(kept, grad):
    return (low(grad),)
low.defvjp(low_keep, low_pass)
low_back.defvjp(back_keep, back_low)
EPSILON = 1e-06
THETA = 1000000.0
HIGHEST = lax.Precision.HIGHEST

def rms_norm(values, gain_vec):
    inverse = lax.rsqrt(lax.optimization_barrier(jnp.mean(values * values, axis=-1, keepdims=True)) + EPSILON)
    return values * inverse * gain_vec

def rope_tables(length, head_width):
    half_width = head_width // 2
    frequency = THETA ** (-2.0 * jnp.arange(half_width, dtype=jnp.float32) / head_width)
    angles = jnp.arange(length, dtype=jnp.float32)[:, None] * frequency[None, :]
    cosine = jnp.concatenate([jnp.cos(angles), jnp.cos(angles)], axis=-1)[:, None, :]
    sine_part = jnp.concatenate([jnp.sin(angles), jnp.sin(angles)], axis=-1)[:, None, :]
    return (cosine, sine_part)

def rotate(values, cosine, sine_part):
    half_width = values.shape[-1] // 2
    turned = jnp.concatenate([-values[..., half_width:], values[..., :half_width]], axis=-1)
    return values * cosine + turned * sine_part

def piece_visible(starts, kinds, length):
    places = jnp.arange(length, dtype=jnp.int32)
    piece_of = lax.optimization_barrier(jnp.sum((places[:, None] >= starts[None, :]).astype(jnp.int32), axis=1)) - 1
    slot_ids = jnp.arange(starts.shape[0], dtype=jnp.int32)
    kind_of = lax.optimization_barrier(jnp.sum(jnp.where(piece_of[:, None] == slot_ids[None, :], kinds[None, :], 0), axis=1))
    inside = (piece_of[:, None] == piece_of[None, :]) & (kind_of[:, None] == 1)
    return (places[None, :] <= places[:, None]) | inside

def slot_positions(routes):
    chosen = routes.reshape(-1).astype(jnp.int32)
    onehot = (chosen[:, None] == jnp.arange(EXPERTS, dtype=jnp.int32)[None, :]).astype(jnp.int32)
    earlier = jnp.cumsum(onehot, axis=0) - onehot
    return chosen * CAP + lax.optimization_barrier(jnp.sum(earlier * onehot, axis=1))

def block_forward(x_rows, logits, routes, starts, kinds, wq, wk, wv, wo, gain_one, gain_two, wgate, wup, wdown):
    length = x_rows.shape[0]
    group_size = HEADS // KV_HEADS
    score_scale = HEAD_DIM ** (-0.5)
    normed = low(rms_norm(x_rows, gain_one))
    query = low_back(jnp.dot(normed, wq, precision=HIGHEST)).reshape(length, HEADS, HEAD_DIM)
    key_lin = low_back(jnp.dot(normed, wk, precision=HIGHEST)).reshape(length, KV_HEADS, HEAD_DIM)
    value_rows = low_back(low(jnp.dot(normed, wv, precision=HIGHEST))).reshape(length, KV_HEADS, HEAD_DIM)
    cosine, sine_part = rope_tables(length, HEAD_DIM)
    query_rot = low(rotate(query, cosine, sine_part)).reshape(length, KV_HEADS, group_size, HEAD_DIM)
    key_rot = low(rotate(key_lin, cosine, sine_part))
    scores = low_back(jnp.einsum('qkgd,skd->kgqs', query_rot, key_rot, precision=HIGHEST) * score_scale)
    visible = piece_visible(starts, kinds, length)
    scores = jnp.where(visible[None, None], scores, -1e+30)
    row_max = lax.optimization_barrier(jnp.max(scores, axis=-1, keepdims=True))
    weights = jnp.exp(scores - row_max)
    attn_probs = low(weights / lax.optimization_barrier(jnp.sum(weights, axis=-1, keepdims=True)))
    mixed = jnp.einsum('kgqs,skd->qkgd', attn_probs, value_rows, precision=HIGHEST).reshape(length, HEADS * HEAD_DIM)
    mixed = low_back(low(mixed))
    branch = low_back(jnp.dot(mixed, wo, precision=HIGHEST))
    hidden = x_rows + branch
    normed_two = low(rms_norm(hidden, gain_two))
    positions = slot_positions(routes)
    copies = jnp.repeat(normed_two, TOP, axis=0)
    buffer = jnp.zeros((EXPERTS * CAP, D), jnp.float32).at[positions].add(copies)
    buffer = low_back(buffer.reshape(EXPERTS, CAP, D))
    gate_in = low_back(jnp.einsum('ecd,edf->ecf', buffer, wgate, precision=HIGHEST))
    up_in = low_back(jnp.einsum('ecd,edf->ecf', buffer, wup, precision=HIGHEST))
    act = low(jax.nn.silu(gate_in) * up_in)
    expert_out = low_back(low(jnp.einsum('ecf,edf->ecd', act, wdown, precision=HIGHEST)))
    back_rows = expert_out.reshape(EXPERTS * CAP, D)[positions].reshape(length, TOP, D)
    gates = jax.nn.softmax(logits, axis=-1)
    return hidden + lax.optimization_barrier(jnp.sum(gates[:, :, None] * back_rows, axis=1))

def reference(tokens, cotangent, gate_logits, routes, piece_starts, piece_kinds, q_weight, k_weight, v_weight, o_weight, attn_gain, moe_gain, gate_weight, up_weight, down_weight):
    floats = tuple((arr.astype(jnp.float32) for arr in (tokens, gate_logits, q_weight, k_weight, v_weight, o_weight, attn_gain, moe_gain, gate_weight, up_weight, down_weight)))
    checked = jax.checkpoint(block_forward)

    def forward(x_all, logits_all, wq, wk, wv, wo, gain_one, gain_two, wgate, wup, wdown):

        def one_seq(pieces):
            x_rows, logits, route_rows, starts, kinds = pieces
            return checked(x_rows, logits, route_rows, starts, kinds, wq, wk, wv, wo, gain_one, gain_two, wgate, wup, wdown)
        outs = lax.map(one_seq, (x_all.reshape(SEQS, TOK_DEV, D), logits_all.reshape(SEQS, TOK_DEV, TOP), routes.reshape(SEQS, TOK_DEV, TOP), piece_starts, piece_kinds))
        return outs.reshape(TOKENS, D)
    result, pullback = jax.vjp(forward, *floats)
    grads = pullback(cotangent.astype(jnp.float32))
    return (result.astype(jnp.bfloat16), grads[0].astype(jnp.bfloat16), grads[1], grads[2], grads[3], grads[4], grads[5], grads[6], grads[7], grads[8], grads[9], grads[10])
```

```python
import functools

import jax
import jax.numpy as jnp
from jax import lax
from jax.experimental import pallas as pl
from jax.experimental.pallas import tpu as pltpu
from jax.sharding import PartitionSpec as P

HEADS = 12
KV_HEADS = 2
HEAD_DIM = 128
EXPERTS = 32
TOP = 4
CAP = 112
EPSILON = 1e-06
THETA = 1000000.0
SCALE = HEAD_DIM ** (-0.5)
CORE = 1
PAIR = 2
VMEM = 58 * 1024 * 1024
BF16 = jnp.bfloat16
F32 = jnp.float32


class Flow:
    def __init__(self):
        self.last = None

    def after(self, *arrays):
        if self.last is None:
            return arrays if len(arrays) > 1 else arrays[0]
        out = lax.optimization_barrier(tuple(arrays) + (self.last,))[:-1]
        return out if len(out) > 1 else out[0]

    def mark(self, value):
        self.last = value
        return value


def swap(values, axis, bit):
    size = lax.axis_size(axis)
    return lax.ppermute(values, axis, [(i, i ^ bit) for i in range(size)])


def bits_of(size):
    return [1 << i for i in range(size.bit_length() - 1)]


def bit_at(index, bit):
    return (index // bit) % 2


def rope_tables(length):
    half = HEAD_DIM // 2
    frequency = THETA ** (-2.0 * jnp.arange(half, dtype=F32) / HEAD_DIM)
    angles = jnp.arange(length, dtype=F32)[:, None] * frequency[None, :]
    cosine, sine = jnp.cos(angles), jnp.sin(angles)
    return jnp.concatenate([cosine, cosine], axis=-1), jnp.concatenate([-sine, sine], axis=-1)


def piece_tags(starts, kinds, length):
    places = jnp.arange(length, dtype=jnp.int32)
    piece_of = jnp.sum((places[:, None] >= starts[None, :]).astype(jnp.int32), axis=1) - 1
    slot_ids = jnp.arange(starts.shape[0], dtype=jnp.int32)
    kind_of = jnp.sum(jnp.where(piece_of[:, None] == slot_ids[None, :], kinds[None, :], 0), axis=1)
    return jnp.where(kind_of == 1, piece_of + 1, 0)


def call(body, **kw):
    params = pltpu.CompilerParams(vmem_limit_bytes=VMEM)
    cost = pl.CostEstimate(flops=1, bytes_accessed=1, transcendentals=0)
    return pl.pallas_call(body, compiler_params=params, cost_estimate=cost, **kw)


def shape(*dims, dtype=BF16):
    return jax.ShapeDtypeStruct(dims, dtype)


def dot(a, b, ca=1, cb=0):
    return lax.dot_general(a, b, (((ca,), (cb,)), ((), ())), preferred_element_type=F32)


ANY = pl.BlockSpec(memory_space=pl.ANY)
WHOLE = pl.BlockSpec(memory_space=pltpu.VMEM)
SCALAR = pl.BlockSpec(memory_space=pltpu.SMEM)


def fixed(*dims):
    return pl.BlockSpec(dims, lambda *_: (0,) * len(dims))


def attend_body(
    x_ref, gain_ref, wq_ref, wk_ref, wv_ref, cos_ref, sin_ref, tagc_ref, tagr_ref,
    n1_ref, inv_ref, qr_ref, kr_ref, v_ref, mix_ref, lse_ref,
    mask_ref,
):
    step = pl.program_id(0)
    length = x_ref.shape[0]
    block = 256
    pairs_per_group = pl.num_programs(0) // KV_HEADS

    @pl.when(step == 0)
    def _():
        for r in range(0, length, block):
            x = x_ref[r : r + block].astype(F32)
            inverse = lax.rsqrt(jnp.mean(x * x, axis=-1, keepdims=True) + EPSILON)
            inv_ref[r : r + block] = inverse
            n1_ref[r : r + block] = (x * inverse * gain_ref[...]).astype(BF16)
            row = lax.broadcasted_iota(jnp.int32, (block, length), 0) + r
            col = lax.broadcasted_iota(jnp.int32, (block, length), 1)
            tag = tagc_ref[r : r + block]
            inside = (tag == tagr_ref[...]) & (tag > 0)
            mask_ref[r : r + block] = jnp.where((col <= row) | inside, 0.0, -1e30)

    def turn(u):
        return u * cos_ref[...] + pltpu.roll(u, HEAD_DIM // 2, 1) * sin_ref[...]

    @pl.when(step % pairs_per_group == 0)
    def _():
        kr_ref[...] = turn(dot(n1_ref[...], wk_ref[...])).astype(BF16)
        v_ref[...] = dot(n1_ref[...], wv_ref[...]).astype(BF16)

    q2 = dot(n1_ref[...], wq_ref[...])
    for h in range(2):
        cols = slice(h * HEAD_DIM, (h + 1) * HEAD_DIM)
        qr_ref[:, cols] = turn(q2[:, cols]).astype(BF16)
        for r in range(0, length, block):
            keys = min(length, r + 2 * block)
            s = dot(qr_ref[r : r + block, cols], kr_ref[:keys], 1, 1) * SCALE
            s = s + mask_ref[r : r + block, :keys]
            top = jnp.max(s, axis=-1, keepdims=True)
            e = jnp.exp(s - top)
            total = jnp.sum(e, axis=-1, keepdims=True)
            p = (e * (1.0 / total)).astype(BF16)
            mix_ref[r : r + block, cols] = dot(p, v_ref[:keys]).astype(BF16)
            lse_ref[h, r : r + block] = top + jnp.log(total)


def attend(x, gain, w, cosine, sine, tagc, tagr):
    length, width = x.shape
    pairs = HEADS // 2
    per = pairs // KV_HEADS
    q_blocks = HEADS
    return call(
        attend_body,
        grid=(pairs,),
        in_specs=[
            fixed(length, width),
            fixed(1, width),
            pl.BlockSpec((width, 2 * HEAD_DIM), lambda p: (0, p)),
            pl.BlockSpec((width, HEAD_DIM), lambda p: (0, q_blocks + p // per)),
            pl.BlockSpec((width, HEAD_DIM), lambda p: (0, q_blocks + KV_HEADS + p // per)),
            fixed(length, HEAD_DIM),
            fixed(length, HEAD_DIM),
            fixed(length, 1),
            fixed(1, length),
        ],
        out_specs=[
            fixed(length, width),
            fixed(length, 1),
            pl.BlockSpec((length, 2 * HEAD_DIM), lambda p: (0, p)),
            pl.BlockSpec((length, HEAD_DIM), lambda p: (0, p // per)),
            pl.BlockSpec((length, HEAD_DIM), lambda p: (0, p // per)),
            pl.BlockSpec((length, 2 * HEAD_DIM), lambda p: (0, p)),
            pl.BlockSpec((2, length, 1), lambda p: (p, 0, 0)),
        ],
        out_shape=[
            shape(length, width),
            shape(length, 1, dtype=F32),
            shape(length, HEADS * HEAD_DIM),
            shape(length, KV_HEADS * HEAD_DIM),
            shape(length, KV_HEADS * HEAD_DIM),
            shape(length, HEADS * HEAD_DIM),
            shape(HEADS, length, 1, dtype=F32),
        ],
        scratch_shapes=[pltpu.VMEM((length, length), F32)],
        name="attend",
    )(x, gain, w, w, w, cosine, sine, tagc, tagr)


def project_body(x_ref, mix_ref, wo_ref, gain_ref, hid_ref, n2_ref, inv_ref):
    rows = x_ref.shape[0]
    block = rows // 2
    for r in range(0, rows, block):
        h = x_ref[r : r + block].astype(F32) + dot(mix_ref[r : r + block], wo_ref[...])
        inverse = lax.rsqrt(jnp.mean(h * h, axis=-1, keepdims=True) + EPSILON)
        hid_ref[r : r + block] = h
        inv_ref[r : r + block] = inverse
        n2_ref[r : r + block] = (h * inverse * gain_ref[...]).astype(BF16)


def project(x, mixed, wo, gain):
    length, width = x.shape
    inner = mixed.shape[1]
    steps = 2
    rows = length // steps
    by_row = pl.BlockSpec((rows, width), lambda i: (i, 0))
    return call(
        project_body,
        grid=(steps,),
        in_specs=[by_row, pl.BlockSpec((rows, inner), lambda i: (i, 0)), fixed(inner, width), fixed(1, width)],
        out_specs=[by_row, by_row, pl.BlockSpec((rows, 1), lambda i: (i, 0))],
        out_shape=[shape(length, width, dtype=F32), shape(length, width), shape(length, 1, dtype=F32)],
        name="project",
    )(x, mixed, wo, gain)


def hot_rows(rank, s, local, length):
    spot = lax.broadcasted_iota(jnp.int32, (CAP, length), 0)
    picked = rank[s]
    return jnp.concatenate(
        [(picked[e : e + 1] == spot).astype(F32).astype(BF16) for e in range(local)], axis=0
    )


def collect_body(counts, local, rank_ref, *refs):
    total, count = sum(counts), len(counts)
    out_ref, in_buf, out_buf, in_sem, out_sem = refs[total:]
    items, at = [], 0
    for parts in counts:
        items.append(refs[at : at + parts])
        at += parts
    length, width = in_buf.shape[1:]
    half = length // 2
    chunk = 512

    def fetch(i, slot):
        parts = items[i] if len(items[i]) == 2 else [items[i][0].at[pl.ds(p * half, half)] for p in range(2)]
        for p in range(2):
            pltpu.make_async_copy(parts[p], in_buf.at[slot, pl.ds(p * half, half)], in_sem.at[slot, p]).start()

    def leaving(s, slot, e):
        return pltpu.make_async_copy(
            out_buf.at[slot, pl.ds(e * CAP, CAP)],
            out_ref.at[e, pl.ds(pl.multiple_of(s * CAP, 16), CAP)],
            out_sem.at[slot, e],
        )

    fetch(0, 0)

    def body(s, carry):
        slot = s % 2
        for i in range(1, count):
            @pl.when(s + 1 == i)
            def _():
                fetch(i, i % 2)

        for p in range(2):
            rows = in_buf.at[slot, pl.ds(p * half, half)]
            pltpu.make_async_copy(rows, rows, in_sem.at[slot, p]).wait()

        @pl.when(s >= 2)
        def _():
            for e in range(local):
                leaving(s - 2, slot, e).wait()

        hot = hot_rows(rank_ref, s, local, length)
        for c in range(0, width, chunk):
            out_buf[slot, :, c : c + chunk] = dot(hot, in_buf[slot, :, c : c + chunk]).astype(BF16)
        for e in range(local):
            leaving(s, slot, e).start()
        return carry

    lax.fori_loop(0, count, body, 0)
    for s in (count - 2, count - 1):
        for e in range(local):
            leaving(s, s % 2, e).wait()


def collect(rank, items):
    count, local, length = rank.shape
    width = items[0][0].shape[1]
    counts = [len(item) for item in items]
    return call(
        functools.partial(collect_body, counts, local),
        in_specs=[WHOLE] + [ANY] * sum(counts),
        out_specs=ANY,
        out_shape=shape(local, count * CAP, width),
        scratch_shapes=[
            pltpu.VMEM((2, length, width), BF16),
            pltpu.VMEM((2, local * CAP, width), BF16),
            pltpu.SemaphoreType.DMA((2, 2)),
            pltpu.SemaphoreType.DMA((2, local)),
        ],
        name="collect",
    )(rank, *[part for item in items for part in item])


def combine_body(count, local, *refs):
    rank_ref = refs[0]
    far, near, in_buf, out_buf, in_sem, out_sem = refs[-6:]
    rows = refs[1:-6]
    rows = rows if len(rows) == local else [rows[0].at[e] for e in range(local)]
    length, width = out_buf.shape[1:]
    chunk = 512
    first = count // 2

    def coming(s, slot, e):
        return pltpu.make_async_copy(
            rows[e].at[pl.ds(pl.multiple_of(s * CAP, 16), CAP)],
            in_buf.at[slot, pl.ds(e * CAP, CAP)],
            in_sem.at[slot, e],
        )

    for e in range(local):
        coming(first, 0, e).start()

    def body(step, carry):
        slot = step % 2
        s = (step + first) % count

        @pl.when(step + 1 < count)
        def _():
            for e in range(local):
                coming((step + 1 + first) % count, 1 - slot, e).start()

        for e in range(local):
            coming(s, slot, e).wait()

        @pl.when(step >= 2)
        def _():
            pltpu.make_async_copy(out_buf.at[slot], far.at[0], out_sem.at[slot]).wait()

        hot = hot_rows(rank_ref, s, local, length)
        for c in range(0, width, chunk):
            out_buf[slot, :, c : c + chunk] = dot(hot, in_buf[slot, :, c : c + chunk], 0, 0).astype(BF16)

        @pl.when(step < first)
        def _():
            pltpu.make_async_copy(out_buf.at[slot], far.at[step], out_sem.at[slot]).start()

        @pl.when(step >= first)
        def _():
            pltpu.make_async_copy(out_buf.at[slot], near.at[step - first], out_sem.at[slot]).start()

        return carry

    lax.fori_loop(0, count, body, 0)
    for step in (count - 2, count - 1):
        pltpu.make_async_copy(out_buf.at[step % 2], far.at[0], out_sem.at[step % 2]).wait()


def combine(rank, rows, width):
    count, local, length = rank.shape
    return call(
        functools.partial(combine_body, count, local),
        in_specs=[WHOLE] + [ANY] * len(rows),
        out_specs=[ANY] * 2,
        out_shape=[shape(count // 2, length, width)] * 2,
        scratch_shapes=[
            pltpu.VMEM((2, local * CAP, width), BF16),
            pltpu.VMEM((2, length, width), BF16),
            pltpu.SemaphoreType.DMA((2, local)),
            pltpu.SemaphoreType.DMA((2,)),
        ],
        name="combine",
    )(rank, *rows)


def upstream_body(first_ref, y_ref, w_ref, t_ref):
    t_ref[0] = dot(y_ref[0], w_ref[0])


def upstream_product(first, y, w):
    local, rows, width = y.shape
    ff = w.shape[2]
    grid_spec = pltpu.PrefetchScalarGridSpec(
        num_scalar_prefetch=1,
        grid=(local,),
        in_specs=[
            pl.BlockSpec((1, rows, width), lambda e, f: (e, 0, 0)),
            pl.BlockSpec((1, width, ff), lambda e, f: (f[0] + e, 0, 0)),
        ],
        out_specs=pl.BlockSpec((1, rows, ff), lambda e, f: (e, 0, 0)),
    )
    return call(
        upstream_body, grid_spec=grid_spec, out_shape=shape(local, rows, ff, dtype=F32), name="upstream"
    )(first, y, w)


def output_body(first_ref, *refs):
    acts, w_ref, out_ref = refs[:-2], refs[-2], refs[-1]
    step = pl.program_id(0)
    for e, act in enumerate(acts):
        @pl.when(step == e)
        def _():
            out_ref[0] = dot(act[...], w_ref[0], 1, 1).astype(BF16)


def output_rows(first, acts, w):
    local = len(acts)
    rows, ff = acts[0].shape
    width = w.shape[1]
    grid_spec = pltpu.PrefetchScalarGridSpec(
        num_scalar_prefetch=1,
        grid=(local,),
        in_specs=[pl.BlockSpec((rows, ff), lambda e, f: (0, 0))] * local
        + [pl.BlockSpec((1, width, ff), lambda e, f: (f[0] + e, 0, 0))],
        out_specs=pl.BlockSpec((1, rows, width), lambda e, f: (e, 0, 0)),
    )
    return call(
        output_body, grid_spec=grid_spec, out_shape=shape(local, rows, width), name="output"
    )(first, *acts, w)


def expert_body(
    expert, n_grp, info_ref, x_hbm, y_hbm, t_hbm, gate_ref, wg_hbm, wu_hbm,
    out_theirs, out_mine, out_dx, out_act, dg_ref,
    x, y, t, w, gu, d, act, theirs, mine, dx, sems,
):
    rows, width = x.shape
    ff = t.shape[1]
    block = 448 if rows % 448 == 0 else rows
    index = info_ref[0] + expert
    place = info_ref[1]
    copies = [
        pltpu.make_async_copy(x_hbm.at[expert], x, sems.at[0]),
        pltpu.make_async_copy(wg_hbm.at[index], w.at[:, pl.ds(0, ff)], sems.at[1]),
        pltpu.make_async_copy(wu_hbm.at[index], w.at[:, pl.ds(ff, ff)], sems.at[2]),
        pltpu.make_async_copy(t_hbm.at[expert], t, sems.at[3]),
        pltpu.make_async_copy(y_hbm.at[expert], y, sems.at[4]),
    ]
    for copy in copies:
        copy.start()
    for copy in copies[:3]:
        copy.wait()

    def forward(b, carry):
        at = pl.ds(pl.multiple_of(b * block, 16), block)
        gu[...] = dot(x[at], w[...])

        @pl.when(b == 0)
        def _():
            copies[3].wait()

        def point(i, carry):
            inner = pl.ds(pl.multiple_of(i * 32, 32), 32)
            outer = pl.ds(pl.multiple_of(b * block + i * 32, 32), 32)
            g, u = gu[inner, :ff], gu[inner, ff:]
            tt, gate = t[outer], gate_ref[0, outer]
            sig = 1.0 / (1.0 + jnp.exp(-g))
            silu = g * sig
            a = (silu * u).astype(BF16)
            a32 = a.astype(F32)
            dg_ref[outer] = jnp.sum(a32 * tt, axis=-1, keepdims=True)
            act[outer] = (a32 * gate).astype(BF16)
            da = gate * tt
            d[outer, :ff] = (da * u * sig * (1.0 + g * (1.0 - sig))).astype(BF16)
            d[outer, ff:] = (da * silu).astype(BF16)
            return carry

        return lax.fori_loop(0, block // 32, point, carry)

    lax.fori_loop(0, rows // block, forward, 0)
    copies[4].wait()
    act_out = pltpu.make_async_copy(act, out_act, sems.at[0])
    act_out.start()

    piece = width // n_grp
    band = 384
    keep = band // 2

    def split(j, k, res):
        res = res.astype(BF16)
        for p in range(band // (2 * piece)):
            low = res[2 * p * piece : (2 * p + 1) * piece]
            high = res[(2 * p + 1) * piece : (2 * p + 2) * piece]
            at = pl.ds(pl.multiple_of(j * keep + p * piece, 16), piece)

            @pl.when(place == 0)
            def _():
                theirs[k, at] = high
                mine[k, at] = low

            @pl.when(place != 0)
            def _():
                theirs[k, at] = low
                mine[k, at] = high

    def band_down(j, carry):
        cols = pl.ds(pl.multiple_of(j * band, 128), band)
        split(j, 2, dot(y[:, cols], act[...], 0, 0))
        return carry

    def band_gate(j, carry):
        cols = pl.ds(pl.multiple_of(j * band, 128), band)
        res = dot(x[:, cols], d[...], 0, 0)
        split(j, 0, res[:, :ff])
        split(j, 1, res[:, ff:])
        return carry

    bands = width // band
    lax.fori_loop(0, bands, band_gate, 0)
    early = [
        pltpu.make_async_copy(theirs.at[pl.ds(0, 2)], out_theirs.at[pl.ds(0, 2)], sems.at[1]),
        pltpu.make_async_copy(mine.at[pl.ds(0, 2)], out_mine.at[pl.ds(0, 2)], sems.at[2]),
    ]
    for copy in early:
        copy.start()
    lax.fori_loop(0, bands, band_down, 0)
    late = [
        pltpu.make_async_copy(theirs.at[2], out_theirs.at[2], sems.at[5]),
        pltpu.make_async_copy(mine.at[2], out_mine.at[2], sems.at[6]),
    ]
    for copy in late:
        copy.start()

    def back(b, carry):
        at = pl.ds(pl.multiple_of(b * block, 16), block)
        for c in range(0, width, 512):
            dx[at, c : c + 512] = dot(d[at], w[c : c + 512], 1, 1).astype(BF16)
        return carry

    lax.fori_loop(0, rows // block, back, 0)
    dx_out = pltpu.make_async_copy(dx, out_dx, sems.at[7])
    dx_out.start()
    for copy in [act_out] + early + late + [dx_out]:
        copy.wait()


def expert_step(expert, n_grp, info, x, y, t, gate, w_gate, w_up):
    local, rows, width = x.shape
    ff = t.shape[2]
    half = shape(3, width // 2, ff)
    return call(
        functools.partial(expert_body, expert, n_grp),
        grid=(1,),
        in_specs=[SCALAR, ANY, ANY, ANY, pl.BlockSpec((1, rows, 1), lambda _: (expert, 0, 0)), ANY, ANY],
        out_specs=[ANY] * 4 + [fixed(rows, 1)],
        out_shape=[half] * 2 + [shape(rows, width), shape(rows, ff), shape(rows, 1, dtype=F32)],
        scratch_shapes=[
            pltpu.VMEM((rows, width), BF16),
            pltpu.VMEM((rows, width), BF16),
            pltpu.VMEM((rows, ff), F32),
            pltpu.VMEM((width, 2 * ff), BF16),
            pltpu.VMEM((448 if rows % 448 == 0 else rows, 2 * ff), F32),
            pltpu.VMEM((rows, 2 * ff), BF16),
            pltpu.VMEM((rows, ff), BF16),
            pltpu.VMEM((3, width // 2, ff), BF16),
            pltpu.VMEM((3, width // 2, ff), BF16),
            pltpu.VMEM((rows, width), BF16),
            pltpu.SemaphoreType.DMA((8,)),
        ],
        name="expert",
    )(info, x, y, t, gate, w_gate, w_up)


def attend_back_body(
    q_ref, k_ref, v_ref, dm_ref, lse_ref, delta_ref, cos_ref, sin_ref, tagc_ref, tagr_ref,
    dq_ref, dk_ref, dv_ref,
    mask_ref, dk_acc, dv_acc, dq_acc,
):
    step = pl.program_id(0)
    per = pl.num_programs(0) // KV_HEADS
    length = q_ref.shape[0]
    block = 256

    @pl.when(step == 0)
    def _():
        for r in range(0, length, block):
            key = lax.broadcasted_iota(jnp.int32, (block, length), 0) + r
            query = lax.broadcasted_iota(jnp.int32, (block, length), 1)
            tag = tagc_ref[r : r + block]
            inside = (tag == tagr_ref[...]) & (tag > 0)
            mask_ref[r : r + block] = jnp.where((key <= query) | inside, 0.0, -1e30)

    @pl.when(step % per == 0)
    def _():
        dk_acc[...] = jnp.zeros_like(dk_acc)
        dv_acc[...] = jnp.zeros_like(dv_acc)

    def unturn(w):
        return w * cos_ref[...] - pltpu.roll(w, HEAD_DIM // 2, 1) * sin_ref[...]

    for h in range(2):
        cols = slice(h * HEAD_DIM, (h + 1) * HEAD_DIM)
        dq_acc[...] = jnp.zeros_like(dq_acc)
        for r in range(0, length, block):
            low = max(0, r - block)
            q, dm = q_ref[low:, cols], dm_ref[low:, cols]
            k, v = k_ref[r : r + block], v_ref[r : r + block]
            s = dot(k, q, 1, 1) * SCALE + mask_ref[r : r + block, low:]
            p = jnp.exp(s - lse_ref[h, :, low:])
            dp = dot(v, dm, 1, 1)
            ds = (p * (dp - delta_ref[h, :, low:])).astype(BF16)
            dk_acc[r : r + block] += dot(ds, q)
            dv_acc[r : r + block] += dot(p.astype(BF16), dm)
            dq_acc[low:] += dot(ds, k, 0, 0)
        dq_ref[:, cols] = unturn(dq_acc[...] * SCALE).astype(BF16)

    @pl.when(step % per == per - 1)
    def _():
        dk_ref[...] = unturn(dk_acc[...] * SCALE).astype(BF16)
        dv_ref[...] = dv_acc[...].astype(BF16)


def attend_back(q, k, v, dm, lse, delta, cosine, sine, tagc, tagr):
    length = q.shape[0]
    pairs = HEADS // 2
    per = pairs // KV_HEADS
    two = pl.BlockSpec((length, 2 * HEAD_DIM), lambda p: (0, p))
    one = pl.BlockSpec((length, HEAD_DIM), lambda p: (0, p // per))
    line = pl.BlockSpec((2, 1, length), lambda p: (p, 0, 0))
    return call(
        attend_back_body,
        grid=(pairs,),
        in_specs=[two, one, one, two, line, line, fixed(length, HEAD_DIM), fixed(length, HEAD_DIM), fixed(length, 1), fixed(1, length)],
        out_specs=[two, one, one],
        out_shape=[shape(length, HEADS * HEAD_DIM), shape(length, KV_HEADS * HEAD_DIM), shape(length, KV_HEADS * HEAD_DIM)],
        scratch_shapes=[
            pltpu.VMEM((length, length), F32),
            pltpu.VMEM((length, HEAD_DIM), F32),
            pltpu.VMEM((length, HEAD_DIM), F32),
            pltpu.VMEM((length, HEAD_DIM), F32),
        ],
        name="attend_back",
    )(q, k, v, dm, lse, delta, cosine, sine, tagc, tagr)


def cluster_steps():
    return [("exp", bit) for bit in bits_of(lax.axis_size("exp"))[1:]]


def gather_now(own):
    half = own.shape[0] // 2
    steps = cluster_steps()
    items = [own]
    for axis, bit in steps[:-1]:
        items = items + [swap(item, axis, bit) for item in items]
    axis, bit = steps[-1]
    along = [swap(item, axis, bit) for item in items]
    across = [swap(item, "grp", PAIR) for item in items]
    corner = [(swap(z[:half], axis, bit), swap(y[half:], "grp", PAIR)) for y, z in zip(along, across)]
    items = [(item,) for item in items + along + across] + corner
    return items + [tuple(swap(part, "exp", CORE) for part in item) for item in items]


def gather_late(own, first, gate_value):
    steps = cluster_steps()
    own = lax.optimization_barrier((own, first))[0]
    items = [own]
    for axis, bit in steps:
        items = items + [swap(item, axis, bit) for item in items]
    held = lax.optimization_barrier((own, gate_value))[0]
    across = [swap(held, "grp", PAIR)]
    for axis, bit in steps:
        across = across + [swap(item, axis, bit) for item in across]
    items = items + across
    items = items + [swap(item, "exp", CORE) for item in items]
    return [(item,) for item in items]


def gather_small(own):
    items = [own]
    for axis, bit in cluster_steps() + [("grp", PAIR), ("exp", CORE)]:
        block = jnp.stack(items)
        items = items + list(swap(block, axis, bit))
    return items


def add(first, second):
    return (first.astype(F32) + second.astype(F32)).astype(BF16)


class Return:
    def __init__(self, far, near, flow):
        self.flow = flow
        count, length, width = near.shape
        self.dims = (4, count // 4, length, width)
        self.near = near
        self.came = swap(far, "exp", CORE)
        self.stage = 0

    def step(self):
        self.stage += 1
        flow = self.flow
        axis, bit = cluster_steps()[-1]
        half = self.dims[2] // 2
        if self.stage == 1:
            near, came = flow.after(self.near, self.came)
            near, came = near.reshape(self.dims), came.reshape(self.dims)

            def part(index, rows):
                return add(near[index, :, rows], came[index, :, rows])

            low, high = slice(0, half), slice(half, None)
            zc = part(slice(2, 4), low)
            yc = part(slice(1, 4, 2), high)
            zc, yc = flow.mark(lax.optimization_barrier((zc, yc)))
            self.zc, self.yc = swap(zc, "grp", PAIR), swap(yc, axis, bit)
            near, came = flow.after(near, came)
            self.low, self.high = part(0, low), part(0, high)
            self.y_low, self.z_high = part(1, low), part(2, high)
        elif self.stage == 2:
            zc, yc = flow.after(self.zc, self.yc)
            y_low, z_high = flow.mark(
                lax.optimization_barrier((add(self.y_low, zc[1]), add(self.z_high, yc[1])))
            )
            self.y_low, self.z_high = swap(y_low, axis, bit), swap(z_high, "grp", PAIR)
            self.zc, self.yc = zc[0], yc[0]
        else:
            y_low, z_high = flow.after(self.y_low, self.z_high)
            low = self.low.astype(F32) + self.zc.astype(F32) + y_low.astype(F32)
            high = self.high.astype(F32) + self.yc.astype(F32) + z_high.astype(F32)
            total = jnp.concatenate([low, high], axis=1)
            for axis, bit in reversed(cluster_steps()[:-1]):
                count = total.shape[0] // 2
                total = total[:count] + swap(total[count:].astype(BF16), axis, bit).astype(F32)
            return total[0]


def exchange_small(items):
    steps = cluster_steps() + [("grp", PAIR), ("exp", CORE)]
    block = jnp.stack(items)
    for axis, bit in reversed(steps):
        count = block.shape[0] // 2
        block = jnp.concatenate([block[:count], swap(block[count:], axis, bit)], axis=2)
    return block[0]


def ring_order(size):
    return list(range(0, size, 2)) + list(range(size - 1, 0, -2))


def ring_origins():
    size = lax.axis_size("grp")
    order = ring_order(size)
    place = [0] * size
    for i, value in enumerate(order):
        place[value] = i
    spot = jnp.array(place, jnp.int32)[lax.axis_index("grp")]
    ahead = [(spot - step) % size for step in range(size // 2 + 1)]
    behind = [(spot + step) % size for step in range(1, size - size // 2)]
    return jnp.array(order, jnp.int32)[jnp.stack(ahead + behind)]


def ring_pieces(own):
    size = lax.axis_size("grp")
    order = ring_order(size)
    onward = [(order[i], order[(i + 1) % size]) for i in range(size)]
    back = [(order[(i + 1) % size], order[i]) for i in range(size)]
    first, second = [own], []
    for step in range(1, size // 2 + 1):
        first.append(lax.ppermute(first[-1], "grp", onward))
        if step < size - size // 2:
            second.append(lax.ppermute(second[-1] if second else own, "grp", back))
    return first + second


def assemble_body(count, info_ref, *refs):
    out, sems = refs[-2:]
    rows, half = refs[0].shape
    core = info_ref[count]
    copies = []
    for i in range(count):
        at = pl.ds(pl.multiple_of(info_ref[i] * rows, 16), rows)
        for side in range(2):
            column = side * (1 - core) + (1 - side) * core
            to = out.at[at, pl.ds(pl.multiple_of(column * half, 128), half)]
            copies.append(pltpu.make_async_copy(refs[2 * i + side], to, sems.at[i, side]))
    for copy in copies:
        copy.start()
    for copy in copies:
        copy.wait()


def gather_weights(shard, origins, core):
    rows, width = shard.shape
    half = width // 2
    mine = lax.dynamic_slice_in_dim(shard, core * half, half, 1)
    pieces = ring_pieces(mine)
    others = [swap(piece, "exp", CORE) for piece in pieces]
    count = len(pieces)
    info = jnp.concatenate([origins, core[None]])
    both = [part for pair in zip(pieces, others) for part in pair]
    whole = call(
        functools.partial(assemble_body, count),
        in_specs=[SCALAR] + [ANY] * (2 * count),
        out_specs=WHOLE,
        out_shape=shape(count * rows, width),
        scratch_shapes=[pltpu.SemaphoreType.DMA((count, 2))],
        name="assemble",
    )(info, *both)
    return whole, pieces[count // 2]


class GradSum:
    def __init__(self, theirs, mine, flow):
        kinds, rows, width = mine.shape
        bits = bits_of(lax.axis_size("grp"))
        self.flow = flow
        self.left = list(reversed(bits[1:]))
        self.todo = [bit for bit in bits[1:] if bit != PAIR] + [PAIR]
        self.dims = [kinds] + [2] * len(self.left) + [rows >> len(self.left), width]
        self.mine = mine
        self.coming = swap(theirs, "grp", bits[0])
        self.done = False

    def step(self):
        if self.done:
            return
        mine, coming = self.flow.after(self.mine, self.coming)
        block = self.flow.mark(add(mine, coming)).reshape(self.dims)
        bit = self.todo.pop(0)
        axis = self.left.index(bit) + 1
        self.left.pop(axis - 1)
        self.dims.pop(axis)
        place = bit_at(lax.axis_index("grp"), bit)
        theirs = lax.dynamic_index_in_dim(block, 1 - place, axis, keepdims=False)
        self.mine = lax.dynamic_index_in_dim(block, place, axis, keepdims=False)
        self.coming = swap(theirs, "grp", bit)
        self.done = not self.todo


class AllSum:
    def __init__(self, block, flow):
        self.flow = flow
        rows, width = block.shape
        n_grp, n_exp = lax.axis_size("grp"), lax.axis_size("exp")
        grp_bits, exp_bits = bits_of(n_grp), bits_of(n_exp)
        self.left = [("grp", bit) for bit in reversed(grp_bits)] + [("exp", bit) for bit in reversed(exp_bits)]
        others = [bit for bit in reversed(grp_bits) if bit != PAIR]
        self.todo = [("exp", bit) for bit in exp_bits] + [("grp", bit) for bit in [PAIR] + others]
        self.block = block.reshape([2] * len(self.left) + [rows // (n_grp * n_exp), width])
        self.coming = None
        self.send()

    def send(self):
        name, bit = self.todo.pop(0)
        axis = self.left.index((name, bit))
        self.left.pop(axis)
        place = bit_at(lax.axis_index(name), bit)
        theirs = lax.dynamic_index_in_dim(self.block, 1 - place, axis, keepdims=False)
        self.mine = lax.dynamic_index_in_dim(self.block, place, axis, keepdims=False)
        self.coming = swap(theirs, name, bit)

    def step(self):
        if self.coming is None:
            return
        mine, coming = self.flow.after(self.mine, self.coming)
        if self.todo:
            self.block = self.flow.mark(add(mine, coming) if mine.dtype == BF16 else mine + coming)
            self.send()
        else:
            self.block = mine.astype(F32) + coming.astype(F32)
            self.coming = None


def norm_backward(upstream, normal, inverse, gain_vec):
    scaled = upstream * gain_vec
    return inverse * (scaled - normal * jnp.mean(scaled * normal, axis=-1, keepdims=True))


def shards(
    tokens,
    cotangent,
    gate_logits,
    routes,
    piece_starts,
    piece_kinds,
    q_weight,
    k_weight,
    v_weight,
    o_weight,
    attn_gain,
    moe_gain,
    gate_weight,
    up_weight,
    down_weight,
):
    grp, exp = lax.axis_index("grp"), lax.axis_index("exp")
    n_grp = lax.axis_size("grp")
    core = exp % 2
    pair = bit_at(grp, PAIR)
    length, width = tokens.shape
    held = gate_weight.shape[0]
    local = held // 2
    q_width, kv_width = q_weight.shape[1], k_weight.shape[1]

    gates = jax.nn.softmax(gate_logits, axis=-1)
    small_all = jnp.stack(gather_small(jnp.concatenate([routes.astype(F32), gates], axis=1)))
    gain = jnp.stack([attn_gain, moe_gain]).astype(F32)[None]
    for bit in bits_of(n_grp):
        gain = jnp.concatenate([gain, swap(gain, "grp", bit)], axis=0)
    gain = gain[jnp.arange(n_grp, dtype=jnp.int32) ^ grp]
    gain_one = gain[:, 0].reshape(1, width)
    gain_two = gain[:, 1].reshape(1, width)
    origins = ring_origins()
    qkv_full, last = gather_weights(jnp.concatenate([q_weight, k_weight, v_weight], axis=1), origins, core)
    o_full, last = gather_weights(lax.optimization_barrier((o_weight, last))[0], origins, core)
    dy_items = gather_late(cotangent, small_all, last)

    cosine, sine = rope_tables(length)
    tags = piece_tags(piece_starts[0], piece_kinds[0], length)
    tagc, tagr = tags.reshape(length, 1), tags.reshape(1, length)

    routes_all = small_all[:, :, :TOP].astype(jnp.int32)
    gates_all = small_all[:, :, TOP:]
    seqs = routes_all.shape[0]
    first_expert = exp * held + pair * local
    chosen = routes_all[:, :, :, None] == (first_expert + jnp.arange(local, dtype=jnp.int32))
    member = jnp.any(chosen, axis=2)
    gate_te = jnp.sum(jnp.where(chosen, gates_all[:, :, :, None], 0.0), axis=2)
    places = jnp.arange(length, dtype=jnp.int32)
    earlier = (places[None, :] < places[:, None]).astype(BF16)
    order = jnp.einsum("ut,ste->seu", earlier, member.astype(BF16), preferred_element_type=F32)
    rank = jnp.where(jnp.swapaxes(member, 1, 2), order.astype(jnp.int32), -1)
    hot = jnp.swapaxes(rank, 0, 1)[:, :, None, :] == jnp.arange(CAP, dtype=jnp.int32)[None, None, :, None]
    gate_slot = jnp.sum(jnp.where(hot, jnp.transpose(gate_te, (2, 0, 1))[:, :, None, :], 0.0), axis=-1)
    gate_slot = gate_slot.reshape(local, seqs * CAP, 1)

    flow = Flow()
    normed, inverse_one, query_rot, key_rot, value_rows, mixed, log_total = attend(
        tokens, gain_one, qkv_full, cosine, sine, tagc, tagr
    )
    hidden, normed_two, inverse_two = project(tokens, mixed, o_full, gain_two)
    flow.mark(inverse_two)
    n2_items = gather_now(normed_two)

    rank, gate_slot = flow.after(rank, gate_slot)
    y_rows = collect(rank, dy_items)
    first = jnp.reshape(pair * local, (1,))
    t_rows = flow.mark(upstream_product(first, y_rows, down_weight))
    rank = flow.after(rank)
    x_rows = flow.mark(collect(rank, n2_items))
    info = jnp.stack([pair * local, bit_at(grp, 1)])
    sums, d_rows, d_gate_slots, acts = [], [], [], []
    for e in range(local):
        gate_slot = flow.after(gate_slot)
        theirs, mine, dx, act, d_gate = expert_step(
            e, n_grp, info, x_rows, y_rows, t_rows, gate_slot, gate_weight, up_weight
        )
        flow.mark(d_gate)
        sums.append(GradSum(theirs, mine, flow))
        d_rows.append(dx)
        acts.append(act)
        d_gate_slots.append(d_gate.reshape(seqs, CAP))

    def pump(group):
        if group < local:
            sums[group].step()

    pump(0)
    rank = flow.after(rank)
    far, near = combine(rank, d_rows, width)
    flow.mark(near)
    d_return = Return(far, near, flow)
    first = flow.after(first)
    out_rows = flow.mark(output_rows(first, acts, down_weight))
    d_return.step()
    rank = flow.after(rank)
    far, near = combine(rank, [out_rows], width)
    flow.mark(near)
    out_return = Return(far, near, flow)
    pump(1)
    d_return.step()
    pump(0)
    d_normed_two = d_return.step()

    normal_two = hidden * inverse_two
    upstream = cotangent.astype(F32)
    d_hidden = upstream + norm_backward(d_normed_two, normal_two, inverse_two, gain_two)
    moe_gain_grad = jnp.sum(d_normed_two * normal_two, axis=0)
    d_branch = d_hidden.astype(BF16)
    d_mixed = jnp.einsum("td,id->ti", d_branch, o_full, preferred_element_type=F32).astype(BF16)
    delta = jnp.sum(
        (d_mixed.astype(F32) * mixed.astype(F32)).reshape(length, HEADS, HEAD_DIM), axis=-1
    )
    flow.mark(delta)
    out_return.step()
    d_branch = flow.after(d_branch)
    grad_out = flow.mark(jnp.einsum("ti,td->id", mixed, d_branch, preferred_element_type=F32).astype(BF16))
    o_sum = AllSum(grad_out, flow)
    delta = flow.after(delta)
    d_query, d_key, d_value = attend_back(
        query_rot, key_rot, value_rows, d_mixed,
        log_total.reshape(HEADS, 1, length), delta.T.reshape(HEADS, 1, length),
        cosine, sine, tagc, tagr,
    )
    flow.mark(d_key)
    pump(2)
    pump(1)
    o_sum.step()
    d_query = flow.after(d_query)
    d_qkv = jnp.concatenate([d_query, d_key, d_value], axis=1)
    d_normed = jnp.einsum("tj,ij->ti", d_qkv, qkv_full, preferred_element_type=F32)
    normal_one = tokens.astype(F32) * inverse_one
    attn_gain_grad = jnp.sum(d_normed * normal_one, axis=0)
    tokens_grad = flow.mark(
        (d_hidden + norm_backward(d_normed, normal_one, inverse_one, gain_one)).astype(BF16)
    )
    out_return.step()
    d_qkv = flow.after(d_qkv)
    grad_qkv = jnp.einsum("ti,tj->ij", normed, d_qkv, preferred_element_type=F32).astype(BF16)
    gain_grads = jnp.stack([attn_gain_grad, moe_gain_grad], axis=1).astype(BF16)
    gain_grads = jnp.pad(gain_grads, ((0, 0), (0, 126)))
    grad_qkv = flow.mark(jnp.concatenate([grad_qkv, gain_grads], axis=1))
    qkv_sum = AllSum(grad_qkv, flow)
    qkv_sum.step()
    o_sum.step()
    pump(2)
    qkv_sum.step()
    o_sum.step()
    pump(3)
    qkv_sum.step()
    o_sum.step()
    mixed_out = out_return.step()
    layer_out = (hidden + mixed_out).astype(BF16)

    d_gate_te = jnp.sum(jnp.where(hot, jnp.stack(d_gate_slots)[:, :, :, None], 0.0), axis=2)
    d_gate_te = jnp.transpose(d_gate_te, (1, 2, 0))
    d_gates_all = exchange_small([d_gate_te[i] for i in range(seqs)])
    steps = cluster_steps() + [("grp", PAIR), ("exp", CORE)]
    target_exp, target_pair, inner = routes // held, (routes % held) // local, routes % local
    far = jnp.zeros_like(routes)
    for place, (name, bit) in enumerate(steps):
        if name == "exp":
            differs = bit_at(target_exp, bit) != bit_at(exp, bit)
        else:
            differs = target_pair != pair
        far = far + differs.astype(jnp.int32) * (1 << (len(steps) - 1 - place))
    column = far * local + inner
    d_gates = jnp.sum(
        jnp.where(
            column[:, :, None] == jnp.arange(d_gates_all.shape[1], dtype=jnp.int32),
            d_gates_all[:, None, :],
            0.0,
        ),
        axis=-1,
    )
    logits_grad = gates * (d_gates - jnp.sum(gates * d_gates, axis=-1, keepdims=True))

    while not all(item.done for item in sums):
        for item in sums:
            item.step()
    while qkv_sum.coming is not None:
        qkv_sum.step()
        o_sum.step()

    def finish(kind):
        low, high = [], []
        for group in sums:
            mine, coming = group.mine[kind], group.coming[kind]
            low.append(jnp.where(pair == 0, mine, coming).astype(F32))
            high.append(jnp.where(pair == 0, coming, mine).astype(F32))
        return jnp.stack(low + high)

    return (
        layer_out,
        tokens_grad,
        logits_grad,
        qkv_sum.block[:, :q_width],
        qkv_sum.block[:, q_width : q_width + kv_width],
        qkv_sum.block[:, q_width + kv_width : q_width + 2 * kv_width],
        o_sum.block,
        qkv_sum.block[:, q_width + 2 * kv_width],
        qkv_sum.block[:, q_width + 2 * kv_width + 1],
        finish(0),
        finish(1),
        finish(2),
    )


def solution(mesh):
    rows = P(("grp", "exp"), None)
    placed = (rows,) * 6 + (P("grp", None),) * 4 + (P("grp"),) * 2 + (P("exp", None, None),) * 3
    outs = (rows,) * 7 + (P(("grp", "exp")),) * 2 + (P("exp", "grp", None),) * 3
    return jax.shard_map(shards, mesh=mesh, in_specs=placed, out_specs=outs, check_vma=False)
```

```python
import functools
from types import SimpleNamespace

import jax
import jax.numpy as jnp
import numpy as np
from jax import lax
from jax.experimental import pallas as pl
from jax.experimental.pallas import tpu as pltpu
from jax.sharding import PartitionSpec as P

HEADS = 12
KV_HEADS = 2
HEAD_DIM = 128
EXPERTS = 32
TOP = 4
CAP = 112
EPSILON = 1e-06
THETA = 1000000.0
SCALE = HEAD_DIM ** (-0.5)
GRP = "grp"
EXP = "exp"
CORE = 1
PAIR = 2
VMEM = 58 * 1024 * 1024
BF16 = jnp.bfloat16
F32 = jnp.float32


def bits_of(size):
    return [1 << i for i in range(size.bit_length() - 1)]


def bit_at(index, bit):
    return lax.rem(lax.div(index, jnp.int32(bit)), jnp.int32(2))


def space(tree):
    if isinstance(tree, dict):
        return SimpleNamespace(**{name: space(value) for name, value in tree.items()})
    return [space(value) for value in tree] if isinstance(tree, list) else tree


def rope_tables(length):
    half = HEAD_DIM // 2
    frequency = THETA ** (-2.0 * np.arange(half) / HEAD_DIM)
    angles = np.arange(length)[:, None] * frequency[None, :]
    cosine, sine = np.cos(angles), np.sin(angles)
    tables = [np.concatenate([cosine, cosine], axis=1), np.concatenate([-sine, sine], axis=1)]
    return [jnp.asarray(table.astype(np.float32)) for table in tables]


def piece_tags(starts, kinds, length):
    places = jnp.arange(length, dtype=jnp.int32)
    piece_of = jnp.sum((places[:, None] >= starts[None, :]).astype(jnp.int32), axis=1) - 1
    slot_ids = jnp.arange(starts.shape[0], dtype=jnp.int32)
    kind_of = jnp.sum(jnp.where(piece_of[:, None] == slot_ids[None, :], kinds[None, :], 0), axis=1)
    return jnp.where(kind_of == 1, piece_of + 1, 0)


def call(body, **kw):
    params = pltpu.CompilerParams(vmem_limit_bytes=VMEM)
    cost = pl.CostEstimate(flops=1, bytes_accessed=1, transcendentals=0)
    return pl.pallas_call(body, compiler_params=params, cost_estimate=cost, **kw)


def shape(*dims, dtype=BF16):
    return jax.ShapeDtypeStruct(dims, dtype)


def dot(a, b, ca=1, cb=0):
    return lax.dot_general(a, b, (((ca,), (cb,)), ((), ())), preferred_element_type=F32)


ANY = pl.BlockSpec(memory_space=pl.ANY)
WHOLE = pl.BlockSpec(memory_space=pltpu.VMEM)
SCALAR = pl.BlockSpec(memory_space=pltpu.SMEM)


def fixed(*dims):
    return pl.BlockSpec(dims, lambda *_: (0,) * len(dims))


def shape(*dims, dtype=BF16):
    return jax.ShapeDtypeStruct(dims, dtype)


def dot(a, b, ca=1, cb=0):
    return lax.dot_general(a, b, (((ca,), (cb,)), ((), ())), preferred_element_type=F32)


ANY = pl.BlockSpec(memory_space=pl.ANY)
WHOLE = pl.BlockSpec(memory_space=pltpu.VMEM)


def hot_rows(rank, s, local, length):
    spot = lax.broadcasted_iota(jnp.int32, (CAP, length), 0)
    picked = rank[s]
    return jnp.concatenate(
        [(picked[e : e + 1] == spot).astype(F32).astype(BF16) for e in range(local)], axis=0
    )


def ring_spot(group, size):
    odd = lax.rem(group, jnp.int32(2))
    half = lax.div(group, jnp.int32(2))
    return (1 - odd) * half + odd * (size - 1 - half)


def ring_group(spot, size):
    spot = lax.rem(spot + 2 * size, jnp.int32(size))
    upper = lax.div(spot, jnp.int32(size // 2))
    return (1 - upper) * (2 * spot) + upper * (2 * (size - 1 - spot) + 1)


def front_body(dims, in_tree, out_tree, sem_tree, *refs):
    local, seqs, length, width, ff, n_grp, n_exp, rows_w = dims
    n_in, n_out = in_tree.num_leaves, out_tree.num_leaves
    I = space(jax.tree.unflatten(in_tree, refs[:n_in]))
    O = space(jax.tree.unflatten(out_tree, refs[n_in : n_in + n_out]))
    S = space(jax.tree.unflatten(sem_tree, refs[n_in + n_out :]))
    half = length // 2
    qkv = (HEADS + 2 * KV_HEADS) * HEAD_DIM
    grp, exp = lax.axis_index(GRP), lax.axis_index(EXP)
    me = grp * n_exp + exp
    y_bits = bits_of(n_exp)[1:]
    last_y = y_bits[-1]
    core_at = bit_at(exp, CORE)
    pair_at = bit_at(grp, PAIR)
    partner = {(EXP, bit): me + (1 - 2 * bit_at(exp, bit)) * bit for bit in bits_of(n_exp)}
    partner[GRP, PAIR] = me + (1 - 2 * pair_at) * (PAIR * n_exp)
    spot = ring_spot(grp, n_grp)
    around = [ring_group(spot + 1, n_grp) * n_exp + exp, ring_group(spot - 1, n_grp) * n_exp + exp]

    def send(src, dst, sems, device):
        return pltpu.make_async_remote_copy(
            src_ref=src, dst_ref=dst, send_sem=sems.at[0], recv_sem=sems.at[1],
            device_id=device, device_id_type=pl.DeviceIdType.LOGICAL,
        )

    barrier = pltpu.get_barrier_semaphore()
    greeted = list(partner.values()) + around
    for device in greeted:
        pl.semaphore_signal(barrier, inc=1, device_id=device, device_id_type=pl.DeviceIdType.LOGICAL)
    pl.semaphore_wait(barrier, len(greeted))


    hops = (n_grp // 2, n_grp - 1 - n_grp // 2)

    def ring_piece(full, origin):
        w = full.shape[2] // 2
        return full.at[origin, :, pl.ds(pl.multiple_of(core_at * w, 128), w)]

    def ring_send(kind, way, step):
        full = (O.wq, O.wo)[kind]
        origin = ring_group(spot - (step - 1) if way == 0 else spot + (step - 1), n_grp)
        piece = ring_piece(full, origin)
        return send(piece, piece, S.ring.at[kind, way, step], around[way])

    def ring_got(kind, way, step):
        full = (O.wq, O.wo)[kind]
        origin = ring_group(spot - step if way == 0 else spot + step, n_grp)
        return ring_piece(full, origin)

    def core_hand(kind, way, step):
        piece = ring_got(kind, way, step)
        return send(piece, piece, S.hand.at[kind, way, step], partner[EXP, CORE])

    def ring_step(kind, step):
        for way in range(2):
            @pl.when(step <= hops[way])
            def _():
                ring_send(kind, way, step).wait_recv()
                core_hand(kind, way, step).start()

            @pl.when(step + 1 <= hops[way])
            def _():
                ring_send(kind, way, step + 1).start()

    def ring_start(kind):
        for way in range(2):
            if hops[way]:
                ring_send(kind, way, jnp.int32(1)).start()

    def ring_end(kind):
        def body(step, carry):
            for way in range(2):
                @pl.when(step <= hops[way])
                def _():
                    core_hand(kind, way, step).wait()
                    ring_send(kind, way, step).wait_send()

            return carry

        lax.fori_loop(1, hops[0] + 1, body, 0)


    quads = 2 ** len(y_bits)
    first = seqs // 2

    def spread_send(all_ref, sems, k, axis, bit, low, count, to, part=None):
        src, dst = all_ref.at[pl.ds(low, count)], all_ref.at[pl.ds(to, count)]
        if part is not None:
            src, dst = src.at[:, part], dst.at[:, part]
        return send(src, dst, sems.at[k], partner[axis, bit])

    def y_spread(all_ref, sems, k, base, bits):
        return [spread_send(all_ref, sems, k + i, EXP, bit, base, 2**i, base + 2**i) for i, bit in enumerate(bits)]

    def core_spread(all_ref, sems, k, item):
        return spread_send(all_ref, sems, k, EXP, CORE, item, 1, item + first)

    own = [
        pltpu.make_async_copy(I.small, O.small.at[0], S.own.at[0]),
        pltpu.make_async_copy(I.wq, O.wq.at[grp], S.own.at[1]),
        pltpu.make_async_copy(I.wo, O.wo.at[grp], S.own.at[2]),
        pltpu.make_async_copy(I.dy, O.dy.at[0], S.own.at[3]),
    ]
    for copy in own:
        copy.start()
    for copy in own:
        copy.wait()
    ring_start(0)
    small = y_spread(O.small, S.small, 0, 0, y_bits)
    small.append(spread_send(O.small, S.small, len(y_bits), GRP, PAIR, 0, quads, quads))
    small.append(spread_send(O.small, S.small, len(y_bits) + 1, EXP, CORE, 0, first, first))
    dy_y = y_spread(O.dy, S.dy, 0, 0, y_bits)
    n_y = len(y_bits)
    dy_z = spread_send(O.dy, S.dy, n_y, GRP, PAIR, 0, 1, quads)
    dy_zy = y_spread(O.dy, S.dy, n_y + 1, quads, y_bits)
    dy_core = [core_spread(O.dy, S.dy, 2 * n_y + 1 + i, i) for i in range(first)]
    for copy in small:
        copy.start()
        copy.wait_recv()
    dy_y[0].start()
    dy_z.start()


    def slots(info, tri, sem):
        load = pltpu.make_async_copy(O.small, info, sem.at[0])
        load.start()
        load.wait()
        base = exp * (2 * local) + pair_at * local
        for r in range(0, length, 256):
            before = lax.broadcasted_iota(jnp.int32, (256, length), 0) + r
            after = lax.broadcasted_iota(jnp.int32, (256, length), 1)
            tri[r : r + 256] = jnp.where(before < after, 1.0, 0.0).astype(BF16)
        index = lax.broadcasted_iota(jnp.int32, (8, length), 0)
        name = (index + base).astype(F32)
        used = index < local

        def body(s, carry):
            member = jnp.zeros((8, length), F32)
            gate = jnp.zeros((8, length), F32)
            number = jnp.zeros((8, length), F32)
            for k in range(TOP):
                hit = (info[s, k : k + 1] == name) & used
                member = jnp.where(hit, 1.0, member)
                gate = jnp.where(hit, info[s, TOP + k : TOP + k + 1], gate)
                number = jnp.where(hit, float(k), number)
            rank = dot(member.astype(BF16), tri[...])
            O.rank[s] = jnp.where(member > 0.0, rank, -1.0).astype(jnp.int32)
            S.gate[s] = gate
            S.number[s] = number
            return carry

        lax.fori_loop(0, seqs, body, 0)

    pl.run_scoped(
        slots, pltpu.VMEM((seqs, 8, length), F32), pltpu.VMEM((length, length), BF16), pltpu.SemaphoreType.DMA((1,))
    )

    def ring_through(kind):
        def body(step, carry):
            ring_step(kind, step)
            return carry

        lax.fori_loop(1, hops[0] + 1, body, 0)

    ring_through(0)
    ring_start(1)
    ring_end(0)


    def attention(w, n1, mixed, sems):
        loads = [
            pltpu.make_async_copy(O.wq.at[i, pl.ds(0, rows_w)], w.at[pl.ds(i * rows_w, rows_w)], sems.at[0])
            for i in range(n_grp)
        ]
        for copy in loads:
            copy.start()

        lanes = -(-rows_w // 128) * 128

        def gains(buf, total):
            copies = [
                pltpu.make_async_copy(O.wq.at[i, pl.ds(rows_w, 16), pl.ds(0, lanes)], buf.at[i], sems.at[1])
                for i in range(n_grp)
            ]
            for copy in copies:
                copy.start()
            pltpu.make_async_copy(buf, buf, sems.at[1]).wait()
            total[...] = jnp.zeros_like(total)

            def body(i, carry):
                r = lax.broadcasted_iota(jnp.int32, (lanes, width), 0)
                c = lax.broadcasted_iota(jnp.int32, (lanes, width), 1)
                pick = jnp.where((c == r + i * rows_w) & (r < rows_w), 1.0, 0.0).astype(BF16)
                total[...] += dot(buf[i], pick)
                return carry

            lax.fori_loop(0, n_grp, body, 0)
            O.gains[...] = total[0:8]

        pl.run_scoped(gains, pltpu.VMEM((n_grp, 16, lanes), BF16), pltpu.VMEM((16, width), F32))
        chunk = 64

        def norm(j, carry):
            r = pl.ds(pl.multiple_of(j * chunk, chunk), chunk)
            x = I.tokens[r].astype(F32)
            inverse = lax.rsqrt(jnp.mean(x * x, axis=-1, keepdims=True) + EPSILON)
            O.inv_one[r] = inverse
            n1[r] = (x * inverse * O.gains[0:1]).astype(BF16)
            return carry

        lax.fori_loop(0, length // chunk, norm, 0)
        n1_out = pltpu.make_async_copy(n1, O.n1, sems.at[2])
        n1_out.start()
        pltpu.make_async_copy(w, w, sems.at[0]).wait()

        def heads(mask, kr, v, qr, own):
            block = 256
            for r in range(0, length, block):
                row = lax.broadcasted_iota(jnp.int32, (block, length), 0) + r
                col = lax.broadcasted_iota(jnp.int32, (block, length), 1)
                tag = I.tagc[r : r + block]
                inside = (tag == I.tagr[...]) & (tag > 0)
                mask[r : r + block] = jnp.where((col <= row) | inside, 0.0, -1e30)

            def turn(u):
                return u * I.cos[...] + pltpu.roll(u, HEAD_DIM // 2, 1) * I.sin[...]

            per = HEADS // KV_HEADS // 2
            pairs = HEADS // 2
            every = -(-hops[0] // (pairs - 2))
            for g in range(KV_HEADS):
                kv = slice(g * HEAD_DIM, (g + 1) * HEAD_DIM)
                k_at = HEADS * HEAD_DIM + g * HEAD_DIM
                v_at = k_at + KV_HEADS * HEAD_DIM
                both = dot(n1[...], w[:, k_at : k_at + HEAD_DIM])
                kr[:, kv] = turn(both).astype(BF16)
                v[:, kv] = dot(n1[...], w[:, v_at : v_at + HEAD_DIM]).astype(BF16)

                def pair(i, carry):
                    p = g * per + i
                    span = pl.ds(pl.multiple_of(p * 2 * HEAD_DIM, 2 * HEAD_DIM), 2 * HEAD_DIM)
                    q2 = dot(n1[...], w[:, span])
                    for h in range(2):
                        cols = pl.ds(pl.multiple_of((2 * p + h) * HEAD_DIM, HEAD_DIM), HEAD_DIM)
                        qr[:, cols] = turn(q2[:, h * HEAD_DIM : (h + 1) * HEAD_DIM]).astype(BF16)
                        for r in range(0, length, block):
                            keys = min(length, r + 2 * block)
                            s = dot(qr[r : r + block, cols], kr[:keys, kv], 1, 1) * SCALE
                            s = s + mask[r : r + block, :keys]
                            top = jnp.max(s, axis=-1, keepdims=True)
                            e = jnp.exp(s - top)
                            total = jnp.sum(e, axis=-1, keepdims=True)
                            probs = (e * (1.0 / total)).astype(BF16)
                            mixed[r : r + block, cols] = dot(probs, v[:keys, kv]).astype(BF16)
                            O.lse[2 * p + h, r : r + block] = top + jnp.log(total)

                    def hop(j, carry):
                        @pl.when(j <= hops[0])
                        def _():
                            ring_step(1, j)

                        return carry

                    lax.fori_loop(lax.max((p - 1) * every + 1, 1), lax.max(p * every + 1, 1), hop, 0)
                    return carry

                lax.fori_loop(0, per, pair, 0)
            outs = [
                pltpu.make_async_copy(qr, O.q, own.at[0]),
                pltpu.make_async_copy(kr, O.k, own.at[1]),
                pltpu.make_async_copy(v, O.v, own.at[2]),
                pltpu.make_async_copy(mixed, O.mixed, own.at[3]),
            ]
            for copy in outs:
                copy.start()
            for copy in outs:
                copy.wait()

        pl.run_scoped(
            heads, pltpu.VMEM((length, length), F32), pltpu.VMEM((length, KV_HEADS * HEAD_DIM), BF16),
            pltpu.VMEM((length, KV_HEADS * HEAD_DIM), BF16), pltpu.VMEM((length, HEADS * HEAD_DIM), BF16),
            pltpu.SemaphoreType.DMA((4,)),
        )
        n1_out.wait()

    def projection(mixed, wo, n2, hid, sems):
        loads = [
            pltpu.make_async_copy(O.wo.at[i], wo.at[pl.ds(i * rows_w, rows_w)], sems.at[0]) for i in range(n_grp)
        ]
        for copy in loads:
            copy.start()
        pltpu.make_async_copy(wo, wo, sems.at[0]).wait()
        block = 256

        def body(j, carry):
            r = pl.ds(pl.multiple_of(j * block, block), block)
            for c in range(0, width, 512):
                hid[r, c : c + 512] = I.tokens[r, c : c + 512].astype(F32) + dot(mixed[r], wo[:, c : c + 512])

            def point(i, carry):
                r = pl.ds(pl.multiple_of(j * block + i * 64, 64), 64)
                h = hid[r]
                inverse = lax.rsqrt(jnp.mean(h * h, axis=-1, keepdims=True) + EPSILON)
                O.inv_two[r] = inverse
                n2[r] = (h * inverse * O.gains[1:2]).astype(BF16)
                return carry

            return lax.fori_loop(0, block // 64, point, carry)

        lax.fori_loop(0, length // block, body, 0)
        outs = [
            pltpu.make_async_copy(n2, O.n2.at[0], sems.at[0]),
            pltpu.make_async_copy(hid, O.hidden, sems.at[1]),
        ]
        for copy in outs:
            copy.start()
        outs[0].wait()
        n2_start()
        outs[1].wait()


    low, high = pl.ds(0, half), pl.ds(half, half)
    steps = len(y_bits) - 1
    mid = 2**steps
    n2_pre = y_spread(O.n2, S.n2, 0, 0, y_bits[:-1])
    n2_y = spread_send(O.n2, S.n2, steps, EXP, last_y, 0, mid, mid)
    n2_z = spread_send(O.n2, S.n2, steps + 1, GRP, PAIR, 0, mid, 2 * mid)
    n2_low = spread_send(O.n2, S.n2, steps + 2, EXP, last_y, 2 * mid, mid, 3 * mid, low)
    n2_high = spread_send(O.n2, S.n2, steps + 3, GRP, PAIR, mid, mid, 3 * mid, high)
    n2_core = [core_spread(O.n2, S.n2, steps + 4 + i, i) for i in range(first)]

    def n2_start():
        for copy in n2_pre:
            copy.start()
            copy.wait_recv()
        n2_y.start()
        n2_z.start()
        for i in range(mid):
            n2_core[i].start()

    def n2_ready(step):
        for i in range(first):
            @pl.when(step == 2 * i)
            def _():
                if i == mid:
                    n2_y.wait_recv()
                    n2_high.start()
                    for j in range(mid):
                        n2_core[mid + j].start()
                    n2_z.wait_recv()
                    n2_low.start()
                    for j in range(mid):
                        n2_core[2 * mid + j].start()
                if i == 3 * mid:
                    n2_low.wait_recv()
                    n2_high.wait_recv()
                    for j in range(mid):
                        n2_core[3 * mid + j].start()

            @pl.when(step == 2 * i + 1)
            def _():
                n2_core[i].wait_recv()

    def dy_ready(step):
        for i in range(first):
            @pl.when(step == 2 * i)
            def _():
                if i == quads:
                    for j in range(1, quads):
                        dy_core[quads + j].start()

            @pl.when(step == 2 * i + 1)
            def _():
                dy_core[i].wait_recv()


    def gather(all_ref, out_ref, ready, with_slots):
        chunk = 512

        def scoped(in_buf, out_buf, in_sem, out_sem):
            def seq_of(step):
                return lax.div(step, jnp.int32(2)) + lax.rem(step, jnp.int32(2)) * first

            def fetch(step, slot):
                return pltpu.make_async_copy(all_ref.at[seq_of(step)], in_buf.at[slot], in_sem.at[slot])

            def leaving(step, slot, e):
                row = pl.multiple_of(seq_of(step) * CAP, 16)
                return pltpu.make_async_copy(
                    out_buf.at[slot, pl.ds(e * CAP, CAP)], out_ref.at[e, pl.ds(row, CAP)], out_sem.at[slot, e]
                )

            def body(step, carry):
                slot = lax.rem(step, jnp.int32(2))
                s = seq_of(step)
                ready(step)
                fetch(step, slot).start()
                fetch(step, slot).wait()

                @pl.when(step >= 2)
                def _():
                    for e in range(local):
                        leaving(step - 2, slot, e).wait()

                place = lax.broadcasted_iota(jnp.int32, (CAP, length), 0)
                ranks = O.rank[s]
                hits = [ranks[e : e + 1] == place for e in range(local)]
                if with_slots:
                    gate, number = S.gate[s], S.number[s]
                    rows = pl.ds(pl.multiple_of(s * CAP, 16), CAP)
                    for e in range(local):
                        O.gate[e, rows] = jnp.sum(jnp.where(hits[e], gate[e : e + 1], 0.0), axis=-1, keepdims=True)
                        O.choice[e, rows] = jnp.sum(
                            jnp.where(hits[e], number[e : e + 1], 0.0), axis=-1, keepdims=True
                        )
                hot = jnp.concatenate([hit.astype(F32).astype(BF16) for hit in hits], axis=0)
                for c in range(0, width, chunk):
                    out_buf[slot, :, c : c + chunk] = dot(hot, in_buf[slot, :, c : c + chunk]).astype(BF16)
                for e in range(local):
                    leaving(step, slot, e).start()
                return carry

            lax.fori_loop(0, seqs, body, 0)
            for step in (seqs - 2, seqs - 1):
                for e in range(local):
                    leaving(jnp.int32(step), step % 2, e).wait()

        pl.run_scoped(
            scoped, pltpu.VMEM((2, length, width), BF16), pltpu.VMEM((2, local * CAP, width), BF16),
            pltpu.SemaphoreType.DMA((2,)), pltpu.SemaphoreType.DMA((2, local)),
        )

    def upstream(y, w, t, sems):
        rows = seqs * CAP
        block = 448 if rows % 448 == 0 else rows

        def body(e, carry):
            loads = [
                pltpu.make_async_copy(O.y.at[e], y, sems.at[0]),
                pltpu.make_async_copy(I.w_down.at[pair_at * local + e], w, sems.at[1]),
            ]
            for copy in loads:
                copy.start()
            for copy in loads:
                copy.wait()

            @pl.when(e >= 1)
            def _():
                pltpu.make_async_copy(t, O.t.at[e], sems.at[2]).wait()

            def part(b, carry):
                span = pl.ds(pl.multiple_of(b * block, 16), block)
                t[span] = dot(y[span], w[...])
                return carry

            lax.fori_loop(0, rows // block, part, 0)
            pltpu.make_async_copy(t, O.t.at[e], sems.at[2]).start()
            return carry

        lax.fori_loop(0, local, body, 0)
        pltpu.make_async_copy(t, O.t.at[0], sems.at[2]).wait()


    def attend_and_project(mixed, sems):
        pl.run_scoped(
            lambda w, n1: attention(w, n1, mixed, sems),
            pltpu.VMEM((width, qkv), BF16), pltpu.VMEM((length, width), BF16),
        )
        for i, copy in enumerate(dy_y):
            copy.wait_recv()
            if i + 1 < n_y:
                dy_y[i + 1].start()
        for i in range(quads):
            dy_core[i].start()
        dy_z.wait_recv()
        dy_zy[0].start()
        dy_core[quads].start()
        ring_end(1)
        pl.run_scoped(
            lambda wo, n2, hid: projection(mixed, wo, n2, hid, sems),
            pltpu.VMEM((width, width), BF16), pltpu.VMEM((length, width), BF16), pltpu.VMEM((length, width), F32),
        )

    pl.run_scoped(attend_and_project, pltpu.VMEM((length, HEADS * HEAD_DIM), BF16), pltpu.SemaphoreType.DMA((3,)))
    for i, copy in enumerate(dy_zy):
        copy.wait_recv()
        if i + 1 < n_y:
            dy_zy[i + 1].start()
    gather(O.dy, O.y, dy_ready, True)
    rows = seqs * CAP
    pl.run_scoped(
        upstream, pltpu.VMEM((rows, width), BF16), pltpu.VMEM((width, ff), BF16), pltpu.VMEM((rows, ff), F32),
        pltpu.SemaphoreType.DMA((3,)),
    )
    gather(O.n2, O.x, n2_ready, False)
    for copy in small + dy_y + [dy_z] + dy_zy + dy_core + n2_pre + [n2_y, n2_z, n2_low, n2_high] + n2_core:
        copy.wait_send()


def front(dims, arrays):
    local, seqs, length, width, ff, n_grp, n_exp, rows_w = dims
    rows = seqs * CAP
    qkv = (HEADS + 2 * KV_HEADS) * HEAD_DIM
    kv = KV_HEADS * HEAD_DIM
    n_y = len(bits_of(n_exp)) - 1
    vmem = dict(
        rank=shape(seqs, 8, length, dtype=jnp.int32),
        gate=shape(local, rows, 1, dtype=F32),
        choice=shape(local, rows, 1, dtype=F32),
        gains=shape(8, width, dtype=F32),
        inv_one=shape(length, 1, dtype=F32),
        inv_two=shape(length, 1, dtype=F32),
        lse=shape(HEADS, length, 1, dtype=F32),
    )
    hbm = dict(
        small=shape(seqs, 8, length, dtype=F32),
        wq=shape(n_grp, rows_w + 16, qkv),
        wo=shape(n_grp, rows_w, width),
        dy=shape(seqs, length, width),
        n2=shape(seqs, length, width),
        n1=shape(length, width),
        q=shape(length, HEADS * HEAD_DIM),
        k=shape(length, kv),
        v=shape(length, kv),
        mixed=shape(length, HEADS * HEAD_DIM),
        hidden=shape(length, width, dtype=F32),
        x=shape(local, rows, width),
        y=shape(local, rows, width),
        t=shape(local, rows, ff, dtype=F32),
    )
    hops = n_grp // 2 + 1
    dma = pltpu.SemaphoreType.DMA
    scratch = dict(
        ring=dma((2, 2, hops, 2)),
        hand=dma((2, 2, hops, 2)),
        own=dma((4,)),
        small=dma((n_y + 2, 2)),
        dy=dma((2 * n_y + 1 + seqs // 2, 2)),
        n2=dma((n_y + 3 + seqs // 2, 2)),
        gate=pltpu.VMEM((seqs, 8, length), F32),
        number=pltpu.VMEM((seqs, 8, length), F32),
    )
    outs = dict(vmem, **hbm)
    in_leaves, in_tree = jax.tree.flatten(arrays)
    far = {id(arrays["w_down"])}
    out_leaves, out_tree = jax.tree.flatten(outs)
    near = {id(value) for value in vmem.values()}
    sem_leaves, sem_tree = jax.tree.flatten(scratch)
    results = pl.pallas_call(
        functools.partial(front_body, dims, in_tree, out_tree, sem_tree),
        in_specs=[ANY if id(leaf) in far else WHOLE for leaf in in_leaves],
        out_specs=[WHOLE if id(leaf) in near else ANY for leaf in out_leaves],
        out_shape=out_leaves,
        scratch_shapes=sem_leaves,
        compiler_params=pltpu.CompilerParams(vmem_limit_bytes=VMEM, collective_id=1, has_side_effects=True),
        name="front",
    )(*in_leaves)
    return space(jax.tree.unflatten(out_tree, results))


def share_rows(width, devices):
    return -(-width // (16 * devices)) * 16


def spread(block, devices):
    rows, width = block.shape
    share = width // devices
    extra = share_rows(width, devices) - share
    if extra == 0:
        return block
    block = jnp.pad(block.reshape(rows, devices, share), ((0, 0), (0, 0), (0, extra)))
    return block.reshape(rows, -1)


def mega_plan(local, seqs, length, width, ff, n_grp, n_exp, rows_w):
    rows = seqs * CAP
    half = length // 2
    quads = seqs // 8
    wide = width + 128
    chunks = 3 * local
    qkv = (HEADS + 2 * KV_HEADS) * HEAD_DIM
    mids = [bit for bit in reversed(bits_of(n_grp)) if bit > PAIR]
    stages = len(bits_of(n_grp)) + len(bits_of(n_exp))
    share = share_rows(width, n_grp * n_exp)
    dma = pltpu.SemaphoreType.DMA

    def returned(w):
        quad = shape(quads, half, w)
        two = shape(2, quads, half, w)
        more = [shape(quads, 2, half, w)] * 2 if quads > 1 else []
        return dict(
            came=shape(seqs // 2, length, w), kept=shape(4, quads, half, w),
            zc=two, yc=two, zcin=two, ycin=two, ylow=quad, zhigh=quad, ylowin=quad, zhighin=quad, more=more,
        )

    def summed(w):
        return dict(
            block=shape(*[2] * stages, share, w),
            came=[shape(*[2] * (stages - 1 - i), share, w) for i in range(stages)],
        )

    gain = shape(8, width, dtype=F32)
    outs = dict(
        layer=shape(length, width),
        d_gates=shape(length, 128, dtype=F32),
        d_tokens=shape(length, width),
        final=shape(3, 2 * local, width // n_grp, ff),
        o_out=shape(share, width, dtype=F32),
        qkv_out=shape(share, qkv, dtype=F32),
        gains=gain,
        theirs=shape(chunks, width // 2, ff),
        mine=shape(chunks, width // 2, ff),
        come=[shape(chunks, width >> (i + 1), ff) for i in range(len(mids) + 1)],
        act=shape(local, rows, ff),
        outs=shape(local, rows, wide),
        far=shape(seqs // 2, length, wide),
        near=shape(seqs // 2, length, wide),
        ret=[returned(width), returned(wide)],
        d_hidden=shape(length, width, dtype=F32),
        sums=[summed(width), summed(qkv)],
        gsum=[gain] * stages,
        gin=[gain] * stages,
    )
    hops = [dma((2, 2)), dma((2, 2)), dma((2, n_exp.bit_length()))]
    sems = dict(
        ret=[dict(core=dma((2, seqs // 2)), hops=hops)] * 2,
        sums=[dma((2, stages))] * 2,
        gall=dma((2, stages)),
        grad=[dma((2, chunks))] * (len(mids) + 1),
        pair=dma((2, chunks)),
        d_gate=pltpu.VMEM((local, rows, 1), F32),
        gain=pltpu.VMEM((8, width), F32),
    )
    return outs, sems


def mega_body(dims, in_tree, out_tree, sem_tree, *refs):
    local, seqs, length, width, ff, n_grp, n_exp, rows_w = dims
    n_in, n_out = in_tree.num_leaves, out_tree.num_leaves
    I = space(jax.tree.unflatten(in_tree, refs[:n_in]))
    O = space(jax.tree.unflatten(out_tree, refs[n_in : n_in + n_out]))
    S = space(jax.tree.unflatten(sem_tree, refs[n_in + n_out :]))
    rows = seqs * CAP
    half = length // 2
    wide = width + 128
    quads = seqs // 8
    qkv = (HEADS + 2 * KV_HEADS) * HEAD_DIM
    grp, exp = lax.axis_index(GRP), lax.axis_index(EXP)
    grp_bits, exp_bits = bits_of(n_grp), bits_of(n_exp)
    me = grp * n_exp + exp
    places, partners = {}, {}
    for axis, index, bits, unit in ((GRP, grp, grp_bits, n_exp), (EXP, exp, exp_bits, 1)):
        for bit in bits:
            place = bit_at(index, bit)
            places[axis, bit] = place
            partners[axis, bit] = me + (1 - 2 * place) * (bit * unit)
    pair_at, x_at = places[GRP, PAIR], places[GRP, 1]
    y_bits = exp_bits[1:]
    mids = [bit for bit in reversed(grp_bits) if bit > PAIR]

    def send(src, dst, sems, axis, bit):
        return pltpu.make_async_remote_copy(
            src_ref=src, dst_ref=dst, send_sem=sems[0], recv_sem=sems[1],
            device_id=partners[axis, bit], device_id_type=pl.DeviceIdType.LOGICAL,
        )

    barrier = pltpu.get_barrier_semaphore()
    for partner in partners.values():
        pl.semaphore_signal(barrier, inc=1, device_id=partner, device_id_type=pl.DeviceIdType.LOGICAL)
    pl.semaphore_wait(barrier, len(partners))


    def grad_send(stage, c):
        sems = S.grad[stage]
        if stage == 0:
            src, bit = O.theirs.at[c], grp_bits[0]
        else:
            bit = mids[stage - 1]
            size = O.come[stage].shape[1]
            place = 1 - places[GRP, bit]
            src = O.come[stage - 1].at[c, pl.ds(pl.multiple_of(place * size, 16), size)]
        return send(src, O.come[stage].at[c], (sems.at[0, c], sems.at[1, c]), GRP, bit)

    def pair_send(c):
        e, k = lax.div(c, jnp.int32(3)), lax.rem(c, jnp.int32(3))
        sems = S.pair
        last = O.come[len(mids)]
        size = last.shape[1] // 2
        return send(
            last.at[c, pl.ds(pl.multiple_of((1 - pair_at) * size, 16), size)], O.final.at[k, pair_at * local + e],
            (sems.at[0, c], sems.at[1, c]), GRP, PAIR,
        )

    def grad_step(stage, c):
        grad_send(stage, c).wait_recv()
        size = O.come[stage].shape[1]
        if stage == 0:
            mine = O.mine.at[c]
        else:
            place = places[GRP, mids[stage - 1]]
            mine = O.come[stage - 1].at[c, pl.ds(pl.multiple_of(place * size, 16), size)]
        parts = 2
        piece = size // parts

        def scoped(a, b, sems):
            def load(p):
                span = pl.ds(p * piece, piece)
                return [
                    pltpu.make_async_copy(mine.at[span], a.at[p], sems.at[p, 0]),
                    pltpu.make_async_copy(O.come[stage].at[c, span], b.at[p], sems.at[p, 1]),
                ]

            for p in range(parts):
                for copy in load(p):
                    copy.start()
            stores = []
            for p in range(parts):
                for copy in load(p):
                    copy.wait()

                a[p] = a[p] + b[p]
                if stage < len(mids):
                    stores.append(pltpu.make_async_copy(
                        a.at[p], O.come[stage].at[c, pl.ds(p * piece, piece)], sems.at[p, 2]
                    ))
                    stores[-1].start()
            if stage == len(mids):
                e, k = lax.div(c, jnp.int32(3)), lax.rem(c, jnp.int32(3))
                stores = [
                    pltpu.make_async_copy(a.at[pair_at], O.final.at[k, pair_at * local + e], sems.at[0, 2]),
                    pltpu.make_async_copy(
                        a.at[1 - pair_at],
                        O.come[stage].at[c, pl.ds(pl.multiple_of((1 - pair_at) * piece, 16), piece)],
                        sems.at[1, 2],
                    ),
                ]
                for copy in stores:
                    copy.start()
            for copy in stores:
                copy.wait()

        pl.run_scoped(
            scoped, pltpu.VMEM((parts, piece, ff), BF16), pltpu.VMEM((parts, piece, ff), BF16),
            pltpu.SemaphoreType.DMA((parts, 3)),
        )
        if stage < len(mids):
            grad_send(stage + 1, c).start()
        else:
            pair_send(c).start()

    def grads(stage, first, last):
        def body(c, carry):
            grad_step(stage, c)
            return carry

        lax.fori_loop(first, last, body, 0)


    block = 448 if rows % 448 == 0 else rows
    piece = width // n_grp
    band = 384
    bands = width // band
    keep = band // 2

    def expert(e, x, y, t, w, gu, d, act, theirs, mine, dx, sems):
        index = pair_at * local + e
        copies = [
            pltpu.make_async_copy(I.x.at[e], x, sems.at[0]),
            pltpu.make_async_copy(I.w_gate.at[index], w.at[:, pl.ds(0, ff)], sems.at[1]),
            pltpu.make_async_copy(I.w_up.at[index], w.at[:, pl.ds(ff, ff)], sems.at[2]),
            pltpu.make_async_copy(I.t.at[e], t, sems.at[3]),
            pltpu.make_async_copy(I.y.at[e], y, sems.at[4]),
        ]
        for copy in copies:
            copy.start()
        for copy in copies[:3]:
            copy.wait()

        def forward(b, carry):
            span = pl.ds(pl.multiple_of(b * block, 16), block)
            gu[...] = dot(x[span], w[...])

            @pl.when(b == 0)
            def _():
                copies[3].wait()

            def point(i, carry):
                inner = pl.ds(pl.multiple_of(i * 64, 64), 64)
                outer = pl.ds(pl.multiple_of(b * block + i * 64, 64), 64)
                g, u = gu[inner, :ff], gu[inner, ff:]
                tt, gate = t[outer], I.gate[e, outer]
                sig = 1.0 / (1.0 + jnp.exp(-g))
                silu = g * sig
                a32 = (silu * u).astype(BF16).astype(F32)
                S.d_gate[e, outer] = jnp.sum(a32 * tt, axis=-1, keepdims=True)
                act[outer] = (a32 * gate).astype(BF16)
                da = gate * tt
                d[outer, :ff] = (da * u * sig * (1.0 + g * (1.0 - sig))).astype(BF16)
                d[outer, ff:] = (da * silu).astype(BF16)
                return carry

            return lax.fori_loop(0, block // 64, point, carry)

        lax.fori_loop(0, rows // block, forward, 0)
        copies[4].wait()
        act_out = pltpu.make_async_copy(act, O.act.at[e], sems.at[0])
        act_out.start()

        def split(j, k, res):
            res = res.astype(BF16)
            for p in range(band // (2 * piece)):
                low = res[2 * p * piece : (2 * p + 1) * piece]
                high = res[(2 * p + 1) * piece : (2 * p + 2) * piece]
                span = pl.ds(pl.multiple_of(j * keep + p * piece, 16), piece)
                theirs[k, span] = jnp.where(x_at == 0, high, low)
                mine[k, span] = jnp.where(x_at == 0, low, high)

        def band_gate(j, carry):
            cols = pl.ds(pl.multiple_of(j * band, 128), band)
            res = dot(x[:, cols], d[...], 0, 0)
            split(j, 0, res[:, :ff])
            split(j, 1, res[:, ff:])
            return carry

        def band_down(j, carry):
            cols = pl.ds(pl.multiple_of(j * band, 128), band)
            split(j, 2, dot(y[:, cols], act[...], 0, 0))
            return carry

        def store(k, many, place):
            return [
                pltpu.make_async_copy(theirs.at[pl.ds(k, many)], O.theirs.at[pl.ds(3 * e + k, many)], sems.at[place]),
                pltpu.make_async_copy(mine.at[pl.ds(k, many)], O.mine.at[pl.ds(3 * e + k, many)], sems.at[place + 1]),
            ]

        lax.fori_loop(0, bands, band_gate, 0)
        early = store(0, 2, 1)
        for copy in early:
            copy.start()
        lax.fori_loop(0, bands, band_down, 0)
        late = store(2, 1, 3)
        for copy in late:
            copy.start()
        for copy in early:
            copy.wait()
        for k in range(2):
            grad_send(0, 3 * e + k).start()

        def back(b, carry):
            span = pl.ds(pl.multiple_of(b * block, 16), block)
            for c in range(0, width, 512):
                dx[span, c : c + 512] = dot(d[span], w[c : c + 512], 1, 1).astype(BF16)
            return carry

        lax.fori_loop(0, rows // block, back, 0)
        dx_out = pltpu.make_async_copy(dx, O.outs.at[e, :, pl.ds(0, width)], sems.at[5])
        dx_out.start()
        for copy in late:
            copy.wait()
        grad_send(0, 3 * e + 2).start()
        act_out.wait()
        dx_out.wait()

    def experts(*scratch):
        def body(e, carry):
            expert(e, *scratch)
            if local == 4:
                grads(0, lax.max(e - 1, 0), e + lax.div(e, jnp.int32(3)))
            return carry

        lax.fori_loop(0, local, body, 0)


    def collapse(tag, w):
        first = seqs // 2
        far, near = O.far, O.near
        cols = pl.ds(0, w)
        spans = [(c, min(512, w - c)) for c in range(0, w, 512)]

        def scoped(in_buf, out_buf, in_sem, out_sem):
            def coming(step, slot, e):
                s = lax.rem(step + first, jnp.int32(seqs))
                return pltpu.make_async_copy(
                    O.outs.at[e, pl.ds(pl.multiple_of(s * CAP, 16), CAP), cols],
                    in_buf.at[slot, pl.ds(e * CAP, CAP)],
                    in_sem.at[slot, e],
                )

            def leave(step, slot):
                pltpu.make_async_copy(out_buf.at[slot], near.at[0, :, cols], out_sem.at[slot]).wait()

                @pl.when(step < first)
                def _():
                    core_send(tag, step).start()

            for e in range(local):
                coming(0, 0, e).start()

            def body(step, carry):
                slot = lax.rem(step, jnp.int32(2))

                @pl.when(step + 1 < seqs)
                def _():
                    for e in range(local):
                        coming(step + 1, 1 - slot, e).start()

                for e in range(local):
                    coming(step, slot, e).wait()

                @pl.when(step >= 2)
                def _():
                    leave(step - 2, slot)

                hot = hot_rows(I.rank, lax.rem(step + first, jnp.int32(seqs)), local, length)
                for c, span in spans:
                    out_buf[slot, :, c : c + span] = dot(hot, in_buf[slot, :, c : c + span], 0, 0).astype(BF16)

                @pl.when(step < first)
                def _():
                    pltpu.make_async_copy(out_buf.at[slot], far.at[step, :, cols], out_sem.at[slot]).start()

                @pl.when(step >= first)
                def _():
                    pltpu.make_async_copy(out_buf.at[slot], near.at[step - first, :, cols], out_sem.at[slot]).start()

                return carry

            lax.fori_loop(0, seqs, body, 0)
            for step in (seqs - 2, seqs - 1):
                leave(step, step % 2)

        pl.run_scoped(
            scoped,
            pltpu.VMEM((2, local * CAP, w), BF16),
            pltpu.VMEM((2, length, w), BF16),
            pltpu.SemaphoreType.DMA((2, local)),
            pltpu.SemaphoreType.DMA((2,)),
        )

    def core_send(tag, s):
        sems = S.ret[tag].core
        came = O.ret[tag].came
        src = O.far.at[s, :, pl.ds(0, came.shape[2])]
        return send(src, came.at[s], (sems.at[0, s], sems.at[1, s]), EXP, CORE)

    def hop(tag, number, which):
        sems = S.ret[tag].hops[number - 1]
        pair = (sems.at[0, which], sems.at[1, which])
        r = O.ret[tag]
        src, dst = [(r.zc, r.zcin), (r.yc, r.ycin), (r.ylow, r.ylowin), (r.zhigh, r.zhighin)][2 * (number - 1) + which]
        across = (number == 1) == (which == 0)
        axis, bit = (GRP, PAIR) if across else (EXP, y_bits[-1])
        return send(src, dst, pair, axis, bit)

    def blend(pieces, w):
        def scoped(a, b, load_sem, store_sem):
            def load(i):
                slot = i % 2
                first, second = pieces[i][0]
                return [
                    pltpu.make_async_copy(first, a.at[slot], load_sem.at[slot, 0]),
                    pltpu.make_async_copy(second, b.at[slot], load_sem.at[slot, 1]),
                ]

            def store(i):
                return pltpu.make_async_copy(a.at[i % 2], pieces[i][1], store_sem.at[i % 2])

            for copy in load(0):
                copy.start()
            for i in range(len(pieces)):
                if i >= 1:
                    store(i - 1).wait()
                if i + 1 < len(pieces):
                    for copy in load(i + 1):
                        copy.start()
                for copy in load(i):
                    copy.wait()
                a[i % 2] = a[i % 2] + b[i % 2]
                store(i).start()
            store(len(pieces) - 1).wait()

        pl.run_scoped(
            scoped, pltpu.VMEM((2, half, w), BF16), pltpu.VMEM((2, half, w), BF16),
            pltpu.SemaphoreType.DMA((2, 2)), pltpu.SemaphoreType.DMA((2,)),
        )

    low, high = pl.ds(0, half), pl.ds(half, half)

    def return_one(tag, w):
        for s in range(seqs // 2):
            core_send(tag, s).wait_recv()
        near, came = O.near, O.ret[tag].came

        def piece_of(quad, j, part, to):
            s = quad * quads + j
            return ((near.at[s, part, pl.ds(0, w)], came.at[s, part]), to)

        zc, yc, kept = O.ret[tag].zc, O.ret[tag].yc, O.ret[tag].kept
        every = range(quads)
        blend(
            [piece_of(2, j, low, zc.at[0, j]) for j in every]
            + [piece_of(3, j, low, zc.at[1, j]) for j in every],
            w,
        )
        hop(tag, 1, 0).start()
        blend(
            [piece_of(1, j, high, yc.at[0, j]) for j in every]
            + [piece_of(3, j, high, yc.at[1, j]) for j in every],
            w,
        )
        hop(tag, 1, 1).start()
        blend(
            [piece_of(1, j, low, kept.at[2, j]) for j in every]
            + [piece_of(2, j, high, kept.at[3, j]) for j in every]
            + [piece_of(0, j, low, kept.at[0, j]) for j in every]
            + [piece_of(0, j, high, kept.at[1, j]) for j in every],
            w,
        )

    def return_two(tag, w):
        kept = O.ret[tag].kept
        every = range(quads)
        hop(tag, 1, 0).wait_recv()
        blend([((kept.at[2, j], O.ret[tag].zcin.at[1, j]), O.ret[tag].ylow.at[j]) for j in every], w)
        hop(tag, 2, 0).start()
        hop(tag, 1, 1).wait_recv()
        blend([((kept.at[3, j], O.ret[tag].ycin.at[1, j]), O.ret[tag].zhigh.at[j]) for j in every], w)
        hop(tag, 2, 1).start()

    def return_end(tag, w):
        for which in range(2):
            hop(tag, 2, which).wait_recv()
        kept = O.ret[tag].kept
        terms = [
            [[kept.at[0, j], O.ret[tag].zcin.at[0, j], O.ret[tag].ylowin.at[j]] for j in range(quads)],
            [[kept.at[1, j], O.ret[tag].ycin.at[0, j], O.ret[tag].zhighin.at[j]] for j in range(quads)],
        ]
        if quads == 1:
            return [terms[0][0], terms[1][0]]
        tot, came = O.ret[tag].more
        for part in range(2):
            for j in range(quads):
                a, b, c = terms[part][j]
                blend([((a, b), tot.at[j, part])], w)
                blend([((tot.at[j, part], c), tot.at[j, part])], w)
        count = quads
        for i, bit in enumerate(reversed(y_bits[:-1])):
            count //= 2
            sems = S.ret[tag].hops[2]
            copy = send(
                tot.at[pl.ds(count, count)], came.at[pl.ds(count, count)],
                (sems.at[0, i], sems.at[1, i]), EXP, bit,
            )
            copy.start()
            copy.wait()
            for j in range(count):
                for part in range(2):
                    blend([((tot.at[j, part], came.at[count + j, part]), tot.at[j, part])], w)
        return [[tot.at[0, 0]], [tot.at[0, 1]]]

    def return_close(tag):
        for number in (1, 2):
            for which in range(2):
                hop(tag, number, which).wait_send()

    def output_phase(act, w, res, sems):
        def load(e, slot):
            return [
                pltpu.make_async_copy(O.act.at[e], act.at[slot], sems.at[slot, 0]),
                pltpu.make_async_copy(I.w_down.at[pair_at * local + e], w.at[slot], sems.at[slot, 1]),
            ]

        def store(e, slot):
            return pltpu.make_async_copy(res.at[slot], O.outs.at[e], sems.at[slot, 2])

        for copy in load(0, 0):
            copy.start()

        def body(e, carry):
            slot = lax.rem(e, jnp.int32(2))

            @pl.when(e + 1 < local)
            def _():
                for copy in load(e + 1, 1 - slot):
                    copy.start()

            for copy in load(e, slot):
                copy.wait()

            @pl.when(e >= 2)
            def _():
                store(e - 2, slot).wait()

            def part(b, carry):
                span = pl.ds(pl.multiple_of(b * block, 16), block)
                for c in range(0, width, 512):
                    res[slot, span, c : c + 512] = dot(act[slot, span], w[slot, c : c + 512], 1, 1).astype(BF16)
                value = S.d_gate[e, span]
                top = value.astype(BF16).astype(F32)
                lane = lax.broadcasted_iota(jnp.int32, (block, 128), 1).astype(F32)
                choice = I.choice[e, span]
                res[slot, span, width:] = jnp.where(
                    lane == choice, top, jnp.where(lane == choice + TOP, value - top, 0.0)
                ).astype(BF16)
                return carry

            lax.fori_loop(0, rows // block, part, 0)
            store(e, slot).start()
            return carry

        lax.fori_loop(0, local, body, 0)
        for e in range(max(0, local - 2), local):
            store(e, e % 2).wait()


    order = [(EXP, bit) for bit in exp_bits] + [(GRP, bit) for bit in [PAIR] + mids + [1]]
    left = [(GRP, bit) for bit in reversed(grp_bits)] + [(EXP, bit) for bit in reversed(exp_bits)]
    axis_of = []
    for name in order:
        axis_of.append(left.index(name))
        left.remove(name)
    share = share_rows(width, n_grp * n_exp)

    def all_part(tag, i, place):
        block = O.sums[tag].came[i - 1] if i else O.sums[tag].block
        return block.at[(slice(None),) * axis_of[i] + (place,)]

    def all_send(tag, i):
        sems = S.sums[tag]
        return send(
            all_part(tag, i, 1 - places[order[i]]), O.sums[tag].came[i], (sems.at[0, i], sems.at[1, i]), *order[i]
        )

    def all_step(tag, i):
        all_send(tag, i).wait_recv()
        came = O.sums[tag].came[i]
        last = i + 1 == len(order)

        def scoped(a, b, *rest):
            sems = rest[-1]
            loads = [
                pltpu.make_async_copy(all_part(tag, i, places[order[i]]), a, sems.at[0]),
                pltpu.make_async_copy(came, b, sems.at[1]),
            ]
            for copy in loads:
                copy.start()
            for copy in loads:
                copy.wait()
            if last:
                rest[0][...] = a[...].astype(F32) + b[...].astype(F32)
                store = pltpu.make_async_copy(rest[0], (O.qkv_out if tag else O.o_out), sems.at[0])
            else:
                lead = len(came.shape) - 2
                inner = max(0, lead - 1)

                def body(j, carry):
                    spots, rest_of = [], j
                    for _ in range(inner):
                        spots.insert(0, lax.rem(rest_of, jnp.int32(2)))
                        rest_of = lax.div(rest_of, jnp.int32(2))
                    spots = tuple(spots)
                    a[spots] = a[spots] + b[spots]
                    return carry

                lax.fori_loop(0, 2**inner, body, 0)
                store = pltpu.make_async_copy(a, came, sems.at[0])
            store.start()
            store.wait()

        buffer = pltpu.VMEM(came.shape, BF16)
        more = [pltpu.VMEM(came.shape, F32)] if last else []
        pl.run_scoped(scoped, buffer, buffer, *more, pltpu.SemaphoreType.DMA((2,)))
        if not last:
            all_send(tag, i + 1).start()

    def gain_send(i):
        axis, bit = order[i]
        sems = S.gall
        return send(O.gsum[i], O.gin[i], (sems.at[0, i], sems.at[1, i]), axis, bit)

    def gain_step(i):
        gain_send(i).wait_recv()

        def scoped(a, sems):
            came = pltpu.make_async_copy(O.gin[i], a, sems.at[0])
            came.start()
            came.wait()
            S.gain[...] = S.gain[...] + a[...]
            to = O.gains if i + 1 == len(order) else O.gsum[i + 1]
            store = pltpu.make_async_copy(S.gain, to, sems.at[0])
            store.start()
            store.wait()

        pl.run_scoped(scoped, pltpu.VMEM((8, width), F32), pltpu.SemaphoreType.DMA((1,)))
        if i + 1 < len(order):
            gain_send(i + 1).start()


    def norm_back(up, z, inverse, gain):
        normal = z * inverse
        scaled = up * gain
        mean = jnp.mean(scaled * normal, axis=-1, keepdims=True)
        return normal, inverse * (scaled - normal * mean)

    chunk_rows = 64

    def hidden_grad(terms, branch, dm, dh, wo, sems):
        for i in range(n_grp):
            pltpu.make_async_copy(I.wo.at[i], wo.at[pl.ds(i * rows_w, rows_w)], sems.at[0]).start()
        S.gain[...] = jnp.zeros_like(S.gain)

        def scoped(bufs, hid, up):
            for part in range(2):
                span = pl.ds(part * half, half)
                loads = [
                    pltpu.make_async_copy(term, bufs.at[i], sems.at[1 + i]) for i, term in enumerate(terms[part])
                ] + [
                    pltpu.make_async_copy(I.hidden.at[span], hid, sems.at[4]),
                    pltpu.make_async_copy(I.dy.at[span], up, sems.at[5]),
                ]
                for copy in loads:
                    copy.start()
                for copy in loads:
                    copy.wait()

                def body(j, carry):
                    r = pl.ds(pl.multiple_of(j * chunk_rows, chunk_rows), chunk_rows)
                    big = pl.ds(pl.multiple_of(part * half + j * chunk_rows, chunk_rows), chunk_rows)
                    d_n2 = bufs[0, r].astype(F32)
                    for i in range(1, len(terms[part])):
                        d_n2 = d_n2 + bufs[i, r].astype(F32)
                    normal, back = norm_back(d_n2, hid[r], I.inv_two[big], I.gains[1:2])
                    value = up[r].astype(F32) + back
                    dh[big] = value
                    branch[big] = value.astype(BF16)
                    S.gain[1:2] = S.gain[1:2] + jnp.sum(d_n2 * normal, axis=0, keepdims=True)
                    return carry

                lax.fori_loop(0, half // chunk_rows, body, 0)

        count = len(terms[0])
        pl.run_scoped(
            scoped, pltpu.VMEM((count, half, width), BF16), pltpu.VMEM((half, width), F32), pltpu.VMEM((half, width), BF16)
        )
        dh_out = pltpu.make_async_copy(dh, O.d_hidden, sems.at[1])
        dh_out.start()
        pltpu.make_async_copy(wo, wo, sems.at[0]).wait()

        def body(j, carry):
            r = pl.ds(pl.multiple_of(j * 256, 256), 256)
            for c in range(0, width, 512):
                dm[r, c : c + 512] = dot(branch[r], wo[c : c + 512], 1, 1).astype(BF16)
            return carry

        lax.fori_loop(0, length // 256, body, 0)
        dh_out.wait()

    def outer_grad(left, right, tag, buf, sems):
        dims = buf.shape[1:]
        lead = len(O.sums[tag].block.shape) - len(dims)
        steps = 2**lead
        tall = left.shape[1] // steps

        def store(j):
            spots, rest = [], j
            for _ in range(lead):
                spots.insert(0, lax.rem(rest, 2))
                rest = lax.div(rest, 2)
            slot = lax.rem(j, 2)
            return pltpu.make_async_copy(buf.at[slot], O.sums[tag].block.at[tuple(spots)], sems.at[slot])

        def body(j, carry):
            @pl.when(j >= 2)
            def _():
                store(j - 2).wait()

            cols = pl.ds(pl.multiple_of(j * tall, 128), tall)
            w = right.shape[1]
            for c in range(0, w, 512):
                part = dot(left[:, cols], right[:, c : c + 512], 0, 0).astype(BF16)
                buf[(lax.rem(j, 2),) + (slice(None),) * (len(dims) - 1) + (slice(c, c + 512),)] = part.reshape(
                    *dims[:-1], 512
                )
            store(j).start()
            return carry

        lax.fori_loop(0, steps, body, 0)
        for j in (steps - 2, steps - 1):
            store(jnp.int32(j)).wait()
        all_send(tag, 0).start()

    def attention(q, k, v, mixed, dm, dqkv, mask, dk_acc, dv_acc, dq_acc):
        for r in range(0, length, 256):
            key = lax.broadcasted_iota(jnp.int32, (256, length), 0) + r
            query = lax.broadcasted_iota(jnp.int32, (256, length), 1)
            tag = I.tagc[r : r + 256]
            inside = (tag == I.tagr[...]) & (tag > 0)
            mask[r : r + 256] = jnp.where((key <= query) | inside, 0.0, -1e30)

        def unturn(w):
            return w * I.cos[...] - pltpu.roll(w, HEAD_DIM // 2, 1) * I.sin[...]

        per = HEADS // KV_HEADS
        ones = jnp.ones((8, HEAD_DIM), F32)
        for g in range(KV_HEADS):
            kv = slice(g * HEAD_DIM, (g + 1) * HEAD_DIM)
            dk_acc[...] = jnp.zeros_like(dk_acc)
            dv_acc[...] = jnp.zeros_like(dv_acc)

            def head(i, carry):
                h = g * per + i
                cols = pl.ds(pl.multiple_of(h * HEAD_DIM, HEAD_DIM), HEAD_DIM)
                product = dm[:, cols].astype(F32) * mixed[:, cols].astype(F32)
                delta = lax.dot_general(
                    ones, product, (((1,), (1,)), ((), ())),
                    precision=lax.Precision.HIGHEST, preferred_element_type=F32,
                )[:1]
                lse = I.lse[h]
                dq_acc[...] = jnp.zeros_like(dq_acc)
                for r in range(0, length, 256):
                    start = max(0, r - 256)
                    qq, mm = q[start:, cols], dm[start:, cols]
                    kk, vv = k[r : r + 256, kv], v[r : r + 256, kv]
                    s = dot(kk, qq, 1, 1) * SCALE + mask[r : r + 256, start:]
                    p = jnp.exp(s - lse[:, start:])
                    dp = dot(vv, mm, 1, 1)
                    ds = (p * (dp - delta[:, start:])).astype(BF16)
                    dk_acc[r : r + 256] += dot(ds, qq)
                    dv_acc[r : r + 256] += dot(p.astype(BF16), mm)
                    dq_acc[start:] += dot(ds, kk, 0, 0)
                dqkv[:, cols] = unturn(dq_acc[...] * SCALE).astype(BF16)
                return carry

            lax.fori_loop(0, per, head, 0)
            first = HEADS * HEAD_DIM + g * HEAD_DIM
            dqkv[:, first : first + HEAD_DIM] = unturn(dk_acc[...] * SCALE).astype(BF16)
            first += KV_HEADS * HEAD_DIM
            dqkv[:, first : first + HEAD_DIM] = dv_acc[...].astype(BF16)

    def token_grad(dqkv, wqkv, sems):
        for i in range(n_grp):
            pltpu.make_async_copy(
                I.wqkv.at[i, pl.ds(0, rows_w)], wqkv.at[pl.ds(i * rows_w, rows_w)], sems.at[0]
            ).start()

        def scoped(dn, dh, x, res):
            pltpu.make_async_copy(wqkv, wqkv, sems.at[0]).wait()
            for part in range(2):
                span = pl.ds(part * half, half)
                loads = [
                    pltpu.make_async_copy(O.d_hidden.at[span], dh, sems.at[1]),
                    pltpu.make_async_copy(I.tokens.at[span], x, sems.at[2]),
                ]
                for copy in loads:
                    copy.start()
                for c in range(0, width, 512):
                    dn[:, c : c + 512] = dot(dqkv[part * half : (part + 1) * half], wqkv[c : c + 512], 1, 1)
                for copy in loads:
                    copy.wait()

                def body(j, carry):
                    r = pl.ds(pl.multiple_of(j * chunk_rows, chunk_rows), chunk_rows)
                    big = pl.ds(pl.multiple_of(part * half + j * chunk_rows, chunk_rows), chunk_rows)
                    d_n1 = dn[r]
                    normal, back = norm_back(d_n1, x[r].astype(F32), I.inv_one[big], I.gains[0:1])
                    res[r] = (dh[r] + back).astype(BF16)
                    S.gain[0:1] = S.gain[0:1] + jnp.sum(d_n1 * normal, axis=0, keepdims=True)
                    return carry

                lax.fori_loop(0, half // chunk_rows, body, 0)
                store = pltpu.make_async_copy(res, O.d_tokens.at[span], sems.at[3])
                store.start()
                store.wait()

        pl.run_scoped(
            scoped, pltpu.VMEM((half, width), F32), pltpu.VMEM((half, width), F32),
            pltpu.VMEM((half, width), BF16), pltpu.VMEM((half, width), BF16),
        )
        store = pltpu.make_async_copy(S.gain, O.gsum[0], sems.at[0])
        store.start()
        store.wait()
        gain_send(0).start()

    def layer_end(terms):
        def scoped(bufs, hid, res, extra, sems):
            for part in range(2):
                span = pl.ds(part * half, half)
                loads = [
                    pltpu.make_async_copy(term, bufs.at[i], sems.at[i]) for i, term in enumerate(terms[part])
                ] + [pltpu.make_async_copy(I.hidden.at[span], hid, sems.at[3])]
                for copy in loads:
                    copy.start()
                for copy in loads:
                    copy.wait()

                def body(j, carry):
                    r = pl.ds(pl.multiple_of(j * chunk_rows, chunk_rows), chunk_rows)
                    total = bufs[0, r].astype(F32)
                    for i in range(1, len(terms[part])):
                        total = total + bufs[i, r].astype(F32)
                    res[r] = (hid[r] + total[:, :width]).astype(BF16)
                    extra[r] = total[:, width:]
                    return carry

                lax.fori_loop(0, half // chunk_rows, body, 0)
                stores = [
                    pltpu.make_async_copy(res, O.layer.at[span], sems.at[0]),
                    pltpu.make_async_copy(extra, O.d_gates.at[span], sems.at[1]),
                ]
                for copy in stores:
                    copy.start()
                for copy in stores:
                    copy.wait()

        pl.run_scoped(
            scoped, pltpu.VMEM((len(terms[0]), half, wide), BF16), pltpu.VMEM((half, width), F32),
            pltpu.VMEM((half, width), BF16), pltpu.VMEM((half, 128), F32), pltpu.SemaphoreType.DMA((4,)),
        )


    chunks = 3 * local
    done = [4 if local == 4 else 0] + [0] * len(mids)

    def pump(*upto):
        for stage, last in enumerate(upto):
            if stage >= len(done):
                continue
            if local != 4 and last < chunks:
                continue
            if done[stage] < last:
                grads(stage, done[stage], last)
                done[stage] = last

    pl.run_scoped(
        experts,
        pltpu.VMEM((rows, width), BF16),
        pltpu.VMEM((rows, width), BF16),
        pltpu.VMEM((rows, ff), F32),
        pltpu.VMEM((width, 2 * ff), BF16),
        pltpu.VMEM((block, 2 * ff), F32),
        pltpu.VMEM((rows, 2 * ff), BF16),
        pltpu.VMEM((rows, ff), BF16),
        pltpu.VMEM((3, width // 2, ff), BF16),
        pltpu.VMEM((3, width // 2, ff), BF16),
        pltpu.VMEM((rows, width), BF16),
        pltpu.SemaphoreType.DMA((6,)),
    )
    pump(4, 1)
    collapse(0, width)
    pump(5, 2)
    pl.run_scoped(
        output_phase,
        pltpu.VMEM((2, rows, ff), BF16),
        pltpu.VMEM((2, width, ff), BF16),
        pltpu.VMEM((2, rows, wide), BF16),
        pltpu.SemaphoreType.DMA((2, 3)),
    )
    return_one(0, width)
    pump(6, 3)
    for s in range(seqs // 2):
        core_send(0, s).wait_send()
    collapse(1, wide)
    pump(7, 4)
    return_two(0, width)
    return_one(1, wide)
    pump(8, 5)

    def backward(branch, dm, mixed, sems):
        load = pltpu.make_async_copy(I.mixed, mixed, sems.at[0])
        load.start()
        load.wait()
        terms = return_end(0, width)
        pl.run_scoped(
            functools.partial(hidden_grad, terms, branch, dm),
            pltpu.VMEM((length, width), F32), pltpu.VMEM((width, width), BF16), pltpu.SemaphoreType.DMA((6,)),
        )
        pump(9, 6)
        def out_grad(left, buf, own):
            load = pltpu.make_async_copy(I.mixed_wide, left, own.at[0])
            load.start()
            load.wait()
            outer_grad(left, branch, 0, buf, own)

        tall = share * n_grp * n_exp
        step = [2] * 3 if share > 16 else [2] * 4
        pl.run_scoped(
            out_grad, pltpu.VMEM((length, tall), BF16), pltpu.VMEM((2, *step, share, width), BF16), pltpu.SemaphoreType.DMA((2,))
        )

        def rest(dqkv):
            def first(q, k, v, *acc):
                loads = [
                    pltpu.make_async_copy(I.q, q, sems.at[0]),
                    pltpu.make_async_copy(I.k, k, sems.at[1]),
                    pltpu.make_async_copy(I.v, v, sems.at[2]),
                ]
                for copy in loads:
                    copy.start()
                for copy in loads:
                    copy.wait()
                attention(q, k, v, mixed, dm, dqkv, *acc)

            kv = KV_HEADS * HEAD_DIM
            pl.run_scoped(
                first, pltpu.VMEM((length, width), BF16), pltpu.VMEM((length, kv), BF16), pltpu.VMEM((length, kv), BF16),
                pltpu.VMEM((length, length), F32), pltpu.VMEM((length, HEAD_DIM), F32),
                pltpu.VMEM((length, HEAD_DIM), F32), pltpu.VMEM((length, HEAD_DIM), F32),
            )
            pump(10, 7)
            all_step(0, 0)
            pl.run_scoped(
                functools.partial(token_grad, dqkv),
                pltpu.VMEM((width, qkv), BF16), pltpu.SemaphoreType.DMA((4,)),
            )

            def second(n1, buf, own):
                load = pltpu.make_async_copy(I.n1, n1, own.at[0])
                load.start()
                load.wait()
                outer_grad(n1, dqkv, 1, buf, own)

            pl.run_scoped(
                second, pltpu.VMEM((length, tall), BF16), pltpu.VMEM((2, *step, share, qkv), BF16), pltpu.SemaphoreType.DMA((2,))
            )

        pl.run_scoped(rest, pltpu.VMEM((length, qkv), BF16))

    pl.run_scoped(
        backward, pltpu.VMEM((length, width), BF16), pltpu.VMEM((length, width), BF16),
        pltpu.VMEM((length, width), BF16), pltpu.SemaphoreType.DMA((3,)),
    )
    pump(11, 8)
    return_two(1, wide)
    all_step(1, 0)
    gain_step(0)
    all_step(0, 1)
    pump(12, 9)
    all_step(1, 1)
    gain_step(1)
    all_step(0, 2)
    layer_end(return_end(1, wide))
    pump(12, 10)
    for i in range(2, len(order)):
        all_step(1, i)
        gain_step(i)
        if i + 1 < len(order):
            all_step(0, i + 1)
        if i == 2:
            pump(12, 11)
    pump(*([chunks] * (len(mids) + 1)))

    def close(c, carry):
        for stage in range(len(mids) + 1):
            grad_send(stage, c).wait_send()
        pair_send(c).wait()
        return carry

    lax.fori_loop(0, chunks, close, 0)
    return_close(0)
    return_close(1)
    for s in range(seqs // 2):
        core_send(1, s).wait_send()
    for i in range(len(order)):
        all_send(0, i).wait_send()
        all_send(1, i).wait_send()
        gain_send(i).wait_send()


def mega(dims, arrays, near):
    outs, sems = mega_plan(*dims)
    in_leaves, in_tree = jax.tree.flatten(dict(arrays, **near))
    inside = {id(value) for value in near.values()}
    out_leaves, out_tree = jax.tree.flatten(outs)
    sem_leaves, sem_tree = jax.tree.flatten(sems)
    results = pl.pallas_call(
        functools.partial(mega_body, dims, in_tree, out_tree, sem_tree),
        in_specs=[WHOLE if id(leaf) in inside else ANY for leaf in in_leaves],
        out_specs=[ANY] * len(out_leaves),
        out_shape=out_leaves,
        scratch_shapes=sem_leaves,
        compiler_params=pltpu.CompilerParams(vmem_limit_bytes=VMEM, collective_id=0, has_side_effects=True),
        name="experts_and_back",
    )(*in_leaves)
    return space(jax.tree.unflatten(out_tree, results))


def shards(
    tokens,
    cotangent,
    gate_logits,
    routes,
    piece_starts,
    piece_kinds,
    q_weight,
    k_weight,
    v_weight,
    o_weight,
    attn_gain,
    moe_gain,
    gate_weight,
    up_weight,
    down_weight,
):
    grp, exp = lax.axis_index(GRP), lax.axis_index(EXP)
    n_grp, n_exp = lax.axis_size(GRP), lax.axis_size(EXP)
    devices = n_grp * n_exp
    length, width = tokens.shape
    local = gate_weight.shape[0] // 2
    q_width, kv_width = q_weight.shape[1], k_weight.shape[1]
    rows_w = q_weight.shape[0]
    dims = (local, 2 * n_exp, length, width, gate_weight.shape[2], n_grp, n_exp, rows_w)

    gates = jax.nn.softmax(gate_logits, axis=-1)
    small = jnp.concatenate([routes.T.astype(F32), gates.T], axis=0)
    gains = jnp.pad(jnp.stack([attn_gain, moe_gain]), ((0, 14), (0, q_width + 2 * kv_width - rows_w)))
    shard = jnp.concatenate([jnp.concatenate([q_weight, k_weight, v_weight], axis=1), gains], axis=0)
    cosine, sine = rope_tables(length)
    tags = piece_tags(piece_starts[0], piece_kinds[0], length)
    tagc, tagr = tags.reshape(length, 1), tags.reshape(1, length)

    a = front(
        dims,
        dict(
            tokens=tokens, dy=cotangent, small=small, wq=shard, wo=o_weight, w_down=down_weight,
            cos=cosine, sin=sine, tagc=tagc, tagr=tagr,
        ),
    )
    r = mega(
        dims,
        dict(
            x=a.x, y=a.y, t=a.t, w_gate=gate_weight, w_up=up_weight, w_down=down_weight, hidden=a.hidden,
            dy=cotangent, wo=a.wo, mixed=a.mixed, q=a.q, k=a.k, v=a.v, wqkv=a.wq, tokens=tokens,
            n1=spread(a.n1, devices), mixed_wide=spread(a.mixed, devices),
        ),
        dict(
            gate=a.gate, choice=a.choice, rank=a.rank, inv_one=a.inv_one, inv_two=a.inv_two, gains=a.gains,
            lse=a.lse.reshape(HEADS, 1, length), cos=cosine, sin=sine, tagc=tagc, tagr=tagr,
        ),
    )
    d_gates = r.d_gates[:, :TOP] + r.d_gates[:, TOP : 2 * TOP]
    logits_grad = gates * (d_gates - jnp.sum(gates * d_gates, axis=-1, keepdims=True))
    share = width // devices
    own = lax.dynamic_slice_in_dim(r.gains, (grp * n_exp + exp) * share, share, 1)
    return (
        r.layer,
        r.d_tokens,
        logits_grad,
        r.qkv_out[:share, :q_width],
        r.qkv_out[:share, q_width : q_width + kv_width],
        r.qkv_out[:share, q_width + kv_width :],
        r.o_out[:share],
        own[0],
        own[1],
        *[r.final[kind].astype(F32) for kind in range(3)],
    )


def solution(mesh):
    rows = P((GRP, EXP), None)
    placed = (rows,) * 6 + (P(GRP, None),) * 4 + (P(GRP),) * 2 + (P(EXP, None, None),) * 3
    outs = (rows,) * 7 + (P((GRP, EXP)),) * 2 + (P(EXP, GRP, None),) * 3
    return jax.shard_map(shards, mesh=mesh, in_specs=placed, out_specs=outs, check_vma=False)
```

```python
import functools
from types import SimpleNamespace

import jax
import jax.numpy as jnp
import numpy as np
from jax import lax
from jax.experimental import pallas as pl
from jax.experimental.pallas import tpu as pltpu
from jax.sharding import PartitionSpec as P

HEADS = 12
KV_HEADS = 2
HEAD_DIM = 128
EXPERTS = 32
TOP = 4
CAP = 112
EPSILON = 1e-06
THETA = 1000000.0
SCALE = HEAD_DIM ** (-0.5)
GRP = "grp"
EXP = "exp"
CORE = 1
PAIR = 2
VMEM = 58 * 1024 * 1024
BF16 = jnp.bfloat16
F32 = jnp.float32


def bits_of(size):
    return [1 << i for i in range(size.bit_length() - 1)]


def bit_at(index, bit):
    return lax.rem(lax.div(index, jnp.int32(bit)), jnp.int32(2))


def space(tree):
    if isinstance(tree, dict):
        return SimpleNamespace(**{name: space(value) for name, value in tree.items()})
    return [space(value) for value in tree] if isinstance(tree, list) else tree


def rope_tables(length):
    half = HEAD_DIM // 2
    frequency = THETA ** (-2.0 * np.arange(half) / HEAD_DIM)
    angles = np.arange(length)[:, None] * frequency[None, :]
    cosine, sine = np.cos(angles), np.sin(angles)
    tables = [np.concatenate([cosine, cosine], axis=1), np.concatenate([-sine, sine], axis=1)]
    return [jnp.asarray(table.astype(np.float32)) for table in tables]


def piece_tags(starts, kinds, length):
    places = jnp.arange(length, dtype=jnp.int32)
    piece_of = jnp.sum((places[:, None] >= starts[None, :]).astype(jnp.int32), axis=1) - 1
    slot_ids = jnp.arange(starts.shape[0], dtype=jnp.int32)
    kind_of = jnp.sum(jnp.where(piece_of[:, None] == slot_ids[None, :], kinds[None, :], 0), axis=1)
    return jnp.where(kind_of == 1, piece_of + 1, 0)


def call(body, **kw):
    params = pltpu.CompilerParams(vmem_limit_bytes=VMEM)
    cost = pl.CostEstimate(flops=1, bytes_accessed=1, transcendentals=0)
    return pl.pallas_call(body, compiler_params=params, cost_estimate=cost, **kw)


def shape(*dims, dtype=BF16):
    return jax.ShapeDtypeStruct(dims, dtype)


def dot(a, b, ca=1, cb=0):
    return lax.dot_general(a, b, (((ca,), (cb,)), ((), ())), preferred_element_type=F32)


ANY = pl.BlockSpec(memory_space=pl.ANY)
WHOLE = pl.BlockSpec(memory_space=pltpu.VMEM)
SCALAR = pl.BlockSpec(memory_space=pltpu.SMEM)


def fixed(*dims):
    return pl.BlockSpec(dims, lambda *_: (0,) * len(dims))


def shape(*dims, dtype=BF16):
    return jax.ShapeDtypeStruct(dims, dtype)


def dot(a, b, ca=1, cb=0):
    return lax.dot_general(a, b, (((ca,), (cb,)), ((), ())), preferred_element_type=F32)


ANY = pl.BlockSpec(memory_space=pl.ANY)
WHOLE = pl.BlockSpec(memory_space=pltpu.VMEM)


def hot_rows(rank, s, local, length):
    spot = lax.broadcasted_iota(jnp.int32, (CAP, length), 0)
    picked = rank[s]
    return jnp.concatenate(
        [(picked[e : e + 1] == spot).astype(F32).astype(BF16) for e in range(local)], axis=0
    )


def ring_spot(group, size):
    odd = lax.rem(group, jnp.int32(2))
    half = lax.div(group, jnp.int32(2))
    return (1 - odd) * half + odd * (size - 1 - half)


def ring_group(spot, size):
    spot = lax.rem(spot + 2 * size, jnp.int32(size))
    upper = lax.div(spot, jnp.int32(size // 2))
    return (1 - upper) * (2 * spot) + upper * (2 * (size - 1 - spot) + 1)


def front_body(dims, in_tree, out_tree, sem_tree, *refs):
    local, seqs, length, width, ff, n_grp, n_exp, rows_w = dims
    n_in, n_out = in_tree.num_leaves, out_tree.num_leaves
    I = space(jax.tree.unflatten(in_tree, refs[:n_in]))
    O = space(jax.tree.unflatten(out_tree, refs[n_in : n_in + n_out]))
    S = space(jax.tree.unflatten(sem_tree, refs[n_in + n_out :]))
    half = length // 2
    qkv = (HEADS + 2 * KV_HEADS) * HEAD_DIM
    grp, exp = lax.axis_index(GRP), lax.axis_index(EXP)
    me = grp * n_exp + exp
    y_bits = bits_of(n_exp)[1:]
    last_y = y_bits[-1]
    core_at = bit_at(exp, CORE)
    pair_at = bit_at(grp, PAIR)
    partner = {(EXP, bit): me + (1 - 2 * bit_at(exp, bit)) * bit for bit in bits_of(n_exp)}
    partner[GRP, PAIR] = me + (1 - 2 * pair_at) * (PAIR * n_exp)
    spot = ring_spot(grp, n_grp)
    around = [ring_group(spot + 1, n_grp) * n_exp + exp, ring_group(spot - 1, n_grp) * n_exp + exp]

    def send(src, dst, sems, device):
        return pltpu.make_async_remote_copy(
            src_ref=src, dst_ref=dst, send_sem=sems.at[0], recv_sem=sems.at[1],
            device_id=device, device_id_type=pl.DeviceIdType.LOGICAL,
        )

    barrier = pltpu.get_barrier_semaphore()
    greeted = list(partner.values()) + around
    for device in greeted:
        pl.semaphore_signal(barrier, inc=1, device_id=device, device_id_type=pl.DeviceIdType.LOGICAL)
    pl.semaphore_wait(barrier, len(greeted))


    hops = (n_grp // 2, n_grp - 1 - n_grp // 2)

    def ring_piece(full, origin):
        w = full.shape[2] // 2
        return full.at[origin, :, pl.ds(pl.multiple_of(core_at * w, 128), w)]

    def ring_send(kind, way, step):
        full = (O.wq, O.wo)[kind]
        origin = ring_group(spot - (step - 1) if way == 0 else spot + (step - 1), n_grp)
        piece = ring_piece(full, origin)
        return send(piece, piece, S.ring.at[kind, way, step], around[way])

    def ring_got(kind, way, step):
        full = (O.wq, O.wo)[kind]
        origin = ring_group(spot - step if way == 0 else spot + step, n_grp)
        return ring_piece(full, origin)

    def core_hand(kind, way, step):
        piece = ring_got(kind, way, step)
        return send(piece, piece, S.hand.at[kind, way, step], partner[EXP, CORE])

    def ring_step(kind, step):
        for way in range(2):
            @pl.when(step <= hops[way])
            def _():
                ring_send(kind, way, step).wait_recv()
                core_hand(kind, way, step).start()

            @pl.when(step + 1 <= hops[way])
            def _():
                ring_send(kind, way, step + 1).start()

    def ring_start(kind):
        for way in range(2):
            if hops[way]:
                ring_send(kind, way, jnp.int32(1)).start()

    def ring_end(kind):
        def body(step, carry):
            for way in range(2):
                @pl.when(step <= hops[way])
                def _():
                    core_hand(kind, way, step).wait()
                    ring_send(kind, way, step).wait_send()

            return carry

        lax.fori_loop(1, hops[0] + 1, body, 0)


    quads = 2 ** len(y_bits)
    first = seqs // 2

    def spread_send(all_ref, sems, k, axis, bit, low, count, to, part=None):
        src, dst = all_ref.at[pl.ds(low, count)], all_ref.at[pl.ds(to, count)]
        if part is not None:
            src, dst = src.at[:, part], dst.at[:, part]
        return send(src, dst, sems.at[k], partner[axis, bit])

    def y_spread(all_ref, sems, k, base, bits):
        return [spread_send(all_ref, sems, k + i, EXP, bit, base, 2**i, base + 2**i) for i, bit in enumerate(bits)]

    def core_spread(all_ref, sems, k, item):
        return spread_send(all_ref, sems, k, EXP, CORE, item, 1, item + first)

    own = [
        pltpu.make_async_copy(I.small, O.small.at[0], S.own.at[0]),
        pltpu.make_async_copy(I.wq, O.wq.at[grp], S.own.at[1]),
        pltpu.make_async_copy(I.wo, O.wo.at[grp], S.own.at[2]),
        pltpu.make_async_copy(I.dy, O.dy.at[0], S.own.at[3]),
    ]
    for copy in own:
        copy.start()
    for copy in own:
        copy.wait()
    ring_start(0)
    small = y_spread(O.small, S.small, 0, 0, y_bits)
    small.append(spread_send(O.small, S.small, len(y_bits), GRP, PAIR, 0, quads, quads))
    small.append(spread_send(O.small, S.small, len(y_bits) + 1, EXP, CORE, 0, first, first))
    dy_y = y_spread(O.dy, S.dy, 0, 0, y_bits)
    n_y = len(y_bits)
    quarter = length // 4

    def dy_z(j):
        part = pl.ds(pl.multiple_of(j * quarter, 16), quarter)
        return send(O.dy.at[0, part], O.dy.at[quads, part], S.dyz.at[j], partner[GRP, PAIR])

    def dy_on(j):
        part = pl.ds(pl.multiple_of(j * quarter, 16), quarter)
        return send(O.dy.at[quads, part], O.dy.at[quads + 1, part], S.dyy.at[j], partner[EXP, y_bits[0]])

    def dy_pass(j):
        dy_z(j).wait_recv()
        dy_on(j).start()

    dy_zy = y_spread(O.dy, S.dy, n_y, quads, y_bits)[1:]
    dy_core = [core_spread(O.dy, S.dy, 2 * n_y + 1 + i, i) for i in range(first)]
    for copy in small:
        copy.start()
        copy.wait_recv()
    dy_y[0].start()


    def slots(info, tri, sem):
        load = pltpu.make_async_copy(O.small, info, sem.at[0])
        load.start()
        load.wait()
        base = exp * (2 * local) + pair_at * local
        for r in range(0, length, 256):
            before = lax.broadcasted_iota(jnp.int32, (256, length), 0) + r
            after = lax.broadcasted_iota(jnp.int32, (256, length), 1)
            tri[r : r + 256] = jnp.where(before < after, 1.0, 0.0).astype(BF16)
        index = lax.broadcasted_iota(jnp.int32, (8, length), 0)
        name = (index + base).astype(F32)
        used = index < local

        def body(s, carry):
            member = jnp.zeros((8, length), F32)
            gate = jnp.zeros((8, length), F32)
            number = jnp.zeros((8, length), F32)
            for k in range(TOP):
                hit = (info[s, k : k + 1] == name) & used
                member = jnp.where(hit, 1.0, member)
                gate = jnp.where(hit, info[s, TOP + k : TOP + k + 1], gate)
                number = jnp.where(hit, float(k), number)
            rank = dot(member.astype(BF16), tri[...])
            O.rank[s] = jnp.where(member > 0.0, rank, -1.0).astype(jnp.int32)
            S.gate[s] = gate
            S.number[s] = number
            return carry

        lax.fori_loop(0, seqs, body, 0)

    pl.run_scoped(
        slots, pltpu.VMEM((seqs, 8, length), F32), pltpu.VMEM((length, length), BF16), pltpu.SemaphoreType.DMA((1,))
    )

    def ring_through(kind):
        def body(step, carry):
            ring_step(kind, step)
            return carry

        lax.fori_loop(1, hops[0] + 1, body, 0)

    ring_through(0)
    ring_start(1)
    ring_end(0)


    def attention(w, n1, mixed, sems):
        loads = [
            pltpu.make_async_copy(O.wq.at[i, pl.ds(0, rows_w)], w.at[pl.ds(i * rows_w, rows_w)], sems.at[0])
            for i in range(n_grp)
        ]
        for copy in loads:
            copy.start()

        lanes = -(-rows_w // 128) * 128

        def gains(buf, total):
            copies = [
                pltpu.make_async_copy(O.wq.at[i, pl.ds(rows_w, 16), pl.ds(0, lanes)], buf.at[i], sems.at[1])
                for i in range(n_grp)
            ]
            for copy in copies:
                copy.start()
            pltpu.make_async_copy(buf, buf, sems.at[1]).wait()
            total[...] = jnp.zeros_like(total)

            def body(i, carry):
                r = lax.broadcasted_iota(jnp.int32, (lanes, width), 0)
                c = lax.broadcasted_iota(jnp.int32, (lanes, width), 1)
                pick = jnp.where((c == r + i * rows_w) & (r < rows_w), 1.0, 0.0).astype(BF16)
                total[...] += dot(buf[i], pick)
                return carry

            lax.fori_loop(0, n_grp, body, 0)
            O.gains[...] = total[0:8]

        pl.run_scoped(gains, pltpu.VMEM((n_grp, 16, lanes), BF16), pltpu.VMEM((16, width), F32))
        chunk = 64

        def norm(j, carry):
            r = pl.ds(pl.multiple_of(j * chunk, chunk), chunk)
            x = I.tokens[r].astype(F32)
            inverse = lax.rsqrt(jnp.mean(x * x, axis=-1, keepdims=True) + EPSILON)
            O.inv_one[r] = inverse
            n1[r] = (x * inverse * O.gains[0:1]).astype(BF16)
            return carry

        lax.fori_loop(0, length // chunk, norm, 0)
        n1_out = pltpu.make_async_copy(n1, O.n1, sems.at[2])
        n1_out.start()
        pltpu.make_async_copy(w, w, sems.at[0]).wait()

        def heads(mask, kr, v, qr, own):
            block = 256
            for r in range(0, length, block):
                row = lax.broadcasted_iota(jnp.int32, (block, length), 0) + r
                col = lax.broadcasted_iota(jnp.int32, (block, length), 1)
                tag = I.tagc[r : r + block]
                inside = (tag == I.tagr[...]) & (tag > 0)
                mask[r : r + block] = jnp.where((col <= row) | inside, 0.0, -1e30)

            def turn(u):
                return u * I.cos[...] + pltpu.roll(u, HEAD_DIM // 2, 1) * I.sin[...]

            per = HEADS // KV_HEADS // 2
            pairs = HEADS // 2
            every = -(-hops[0] // (pairs - 2))
            for g in range(KV_HEADS):
                kv = slice(g * HEAD_DIM, (g + 1) * HEAD_DIM)
                k_at = HEADS * HEAD_DIM + g * HEAD_DIM
                v_at = k_at + KV_HEADS * HEAD_DIM
                both = dot(n1[...], w[:, k_at : k_at + HEAD_DIM])
                kr[:, kv] = turn(both).astype(BF16)
                v[:, kv] = dot(n1[...], w[:, v_at : v_at + HEAD_DIM]).astype(BF16)

                def pair(i, carry):
                    p = g * per + i
                    span = pl.ds(pl.multiple_of(p * 2 * HEAD_DIM, 2 * HEAD_DIM), 2 * HEAD_DIM)
                    q2 = dot(n1[...], w[:, span])
                    for h in range(2):
                        cols = pl.ds(pl.multiple_of((2 * p + h) * HEAD_DIM, HEAD_DIM), HEAD_DIM)
                        qr[:, cols] = turn(q2[:, h * HEAD_DIM : (h + 1) * HEAD_DIM]).astype(BF16)
                        for r in range(0, length, block):
                            keys = min(length, r + 2 * block)
                            s = dot(qr[r : r + block, cols], kr[:keys, kv], 1, 1) * SCALE
                            s = s + mask[r : r + block, :keys]
                            top = jnp.max(s, axis=-1, keepdims=True)
                            e = jnp.exp(s - top)
                            total = jnp.sum(e, axis=-1, keepdims=True)
                            probs = (e * (1.0 / total)).astype(BF16)
                            mixed[r : r + block, cols] = dot(probs, v[:keys, kv]).astype(BF16)
                            O.lse[2 * p + h, r : r + block] = top + jnp.log(total)

                    def hop(j, carry):
                        @pl.when(j <= hops[0])
                        def _():
                            ring_step(1, j)

                        @pl.when(j <= 4)
                        def _():
                            dy_z(j - 1).start()

                        @pl.when((j >= 3) & (j <= 4))
                        def _():
                            dy_pass(j - 3)

                        return carry

                    lax.fori_loop(lax.max((p - 1) * every + 1, 1), lax.max(p * every + 1, 1), hop, 0)
                    return carry

                lax.fori_loop(0, per, pair, 0)
            outs = [
                pltpu.make_async_copy(qr, O.q, own.at[0]),
                pltpu.make_async_copy(kr, O.k, own.at[1]),
                pltpu.make_async_copy(v, O.v, own.at[2]),
                pltpu.make_async_copy(mixed, O.mixed, own.at[3]),
            ]
            for copy in outs:
                copy.start()
            for copy in outs:
                copy.wait()

        pl.run_scoped(
            heads, pltpu.VMEM((length, length), F32), pltpu.VMEM((length, KV_HEADS * HEAD_DIM), BF16),
            pltpu.VMEM((length, KV_HEADS * HEAD_DIM), BF16), pltpu.VMEM((length, HEADS * HEAD_DIM), BF16),
            pltpu.SemaphoreType.DMA((4,)),
        )
        n1_out.wait()

    def projection(mixed, wo, n2, hid, sems):
        loads = [
            pltpu.make_async_copy(O.wo.at[i], wo.at[pl.ds(i * rows_w, rows_w)], sems.at[0]) for i in range(n_grp)
        ]
        for copy in loads:
            copy.start()
        pltpu.make_async_copy(wo, wo, sems.at[0]).wait()
        block = 256

        def body(j, carry):
            r = pl.ds(pl.multiple_of(j * block, block), block)
            for c in range(0, width, 512):
                hid[r, c : c + 512] = I.tokens[r, c : c + 512].astype(F32) + dot(mixed[r], wo[:, c : c + 512])

            def point(i, carry):
                r = pl.ds(pl.multiple_of(j * block + i * 64, 64), 64)
                h = hid[r]
                inverse = lax.rsqrt(jnp.mean(h * h, axis=-1, keepdims=True) + EPSILON)
                O.inv_two[r] = inverse
                n2[r] = (h * inverse * O.gains[1:2]).astype(BF16)
                return carry

            return lax.fori_loop(0, block // 64, point, carry)

        lax.fori_loop(0, length // block, body, 0)
        outs = [
            pltpu.make_async_copy(n2, O.n2.at[0], sems.at[0]),
            pltpu.make_async_copy(hid, O.hidden, sems.at[1]),
        ]
        for copy in outs:
            copy.start()
        outs[0].wait()
        dy_pass(jnp.int32(3))
        n2_start()
        outs[1].wait()


    low, high = pl.ds(0, half), pl.ds(half, half)
    steps = len(y_bits) - 1
    mid = 2**steps
    n2_pre = y_spread(O.n2, S.n2, 0, 0, y_bits[:-1])
    n2_y = spread_send(O.n2, S.n2, steps, EXP, last_y, 0, mid, mid)
    n2_z = spread_send(O.n2, S.n2, steps + 1, GRP, PAIR, 0, mid, 2 * mid)
    n2_low = spread_send(O.n2, S.n2, steps + 2, EXP, last_y, 2 * mid, mid, 3 * mid, low)
    n2_high = spread_send(O.n2, S.n2, steps + 3, GRP, PAIR, mid, mid, 3 * mid, high)
    n2_core = [core_spread(O.n2, S.n2, steps + 4 + i, i) for i in range(first)]

    def n2_start():
        for copy in n2_pre:
            copy.start()
            copy.wait_recv()
        n2_y.start()
        n2_z.start()
        for i in range(mid):
            n2_core[i].start()

    def n2_ready(step):
        for i in range(first):
            @pl.when(step == 2 * i)
            def _():
                if i == mid:
                    n2_y.wait_recv()
                    n2_high.start()
                    for j in range(mid):
                        n2_core[mid + j].start()
                    n2_z.wait_recv()
                    n2_low.start()
                    for j in range(mid):
                        n2_core[2 * mid + j].start()
                if i == 3 * mid:
                    n2_low.wait_recv()
                    n2_high.wait_recv()
                    for j in range(mid):
                        n2_core[3 * mid + j].start()

            @pl.when(step == 2 * i + 1)
            def _():
                n2_core[i].wait_recv()

    def dy_ready(step):
        for i in range(first):
            @pl.when(step == 2 * i)
            def _():
                if i == quads + 1:
                    if not dy_zy:
                        for j in range(4):
                            dy_on(jnp.int32(j)).wait_recv()
                    for j in range(1, quads):
                        dy_core[quads + j].start()

            @pl.when(step == 2 * i + 1)
            def _():
                dy_core[i].wait_recv()


    def gather(all_ref, out_ref, ready, with_slots, begin, end):
        chunk = 512

        def scoped(in_buf, out_buf, in_sem, out_sem):
            def seq_of(step):
                return lax.div(step, jnp.int32(2)) + lax.rem(step, jnp.int32(2)) * first

            def fetch(step, slot):
                return pltpu.make_async_copy(all_ref.at[seq_of(step)], in_buf.at[slot], in_sem.at[slot])

            def leaving(step, slot, e):
                row = pl.multiple_of(seq_of(step) * CAP, 16)
                return pltpu.make_async_copy(
                    out_buf.at[slot, pl.ds(e * CAP, CAP)], out_ref.at[e, pl.ds(row, CAP)], out_sem.at[slot, e]
                )

            def body(step, carry):
                slot = lax.rem(step, jnp.int32(2))
                s = seq_of(step)
                ready(step)
                fetch(step, slot).start()
                fetch(step, slot).wait()

                @pl.when(step >= begin + 2)
                def _():
                    for e in range(local):
                        leaving(step - 2, slot, e).wait()

                place = lax.broadcasted_iota(jnp.int32, (CAP, length), 0)
                ranks = O.rank[s]
                hits = [ranks[e : e + 1] == place for e in range(local)]
                if with_slots:
                    gate, number = S.gate[s], S.number[s]
                    rows = pl.ds(pl.multiple_of(s * CAP, 16), CAP)
                    for e in range(local):
                        O.gate[e, rows] = jnp.sum(jnp.where(hits[e], gate[e : e + 1], 0.0), axis=-1, keepdims=True)
                        O.choice[e, rows] = jnp.sum(
                            jnp.where(hits[e], number[e : e + 1], 0.0), axis=-1, keepdims=True
                        )
                hot = jnp.concatenate([hit.astype(F32).astype(BF16) for hit in hits], axis=0)
                for c in range(0, width, chunk):
                    out_buf[slot, :, c : c + chunk] = dot(hot, in_buf[slot, :, c : c + chunk]).astype(BF16)
                for e in range(local):
                    leaving(step, slot, e).start()
                return carry

            lax.fori_loop(begin, end, body, 0)
            for step in (end - 2, end - 1):
                for e in range(local):
                    leaving(jnp.int32(step), step % 2, e).wait()

        pl.run_scoped(
            scoped, pltpu.VMEM((2, length, width), BF16), pltpu.VMEM((2, local * CAP, width), BF16),
            pltpu.SemaphoreType.DMA((2,)), pltpu.SemaphoreType.DMA((2, local)),
        )


    def attend_and_project(mixed, sems):
        pl.run_scoped(
            lambda w, n1: attention(w, n1, mixed, sems),
            pltpu.VMEM((width, qkv), BF16), pltpu.VMEM((length, width), BF16),
        )
        for i, copy in enumerate(dy_y):
            copy.wait_recv()
            if i + 1 < n_y:
                dy_y[i + 1].start()
        for i in range(quads):
            dy_core[i].start()
        ring_end(1)
        dy_pass(jnp.int32(2))
        pl.run_scoped(
            lambda wo, n2, hid: projection(mixed, wo, n2, hid, sems),
            pltpu.VMEM((width, width), BF16), pltpu.VMEM((length, width), BF16), pltpu.VMEM((length, width), F32),
        )

    pl.run_scoped(attend_and_project, pltpu.VMEM((length, HEADS * HEAD_DIM), BF16), pltpu.SemaphoreType.DMA((3,)))
    def rest_of_dy():
        dy_core[quads].start()
        if dy_zy:
            for j in range(4):
                dy_on(jnp.int32(j)).wait_recv()
            for copy in dy_zy:
                copy.start()
                copy.wait_recv()

    gather(O.dy, O.y, dy_ready, True, 0, 2 * quads)
    gather(O.n2, O.x, n2_ready, False, 0, 2 * mid)
    rest_of_dy()
    gather(O.dy, O.y, dy_ready, True, 2 * quads, seqs)
    gather(O.n2, O.x, n2_ready, False, 2 * mid, seqs)
    for j in range(4):
        dy_z(jnp.int32(j)).wait_send()
        dy_on(jnp.int32(j)).wait_send()
    for copy in small + dy_y + dy_zy + dy_core + n2_pre + [n2_y, n2_z, n2_low, n2_high] + n2_core:
        copy.wait_send()


def front(dims, arrays):
    local, seqs, length, width, ff, n_grp, n_exp, rows_w = dims
    rows = seqs * CAP
    qkv = (HEADS + 2 * KV_HEADS) * HEAD_DIM
    kv = KV_HEADS * HEAD_DIM
    n_y = len(bits_of(n_exp)) - 1
    vmem = dict(
        rank=shape(seqs, 8, length, dtype=jnp.int32),
        gate=shape(local, rows, 1, dtype=F32),
        choice=shape(local, rows, 1, dtype=F32),
        gains=shape(8, width, dtype=F32),
        inv_one=shape(length, 1, dtype=F32),
        inv_two=shape(length, 1, dtype=F32),
        lse=shape(HEADS, length, 1, dtype=F32),
    )
    hbm = dict(
        small=shape(seqs, 8, length, dtype=F32),
        wq=shape(n_grp, rows_w + 16, qkv),
        wo=shape(n_grp, rows_w, width),
        dy=shape(seqs, length, width),
        n2=shape(seqs, length, width),
        n1=shape(length, width),
        q=shape(length, HEADS * HEAD_DIM),
        k=shape(length, kv),
        v=shape(length, kv),
        mixed=shape(length, HEADS * HEAD_DIM),
        hidden=shape(length, width, dtype=F32),
        x=shape(local, rows, width),
        y=shape(local, rows, width),
    )
    hops = n_grp // 2 + 1
    dma = pltpu.SemaphoreType.DMA
    scratch = dict(
        ring=dma((2, 2, hops, 2)),
        hand=dma((2, 2, hops, 2)),
        own=dma((4,)),
        small=dma((n_y + 2, 2)),
        dy=dma((2 * n_y + 1 + seqs // 2, 2)),
        dyz=dma((4, 2)),
        dyy=dma((4, 2)),
        n2=dma((n_y + 3 + seqs // 2, 2)),
        gate=pltpu.VMEM((seqs, 8, length), F32),
        number=pltpu.VMEM((seqs, 8, length), F32),
    )
    outs = dict(vmem, **hbm)
    in_leaves, in_tree = jax.tree.flatten(arrays)
    out_leaves, out_tree = jax.tree.flatten(outs)
    near = {id(value) for value in vmem.values()}
    sem_leaves, sem_tree = jax.tree.flatten(scratch)
    results = pl.pallas_call(
        functools.partial(front_body, dims, in_tree, out_tree, sem_tree),
        in_specs=[WHOLE] * len(in_leaves),
        out_specs=[WHOLE if id(leaf) in near else ANY for leaf in out_leaves],
        out_shape=out_leaves,
        scratch_shapes=sem_leaves,
        compiler_params=pltpu.CompilerParams(vmem_limit_bytes=VMEM, collective_id=1, has_side_effects=True),
        name="front",
    )(*in_leaves)
    return space(jax.tree.unflatten(out_tree, results))


def share_rows(width, devices):
    return -(-width // (16 * devices)) * 16


def spread(block, devices):
    rows, width = block.shape
    share = width // devices
    extra = share_rows(width, devices) - share
    if extra == 0:
        return block
    block = jnp.pad(block.reshape(rows, devices, share), ((0, 0), (0, 0), (0, extra)))
    return block.reshape(rows, -1)


def mega_plan(local, seqs, length, width, ff, n_grp, n_exp, rows_w):
    rows = seqs * CAP
    half = length // 2
    quads = seqs // 8
    wide = width + 128
    chunks = 3 * local
    qkv = (HEADS + 2 * KV_HEADS) * HEAD_DIM
    mids = [bit for bit in reversed(bits_of(n_grp)) if bit > PAIR]
    stages = len(bits_of(n_grp)) + len(bits_of(n_exp))
    share = share_rows(width, n_grp * n_exp)
    dma = pltpu.SemaphoreType.DMA

    def first_return(w):
        quad = shape(quads, half, w)
        two = shape(2, quads, half, w)
        more = [shape(quads, 2, half, w)] * 2 if quads > 1 else []
        return dict(
            came=shape(seqs // 2, length, w), kept=shape(4, quads, half, w),
            zc=two, yc=two, zcin=two, ycin=two, ylow=quad, zhigh=quad, ylowin=quad, zhighin=quad, more=more,
        )

    def second_return(w):
        one, two = shape(quads, 2, half, w), shape(2, quads, 2, half, w)
        more = [one] * 2 if quads > 1 else []
        return dict(came=shape(seqs // 2, length, w), out=two, outin=two, pair=one, pairin=one, own=one, more=more)

    def summed(w):
        return dict(
            block=shape(*[2] * stages, share, w),
            came=[shape(*[2] * (stages - 1 - i), share, w) for i in range(stages)],
        )

    gain = shape(8, width, dtype=F32)
    outs = dict(
        layer=shape(length, width),
        d_gates=shape(length, 128, dtype=F32),
        d_tokens=shape(length, width),
        final=shape(3, 2 * local, width // n_grp, ff),
        o_out=shape(share, width, dtype=F32),
        qkv_out=shape(share, qkv, dtype=F32),
        gains=gain,
        theirs=shape(chunks, width // 2, ff),
        mine=shape(chunks, width // 2, ff),
        come=[shape(chunks, width >> (i + 1), ff) for i in range(len(mids) + 1)],
        act=shape(local, rows, ff),
        d=shape(local, rows, 2 * ff),
        outs=shape(local, rows, wide),
        far=shape(seqs // 2, length, wide),
        ret=[first_return(width), second_return(wide)],
        d_hidden=shape(length, width, dtype=F32),
        sums=[summed(width), summed(qkv)],
    )
    hops = [dma((2, 2)), dma((2, 2)), dma((2, n_exp.bit_length()))]
    sems = dict(
        ret=[dict(core=dma((2, seqs // 2)), hops=hops)] * 2,
        sums=[dma((2, stages))] * 2,
        gall=dma((2, stages)),
        grad=[dma((2, chunks))] * (len(mids) + 1),
        pair=dma((2, chunks)),
        d_gate=pltpu.VMEM((local, rows, 1), F32),
        gain=pltpu.VMEM((stages + 1, 8, width), F32),
        gin=pltpu.VMEM((stages, 8, width), F32),
    )
    return outs, sems


def mega_body(dims, in_tree, out_tree, sem_tree, *refs):
    local, seqs, length, width, ff, n_grp, n_exp, rows_w = dims
    n_in, n_out = in_tree.num_leaves, out_tree.num_leaves
    I = space(jax.tree.unflatten(in_tree, refs[:n_in]))
    O = space(jax.tree.unflatten(out_tree, refs[n_in : n_in + n_out]))
    S = space(jax.tree.unflatten(sem_tree, refs[n_in + n_out :]))
    rows = seqs * CAP
    half = length // 2
    wide = width + 128
    quads = seqs // 8
    qkv = (HEADS + 2 * KV_HEADS) * HEAD_DIM
    grp, exp = lax.axis_index(GRP), lax.axis_index(EXP)
    grp_bits, exp_bits = bits_of(n_grp), bits_of(n_exp)
    me = grp * n_exp + exp
    places, partners = {}, {}
    for axis, index, bits, unit in ((GRP, grp, grp_bits, n_exp), (EXP, exp, exp_bits, 1)):
        for bit in bits:
            place = bit_at(index, bit)
            places[axis, bit] = place
            partners[axis, bit] = me + (1 - 2 * place) * (bit * unit)
    pair_at, x_at = places[GRP, PAIR], places[GRP, 1]
    y_bits = exp_bits[1:]
    mids = [bit for bit in reversed(grp_bits) if bit > PAIR]

    def send(src, dst, sems, axis, bit):
        return pltpu.make_async_remote_copy(
            src_ref=src, dst_ref=dst, send_sem=sems[0], recv_sem=sems[1],
            device_id=partners[axis, bit], device_id_type=pl.DeviceIdType.LOGICAL,
        )

    barrier = pltpu.get_barrier_semaphore()
    for partner in partners.values():
        pl.semaphore_signal(barrier, inc=1, device_id=partner, device_id_type=pl.DeviceIdType.LOGICAL)
    pl.semaphore_wait(barrier, len(partners))


    def grad_send(stage, c):
        sems = S.grad[stage]
        if stage == 0:
            src, bit = O.theirs.at[c], grp_bits[0]
        else:
            bit = mids[stage - 1]
            size = O.come[stage].shape[1]
            place = 1 - places[GRP, bit]
            src = O.come[stage - 1].at[c, pl.ds(pl.multiple_of(place * size, 16), size)]
        return send(src, O.come[stage].at[c], (sems.at[0, c], sems.at[1, c]), GRP, bit)

    def pair_send(c):
        e, k = lax.div(c, jnp.int32(3)), lax.rem(c, jnp.int32(3))
        sems = S.pair
        last = O.come[len(mids)]
        size = last.shape[1] // 2
        return send(
            last.at[c, pl.ds(pl.multiple_of((1 - pair_at) * size, 16), size)], O.final.at[k, pair_at * local + e],
            (sems.at[0, c], sems.at[1, c]), GRP, PAIR,
        )

    def grad_step(stage, c):
        grad_send(stage, c).wait_recv()
        size = O.come[stage].shape[1]
        if stage == 0:
            mine = O.mine.at[c]
        else:
            place = places[GRP, mids[stage - 1]]
            mine = O.come[stage - 1].at[c, pl.ds(pl.multiple_of(place * size, 16), size)]
        parts = 2
        piece = size // parts

        def scoped(a, b, sems):
            def load(p):
                span = pl.ds(p * piece, piece)
                return [
                    pltpu.make_async_copy(mine.at[span], a.at[p], sems.at[p, 0]),
                    pltpu.make_async_copy(O.come[stage].at[c, span], b.at[p], sems.at[p, 1]),
                ]

            for p in range(parts):
                for copy in load(p):
                    copy.start()
            stores = []
            for p in range(parts):
                for copy in load(p):
                    copy.wait()

                a[p] = a[p] + b[p]
                if stage < len(mids):
                    stores.append(pltpu.make_async_copy(
                        a.at[p], O.come[stage].at[c, pl.ds(p * piece, piece)], sems.at[p, 2]
                    ))
                    stores[-1].start()
            if stage == len(mids):
                e, k = lax.div(c, jnp.int32(3)), lax.rem(c, jnp.int32(3))
                stores = [
                    pltpu.make_async_copy(a.at[pair_at], O.final.at[k, pair_at * local + e], sems.at[0, 2]),
                    pltpu.make_async_copy(
                        a.at[1 - pair_at],
                        O.come[stage].at[c, pl.ds(pl.multiple_of((1 - pair_at) * piece, 16), piece)],
                        sems.at[1, 2],
                    ),
                ]
                for copy in stores:
                    copy.start()
            for copy in stores:
                copy.wait()

        pl.run_scoped(
            scoped, pltpu.VMEM((parts, piece, ff), BF16), pltpu.VMEM((parts, piece, ff), BF16),
            pltpu.SemaphoreType.DMA((parts, 3)),
        )
        if stage < len(mids):
            grad_send(stage + 1, c).start()
        else:
            pair_send(c).start()

    def grads(stage, first, last):
        def body(c, carry):
            grad_step(stage, c)
            return carry

        lax.fori_loop(first, last, body, 0)


    block = 448 if rows % 448 == 0 else rows
    piece = width // n_grp
    band = 384
    bands = width // band
    keep = band // 2

    slots = 2 if rows <= 1024 else 1

    def expert_loads(e, slot, x, y, w, wd, sems):
        index = pair_at * local + e
        return [
            pltpu.make_async_copy(I.x.at[e], x.at[slot], sems.at[slot, 0]),
            pltpu.make_async_copy(I.w_gate.at[index], w.at[slot, :, pl.ds(0, ff)], sems.at[slot, 1]),
            pltpu.make_async_copy(I.w_up.at[index], w.at[slot, :, pl.ds(ff, ff)], sems.at[slot, 2]),
            pltpu.make_async_copy(I.y.at[e], y.at[slot], sems.at[slot, 3]),
            pltpu.make_async_copy(I.w_down.at[index], wd.at[slot], sems.at[slot, 4]),
        ]

    def expert(e, slot, x, y, w, wd, gu, t, d, act, dx, sems, out_sems):
        def forward(b, carry):
            span = pl.ds(pl.multiple_of(b * block, 16), block)
            gu[...] = dot(x[slot, span], w[slot])
            t[...] = dot(y[slot, span], wd[slot])

            def point(i, carry):
                inner = pl.ds(pl.multiple_of(i * 64, 64), 64)
                outer = pl.ds(pl.multiple_of(b * block + i * 64, 64), 64)
                g, u = gu[inner, :ff], gu[inner, ff:]
                tt, gate = t[inner], I.gate[e, outer]
                sig = 1.0 / (1.0 + jnp.exp(-g))
                silu = g * sig
                a32 = (silu * u).astype(BF16).astype(F32)
                S.d_gate[e, outer] = jnp.sum(a32 * tt, axis=-1, keepdims=True)
                act[outer] = (a32 * gate).astype(BF16)
                da = gate * tt
                d[outer, :ff] = (da * u * sig * (1.0 + g * (1.0 - sig))).astype(BF16)
                d[outer, ff:] = (da * silu).astype(BF16)
                return carry

            return lax.fori_loop(0, block // 64, point, carry)

        lax.fori_loop(0, rows // block, forward, 0)
        stores = [
            pltpu.make_async_copy(act, O.act.at[e], out_sems.at[0]),
            pltpu.make_async_copy(d, O.d.at[e], out_sems.at[1]),
        ]
        for copy in stores:
            copy.start()

        def back(b, carry):
            span = pl.ds(pl.multiple_of(b * block, 16), block)
            for c in range(0, width, 512):
                dx[span, c : c + 512] = dot(d[span], w[slot, c : c + 512], 1, 1).astype(BF16)
            return carry

        lax.fori_loop(0, rows // block, back, 0)
        stores.append(pltpu.make_async_copy(dx, O.outs.at[e, :, pl.ds(0, width)], out_sems.at[2]))
        stores[-1].start()
        for copy in stores:
            copy.wait()

    def expert_grads(e, x, y, d, act, theirs, mine, sems):
        copies = [
            pltpu.make_async_copy(I.x.at[e], x, sems.at[0]),
            pltpu.make_async_copy(O.d.at[e], d, sems.at[1]),
            pltpu.make_async_copy(I.y.at[e], y, sems.at[2]),
            pltpu.make_async_copy(O.act.at[e], act, sems.at[3]),
        ]
        for copy in copies:
            copy.start()
        for copy in copies[:2]:
            copy.wait()

        def split(j, k, res):
            res = res.astype(BF16)
            for p in range(band // (2 * piece)):
                low = res[2 * p * piece : (2 * p + 1) * piece]
                high = res[(2 * p + 1) * piece : (2 * p + 2) * piece]
                span = pl.ds(pl.multiple_of(j * keep + p * piece, 16), piece)
                theirs[k, span] = jnp.where(x_at == 0, high, low)
                mine[k, span] = jnp.where(x_at == 0, low, high)

        def band_gate(j, carry):
            cols = pl.ds(pl.multiple_of(j * band, 128), band)
            res = dot(x[:, cols], d[...], 0, 0)
            split(j, 0, res[:, :ff])
            split(j, 1, res[:, ff:])
            return carry

        def band_down(j, carry):
            cols = pl.ds(pl.multiple_of(j * band, 128), band)
            split(j, 2, dot(y[:, cols], act[...], 0, 0))
            return carry

        def store(k, many, place):
            return [
                pltpu.make_async_copy(theirs.at[pl.ds(k, many)], O.theirs.at[pl.ds(3 * e + k, many)], sems.at[place]),
                pltpu.make_async_copy(mine.at[pl.ds(k, many)], O.mine.at[pl.ds(3 * e + k, many)], sems.at[place + 1]),
            ]

        lax.fori_loop(0, bands, band_gate, 0)
        early = store(0, 2, 0)
        for copy in early:
            copy.start()
        for copy in copies[2:]:
            copy.wait()
        lax.fori_loop(0, bands, band_down, 0)
        late = store(2, 1, 2)
        for copy in late:
            copy.start()
        for copy in early:
            copy.wait()
        for k in range(2):
            grad_send(0, 3 * e + k).start()
        for copy in late:
            copy.wait()
        grad_send(0, 3 * e + 2).start()

    def forward_of(first, last):
        def scoped(x, y, w, wd, *rest):
            sems = rest[-2]

            def load(e, slot):
                return expert_loads(e, slot, x, y, w, wd, sems)

            if slots == 2:
                for copy in load(jnp.int32(first), 0):
                    copy.start()

            def body(e, carry):
                slot = lax.rem(e - first, jnp.int32(slots))

                @pl.when(e + 1 < last + 2 - slots)
                def _():
                    for copy in load(e if slots == 1 else e + 1, 0 if slots == 1 else 1 - slot):
                        copy.start()

                for copy in load(e, slot):
                    copy.wait()
                expert(e, slot, x, y, w, wd, *rest)
                if local == 4 and first > 0:
                    grads(0, lax.max(e - 2, 0), lax.max(e - 1, 0))
                return carry

            lax.fori_loop(first, last, body, 0)

        if first == last:
            return
        pl.run_scoped(
            scoped,
            pltpu.VMEM((slots, rows, width), BF16),
            pltpu.VMEM((slots, rows, width), BF16),
            pltpu.VMEM((slots, width, 2 * ff), BF16),
            pltpu.VMEM((slots, width, ff), BF16),
            pltpu.VMEM((block, 2 * ff), F32),
            pltpu.VMEM((block, ff), F32),
            pltpu.VMEM((rows, 2 * ff), BF16),
            pltpu.VMEM((rows, ff), BF16),
            pltpu.VMEM((rows, width), BF16),
            pltpu.SemaphoreType.DMA((slots, 5)),
            pltpu.SemaphoreType.DMA((3,)),
        )

    def grads_of(first, last):
        def scoped(*scratch):
            def body(e, carry):
                expert_grads(e, *scratch)
                return carry

            lax.fori_loop(first, last, body, 0)

        pl.run_scoped(
            scoped,
            pltpu.VMEM((rows, width), BF16),
            pltpu.VMEM((rows, width), BF16),
            pltpu.VMEM((rows, 2 * ff), BF16),
            pltpu.VMEM((rows, ff), BF16),
            pltpu.VMEM((3, width // 2, ff), BF16),
            pltpu.VMEM((3, width // 2, ff), BF16),
            pltpu.SemaphoreType.DMA((4,)),
        )


    first = seqs // 2
    turns = (3, 1, 2, 0)

    def item_of(step):
        quad = lax.div(step, jnp.int32(quads))
        start = sum(jnp.where(quad == i, turn * quads, 0) for i, turn in enumerate(turns))
        return start + lax.rem(step, jnp.int32(quads))

    def collapse(tag, w, near):
        cols = pl.ds(0, w)
        r = O.ret[tag]
        low, high = pl.ds(0, half), pl.ds(half, half)
        spans = [(c, min(512, w - c)) for c in range(0, w, 512)]

        def scoped(in_buf, out_buf, came, in_sem, out_sem, came_sem):
            def coming(step, slot, e):
                s = item_of(step) + (0 if near else first)
                return pltpu.make_async_copy(
                    O.outs.at[e, pl.ds(pl.multiple_of(s * CAP, 16), CAP), cols],
                    in_buf.at[slot, pl.ds(e * CAP, CAP)],
                    in_sem.at[slot, e],
                )

            def came_load(step, slot):
                return pltpu.make_async_copy(r.came.at[item_of(step)], came.at[slot], came_sem.at[slot])

            def leaving(slot, to_low, to_high):
                return [
                    pltpu.make_async_copy(out_buf.at[slot, low], to_low, out_sem.at[slot, 0]),
                    pltpu.make_async_copy(out_buf.at[slot, high], to_high, out_sem.at[slot, 1]),
                ]

            def left(step, slot):
                for p in range(2):
                    span = out_buf.at[slot, (low, high)[p]]
                    pltpu.make_async_copy(span, span, out_sem.at[slot, p]).wait()
                if near:
                    for i, which in ((1, 1), (2, 0)) if tag == 0 else ((1, 0),):
                        @pl.when(step == (i + 1) * quads - 1)
                        def _():
                            (hop(0, 1, which) if tag == 0 else out_hop(which)).start()
                else:
                    core_send(tag, item_of(step)).start()

            for e in range(local):
                coming(jnp.int32(0), 0, e).start()

            def body(step, carry):
                slot = lax.rem(step, jnp.int32(2))

                @pl.when(step + 1 < first)
                def _():
                    for e in range(local):
                        coming(step + 1, 1 - slot, e).start()

                @pl.when(step >= 1)
                def _():
                    left(step - 1, 1 - slot)

                if near:
                    core_send(tag, item_of(step)).wait_recv()
                    came_load(step, slot).start()
                for e in range(local):
                    coming(step, slot, e).wait()
                hot = hot_rows(I.rank, item_of(step) + (0 if near else first), local, length)
                if near:
                    came_load(step, slot).wait()
                for c, span in spans:
                    total = dot(hot, in_buf[slot, :, c : c + span], 0, 0)
                    if near:
                        total = total + came[slot, :, c : c + span].astype(F32)
                    out_buf[slot, :, c : c + span] = total.astype(BF16)
                if near:
                    j = lax.rem(step, jnp.int32(quads))
                    if tag == 0:
                        ends = [
                            (r.zc.at[1, j], r.yc.at[1, j]), (r.kept.at[2, j], r.yc.at[0, j]),
                            (r.zc.at[0, j], r.kept.at[3, j]), (r.kept.at[0, j], r.kept.at[1, j]),
                        ]
                    else:
                        ends = [
                            (ref.at[j, 0], ref.at[j, 1]) for ref in (r.out.at[1], r.out.at[0], r.pair, r.own)
                        ]
                    for i, (to_low, to_high) in enumerate(ends):
                        @pl.when(lax.div(step, jnp.int32(quads)) == i)
                        def _():
                            for copy in leaving(slot, to_low, to_high):
                                copy.start()
                else:
                    to = O.far.at[item_of(step)]
                    for copy in leaving(slot, to.at[low, cols], to.at[high, cols]):
                        copy.start()
                return carry

            lax.fori_loop(0, first, body, 0)
            left(jnp.int32(first - 1), (first - 1) % 2)

        pl.run_scoped(
            scoped,
            pltpu.VMEM((2, local * CAP, w), BF16),
            pltpu.VMEM((2, length, w), BF16),
            pltpu.VMEM((2, length if near else 16, w), BF16),
            pltpu.SemaphoreType.DMA((2, local)),
            pltpu.SemaphoreType.DMA((2, 2)),
            pltpu.SemaphoreType.DMA((2,)),
        )

    def core_send(tag, s):
        sems = S.ret[tag].core
        came = O.ret[tag].came
        src = O.far.at[s, :, pl.ds(0, came.shape[2])]
        return send(src, came.at[s], (sems.at[0, s], sems.at[1, s]), EXP, CORE)

    def hop(tag, number, which):
        sems = S.ret[tag].hops[number - 1]
        pair = (sems.at[0, which], sems.at[1, which])
        r = O.ret[tag]
        src, dst = [(r.zc, r.zcin), (r.yc, r.ycin), (r.ylow, r.ylowin), (r.zhigh, r.zhighin)][2 * (number - 1) + which]
        across = (number == 1) == (which == 0)
        axis, bit = (GRP, PAIR) if across else (EXP, y_bits[-1])
        return send(src, dst, pair, axis, bit)

    def blend(pieces, w):
        def scoped(a, b, load_sem, store_sem):
            def load(i):
                slot = i % 2
                first, second = pieces[i][0]
                return [
                    pltpu.make_async_copy(first, a.at[slot], load_sem.at[slot, 0]),
                    pltpu.make_async_copy(second, b.at[slot], load_sem.at[slot, 1]),
                ]

            def store(i):
                return pltpu.make_async_copy(a.at[i % 2], pieces[i][1], store_sem.at[i % 2])

            for copy in load(0):
                copy.start()
            for i in range(len(pieces)):
                if i >= 1:
                    store(i - 1).wait()
                if i + 1 < len(pieces):
                    for copy in load(i + 1):
                        copy.start()
                for copy in load(i):
                    copy.wait()
                a[i % 2] = a[i % 2] + b[i % 2]
                store(i).start()
            store(len(pieces) - 1).wait()

        pl.run_scoped(
            scoped, pltpu.VMEM((2, half, w), BF16), pltpu.VMEM((2, half, w), BF16),
            pltpu.SemaphoreType.DMA((2, 2)), pltpu.SemaphoreType.DMA((2,)),
        )

    def out_hop(which):
        r, sems = O.ret[1], S.ret[1].hops[which]
        src, dst = ((r.out, r.outin), (r.pair, r.pairin))[which]
        axis, bit = ((EXP, y_bits[-1]), (GRP, PAIR))[which]
        return send(src, dst, (sems.at[0, 0], sems.at[1, 0]), axis, bit)

    def out_two():
        r = O.ret[1]
        out_hop(0).wait_recv()
        every = [(j, p) for j in range(quads) for p in range(2)]
        blend([((r.pair.at[j, p], r.outin.at[1, j, p]), r.pair.at[j, p]) for j, p in every], wide)
        out_hop(1).start()

    def out_end():
        r = O.ret[1]
        out_hop(1).wait_recv()
        terms = [[[r.own.at[j, p], r.outin.at[0, j, p], r.pairin.at[j, p]] for j in range(quads)] for p in range(2)]
        return last_bits(1, terms, wide)

    def return_two(tag, w):
        kept = O.ret[tag].kept
        every = range(quads)
        hop(tag, 1, 0).wait_recv()
        blend([((kept.at[2, j], O.ret[tag].zcin.at[1, j]), O.ret[tag].ylow.at[j]) for j in every], w)
        hop(tag, 2, 0).start()
        hop(tag, 1, 1).wait_recv()
        blend([((kept.at[3, j], O.ret[tag].ycin.at[1, j]), O.ret[tag].zhigh.at[j]) for j in every], w)
        hop(tag, 2, 1).start()

    def return_end(tag, w):
        for which in range(2):
            hop(tag, 2, which).wait_recv()
        kept = O.ret[tag].kept
        terms = [
            [[kept.at[0, j], O.ret[tag].zcin.at[0, j], O.ret[tag].ylowin.at[j]] for j in range(quads)],
            [[kept.at[1, j], O.ret[tag].ycin.at[0, j], O.ret[tag].zhighin.at[j]] for j in range(quads)],
        ]
        return last_bits(tag, terms, w)

    def last_bits(tag, terms, w):
        if quads == 1:
            return [terms[0][0], terms[1][0]]
        tot, came = O.ret[tag].more
        for part in range(2):
            for j in range(quads):
                a, b, c = terms[part][j]
                blend([((a, b), tot.at[j, part])], w)
                blend([((tot.at[j, part], c), tot.at[j, part])], w)
        count = quads
        for i, bit in enumerate(reversed(y_bits[:-1])):
            count //= 2
            sems = S.ret[tag].hops[2]
            copy = send(
                tot.at[pl.ds(count, count)], came.at[pl.ds(count, count)],
                (sems.at[0, i], sems.at[1, i]), EXP, bit,
            )
            copy.start()
            copy.wait()
            for j in range(count):
                for part in range(2):
                    blend([((tot.at[j, part], came.at[count + j, part]), tot.at[j, part])], w)
        return [[tot.at[0, 0]], [tot.at[0, 1]]]

    def return_close(tag):
        for number in (1, 2):
            for which in range(2):
                hop(tag, number, which).wait_send()

    def output_phase(act, w, res, sems):
        def load(e, slot):
            return [
                pltpu.make_async_copy(O.act.at[e], act.at[slot], sems.at[slot, 0]),
                pltpu.make_async_copy(I.w_down.at[pair_at * local + e], w.at[slot], sems.at[slot, 1]),
            ]

        def store(e, slot):
            return pltpu.make_async_copy(res.at[slot], O.outs.at[e], sems.at[slot, 2])

        for copy in load(0, 0):
            copy.start()

        def body(e, carry):
            slot = lax.rem(e, jnp.int32(2))

            @pl.when(e + 1 < local)
            def _():
                for copy in load(e + 1, 1 - slot):
                    copy.start()

            for copy in load(e, slot):
                copy.wait()

            @pl.when(e >= 2)
            def _():
                store(e - 2, slot).wait()

            def part(b, carry):
                span = pl.ds(pl.multiple_of(b * block, 16), block)
                for c in range(0, width, 512):
                    res[slot, span, c : c + 512] = dot(act[slot, span], w[slot, c : c + 512], 1, 1).astype(BF16)
                value = S.d_gate[e, span]
                top = value.astype(BF16).astype(F32)
                lane = lax.broadcasted_iota(jnp.int32, (block, 128), 1).astype(F32)
                choice = I.choice[e, span]
                res[slot, span, width:] = jnp.where(
                    lane == choice, top, jnp.where(lane == choice + TOP, value - top, 0.0)
                ).astype(BF16)
                return carry

            lax.fori_loop(0, rows // block, part, 0)
            store(e, slot).start()
            return carry

        lax.fori_loop(0, local, body, 0)
        for e in range(max(0, local - 2), local):
            store(e, e % 2).wait()


    order = [(EXP, bit) for bit in exp_bits] + [(GRP, bit) for bit in [1, PAIR] + mids]
    left = [(GRP, bit) for bit in reversed(grp_bits)] + [(EXP, bit) for bit in reversed(exp_bits)]
    axis_of = []
    for name in order:
        axis_of.append(left.index(name))
        left.remove(name)
    share = share_rows(width, n_grp * n_exp)

    def all_part(tag, i, place):
        block = O.sums[tag].came[i - 1] if i else O.sums[tag].block
        return block.at[(slice(None),) * axis_of[i] + (place,)]

    def all_send(tag, i):
        sems = S.sums[tag]
        return send(
            all_part(tag, i, 1 - places[order[i]]), O.sums[tag].came[i], (sems.at[0, i], sems.at[1, i]), *order[i]
        )

    def all_step(tag, i):
        all_send(tag, i).wait_recv()
        came = O.sums[tag].came[i]
        last = i + 1 == len(order)

        def scoped(a, b, *rest):
            sems = rest[-1]
            loads = [
                pltpu.make_async_copy(all_part(tag, i, places[order[i]]), a, sems.at[0]),
                pltpu.make_async_copy(came, b, sems.at[1]),
            ]
            for copy in loads:
                copy.start()
            for copy in loads:
                copy.wait()
            if last:
                rest[0][...] = a[...].astype(F32) + b[...].astype(F32)
                store = pltpu.make_async_copy(rest[0], (O.qkv_out if tag else O.o_out), sems.at[0])
            else:
                lead = len(came.shape) - 2
                inner = max(0, lead - 1)

                def body(j, carry):
                    spots, rest_of = [], j
                    for _ in range(inner):
                        spots.insert(0, lax.rem(rest_of, jnp.int32(2)))
                        rest_of = lax.div(rest_of, jnp.int32(2))
                    spots = tuple(spots)
                    a[spots] = a[spots] + b[spots]
                    return carry

                lax.fori_loop(0, 2**inner, body, 0)
                store = pltpu.make_async_copy(a, came, sems.at[0])
            store.start()
            store.wait()

        buffer = pltpu.VMEM(came.shape, BF16)
        more = [pltpu.VMEM(came.shape, F32)] if last else []
        pl.run_scoped(scoped, buffer, buffer, *more, pltpu.SemaphoreType.DMA((2,)))
        if not last:
            all_send(tag, i + 1).start()

    def gain_send(i):
        return send(S.gain.at[i], S.gin.at[i], (S.gall.at[0, i], S.gall.at[1, i]), *order[i])

    def gain_step(i):
        gain_send(i).wait_recv()
        S.gain[i + 1] = S.gain[i] + S.gin[i]
        if i + 1 < len(order):
            gain_send(i + 1).start()


    def norm_back(up, z, inverse, gain):
        normal = z * inverse
        scaled = up * gain
        mean = jnp.mean(scaled * normal, axis=-1, keepdims=True)
        return normal, inverse * (scaled - normal * mean)

    chunk_rows = 64

    def hidden_grad(terms, branch, dm, dh, wo, sems):
        for i in range(n_grp):
            pltpu.make_async_copy(I.wo.at[i], wo.at[pl.ds(i * rows_w, rows_w)], sems.at[0]).start()
        S.gain[0] = jnp.zeros((8, width), F32)

        def scoped(bufs, hid, up):
            for part in range(2):
                span = pl.ds(part * half, half)
                loads = [
                    pltpu.make_async_copy(term, bufs.at[i], sems.at[1 + i]) for i, term in enumerate(terms[part])
                ] + [
                    pltpu.make_async_copy(I.hidden.at[span], hid, sems.at[4]),
                    pltpu.make_async_copy(I.dy.at[span], up, sems.at[5]),
                ]
                for copy in loads:
                    copy.start()
                for copy in loads:
                    copy.wait()

                def body(j, carry):
                    r = pl.ds(pl.multiple_of(j * chunk_rows, chunk_rows), chunk_rows)
                    big = pl.ds(pl.multiple_of(part * half + j * chunk_rows, chunk_rows), chunk_rows)
                    d_n2 = bufs[0, r].astype(F32)
                    for i in range(1, len(terms[part])):
                        d_n2 = d_n2 + bufs[i, r].astype(F32)
                    normal, back = norm_back(d_n2, hid[r], I.inv_two[big], I.gains[1:2])
                    value = up[r].astype(F32) + back
                    dh[big] = value
                    branch[big] = value.astype(BF16)
                    S.gain[0, 1:2] = S.gain[0, 1:2] + jnp.sum(d_n2 * normal, axis=0, keepdims=True)
                    return carry

                lax.fori_loop(0, half // chunk_rows, body, 0)

        count = len(terms[0])
        pl.run_scoped(
            scoped, pltpu.VMEM((count, half, width), BF16), pltpu.VMEM((half, width), F32), pltpu.VMEM((half, width), BF16)
        )
        dh_out = pltpu.make_async_copy(dh, O.d_hidden, sems.at[1])
        dh_out.start()
        pltpu.make_async_copy(wo, wo, sems.at[0]).wait()

        def body(j, carry):
            r = pl.ds(pl.multiple_of(j * 256, 256), 256)
            for c in range(0, width, 512):
                dm[r, c : c + 512] = dot(branch[r], wo[c : c + 512], 1, 1).astype(BF16)
            return carry

        lax.fori_loop(0, length // 256, body, 0)
        dh_out.wait()

    def outer_grad(left, right, tag, buf, sems):
        dims = buf.shape[1:]
        lead = len(O.sums[tag].block.shape) - len(dims)
        steps = 2**lead
        tall = left.shape[1] // steps

        def store(j):
            spots, rest = [], j
            for _ in range(lead):
                spots.insert(0, lax.rem(rest, 2))
                rest = lax.div(rest, 2)
            slot = lax.rem(j, 2)
            return pltpu.make_async_copy(buf.at[slot], O.sums[tag].block.at[tuple(spots)], sems.at[slot])

        def body(j, carry):
            @pl.when(j >= 2)
            def _():
                store(j - 2).wait()

            cols = pl.ds(pl.multiple_of(j * tall, 128), tall)
            w = right.shape[1]
            for c in range(0, w, 512):
                part = dot(left[:, cols], right[:, c : c + 512], 0, 0).astype(BF16)
                buf[(lax.rem(j, 2),) + (slice(None),) * (len(dims) - 1) + (slice(c, c + 512),)] = part.reshape(
                    *dims[:-1], 512
                )
            store(j).start()
            return carry

        lax.fori_loop(0, steps, body, 0)
        for j in (steps - 2, steps - 1):
            store(jnp.int32(j)).wait()
        all_send(tag, 0).start()

    def attention(q, k, v, mixed, dm, dqkv, mask, dk_acc, dv_acc, dq_acc):
        for r in range(0, length, 256):
            key = lax.broadcasted_iota(jnp.int32, (256, length), 0) + r
            query = lax.broadcasted_iota(jnp.int32, (256, length), 1)
            tag = I.tagc[r : r + 256]
            inside = (tag == I.tagr[...]) & (tag > 0)
            mask[r : r + 256] = jnp.where((key <= query) | inside, 0.0, -1e30)

        def unturn(w):
            return w * I.cos[...] - pltpu.roll(w, HEAD_DIM // 2, 1) * I.sin[...]

        per = HEADS // KV_HEADS
        ones = jnp.ones((8, HEAD_DIM), F32)
        for g in range(KV_HEADS):
            kv = slice(g * HEAD_DIM, (g + 1) * HEAD_DIM)
            dk_acc[...] = jnp.zeros_like(dk_acc)
            dv_acc[...] = jnp.zeros_like(dv_acc)

            def head(i, carry):
                h = g * per + i
                cols = pl.ds(pl.multiple_of(h * HEAD_DIM, HEAD_DIM), HEAD_DIM)
                product = dm[:, cols].astype(F32) * mixed[:, cols].astype(F32)
                delta = lax.dot_general(
                    ones, product, (((1,), (1,)), ((), ())),
                    precision=lax.Precision.HIGHEST, preferred_element_type=F32,
                )[:1]
                lse = I.lse[h]
                dq_acc[...] = jnp.zeros_like(dq_acc)
                for r in range(0, length, 256):
                    start = max(0, r - 256)
                    qq, mm = q[start:, cols], dm[start:, cols]
                    kk, vv = k[r : r + 256, kv], v[r : r + 256, kv]
                    s = dot(kk, qq, 1, 1) * SCALE + mask[r : r + 256, start:]
                    p = jnp.exp(s - lse[:, start:])
                    dp = dot(vv, mm, 1, 1)
                    ds = (p * (dp - delta[:, start:])).astype(BF16)
                    dk_acc[r : r + 256] += dot(ds, qq)
                    dv_acc[r : r + 256] += dot(p.astype(BF16), mm)
                    dq_acc[start:] += dot(ds, kk, 0, 0)
                dqkv[:, cols] = unturn(dq_acc[...] * SCALE).astype(BF16)
                return carry

            lax.fori_loop(0, per, head, 0)
            first = HEADS * HEAD_DIM + g * HEAD_DIM
            dqkv[:, first : first + HEAD_DIM] = unturn(dk_acc[...] * SCALE).astype(BF16)
            first += KV_HEADS * HEAD_DIM
            dqkv[:, first : first + HEAD_DIM] = dv_acc[...].astype(BF16)

    def token_grad(dqkv, wqkv, sems):
        for i in range(n_grp):
            pltpu.make_async_copy(
                I.wqkv.at[i, pl.ds(0, rows_w)], wqkv.at[pl.ds(i * rows_w, rows_w)], sems.at[0]
            ).start()

        def scoped(dn, dh, x, res):
            pltpu.make_async_copy(wqkv, wqkv, sems.at[0]).wait()
            for part in range(2):
                span = pl.ds(part * half, half)
                loads = [
                    pltpu.make_async_copy(O.d_hidden.at[span], dh, sems.at[1]),
                    pltpu.make_async_copy(I.tokens.at[span], x, sems.at[2]),
                ]
                for copy in loads:
                    copy.start()
                for c in range(0, width, 512):
                    dn[:, c : c + 512] = dot(dqkv[part * half : (part + 1) * half], wqkv[c : c + 512], 1, 1)
                for copy in loads:
                    copy.wait()

                def body(j, carry):
                    r = pl.ds(pl.multiple_of(j * chunk_rows, chunk_rows), chunk_rows)
                    big = pl.ds(pl.multiple_of(part * half + j * chunk_rows, chunk_rows), chunk_rows)
                    d_n1 = dn[r]
                    normal, back = norm_back(d_n1, x[r].astype(F32), I.inv_one[big], I.gains[0:1])
                    res[r] = (dh[r] + back).astype(BF16)
                    S.gain[0, 0:1] = S.gain[0, 0:1] + jnp.sum(d_n1 * normal, axis=0, keepdims=True)
                    return carry

                lax.fori_loop(0, half // chunk_rows, body, 0)
                store = pltpu.make_async_copy(res, O.d_tokens.at[span], sems.at[3])
                store.start()
                store.wait()

        pl.run_scoped(
            scoped, pltpu.VMEM((half, width), F32), pltpu.VMEM((half, width), F32),
            pltpu.VMEM((half, width), BF16), pltpu.VMEM((half, width), BF16),
        )
        gain_send(0).start()

    def layer_end(terms):
        def scoped(bufs, hid, res, extra, sems):
            for part in range(2):
                span = pl.ds(part * half, half)
                loads = [
                    pltpu.make_async_copy(term, bufs.at[i], sems.at[i]) for i, term in enumerate(terms[part])
                ] + [pltpu.make_async_copy(I.hidden.at[span], hid, sems.at[3])]
                for copy in loads:
                    copy.start()
                for copy in loads:
                    copy.wait()

                def body(j, carry):
                    r = pl.ds(pl.multiple_of(j * chunk_rows, chunk_rows), chunk_rows)
                    total = bufs[0, r].astype(F32)
                    for i in range(1, len(terms[part])):
                        total = total + bufs[i, r].astype(F32)
                    res[r] = (hid[r] + total[:, :width]).astype(BF16)
                    extra[r] = total[:, width:]
                    return carry

                lax.fori_loop(0, half // chunk_rows, body, 0)
                stores = [
                    pltpu.make_async_copy(res, O.layer.at[span], sems.at[0]),
                    pltpu.make_async_copy(extra, O.d_gates.at[span], sems.at[1]),
                ]
                for copy in stores:
                    copy.start()
                for copy in stores:
                    copy.wait()

        pl.run_scoped(
            scoped, pltpu.VMEM((len(terms[0]), half, wide), BF16), pltpu.VMEM((half, width), F32),
            pltpu.VMEM((half, width), BF16), pltpu.VMEM((half, 128), F32), pltpu.SemaphoreType.DMA((4,)),
        )


    chunks = 3 * local
    done = [2 if local == 4 else 0] + [0] * len(mids)

    def pump(*upto):
        for stage, last in enumerate(upto):
            if stage >= len(done):
                continue
            if local != 4 and last < chunks:
                continue
            if done[stage] < last:
                grads(stage, done[stage], last)
                done[stage] = last

    forward_of(0, 1)
    grads_of(0, 1)
    forward_of(1, local)
    collapse(0, width, False)
    pump(3, 1)
    grads_of(1, 2)
    collapse(0, width, True)
    grads_of(2, max(2, local - 1))
    pl.run_scoped(
        output_phase,
        pltpu.VMEM((2, rows, ff), BF16),
        pltpu.VMEM((2, width, ff), BF16),
        pltpu.VMEM((2, rows, wide), BF16),
        pltpu.SemaphoreType.DMA((2, 3)),
    )
    for s in range(seqs // 2):
        core_send(0, s).wait_send()
    collapse(1, wide, False)
    return_two(0, width)
    pump(6, 3)
    collapse(1, wide, True)
    grads_of(max(2, local - 1), local)

    def backward(branch, dm, mixed, sems):
        load = pltpu.make_async_copy(I.mixed, mixed, sems.at[0])
        load.start()
        load.wait()
        terms = return_end(0, width)
        pl.run_scoped(
            functools.partial(hidden_grad, terms, branch, dm),
            pltpu.VMEM((length, width), F32), pltpu.VMEM((width, width), BF16), pltpu.SemaphoreType.DMA((6,)),
        )
        pump(7, 5)

        def out_grad(left, buf, own):
            load = pltpu.make_async_copy(I.mixed_wide, left, own.at[0])
            load.start()
            load.wait()
            outer_grad(left, branch, 0, buf, own)

        tall = share * n_grp * n_exp
        step = [2] * 3 if share > 16 else [2] * 4
        pl.run_scoped(
            out_grad, pltpu.VMEM((length, tall), BF16), pltpu.VMEM((2, *step, share, width), BF16), pltpu.SemaphoreType.DMA((2,))
        )

        def rest(dqkv):
            def first(q, k, v, *acc):
                loads = [
                    pltpu.make_async_copy(I.q, q, sems.at[0]),
                    pltpu.make_async_copy(I.k, k, sems.at[1]),
                    pltpu.make_async_copy(I.v, v, sems.at[2]),
                ]
                for copy in loads:
                    copy.start()
                for copy in loads:
                    copy.wait()
                attention(q, k, v, mixed, dm, dqkv, *acc)

            kv = KV_HEADS * HEAD_DIM
            pl.run_scoped(
                first, pltpu.VMEM((length, width), BF16), pltpu.VMEM((length, kv), BF16), pltpu.VMEM((length, kv), BF16),
                pltpu.VMEM((length, length), F32), pltpu.VMEM((length, HEAD_DIM), F32),
                pltpu.VMEM((length, HEAD_DIM), F32), pltpu.VMEM((length, HEAD_DIM), F32),
            )
            all_step(0, 0)
            pump(9, 7)

            def second(n1, buf, own):
                load = pltpu.make_async_copy(I.n1, n1, own.at[0])
                load.start()
                load.wait()
                outer_grad(n1, dqkv, 1, buf, own)

            pl.run_scoped(
                second, pltpu.VMEM((length, tall), BF16), pltpu.VMEM((2, *step, share, qkv), BF16), pltpu.SemaphoreType.DMA((2,))
            )
            pl.run_scoped(
                functools.partial(token_grad, dqkv),
                pltpu.VMEM((width, qkv), BF16), pltpu.SemaphoreType.DMA((4,)),
            )

        pl.run_scoped(rest, pltpu.VMEM((length, qkv), BF16))

    pl.run_scoped(
        backward, pltpu.VMEM((length, width), BF16), pltpu.VMEM((length, width), BF16),
        pltpu.VMEM((length, width), BF16), pltpu.SemaphoreType.DMA((3,)),
    )
    all_step(1, 0)
    gain_step(0)
    all_step(0, 1)
    pump(11, 8)
    out_two()
    gain_step(1)
    all_step(1, 1)
    pump(12, 9)
    layer_end(out_end())
    all_step(0, 2)
    gain_step(2)
    all_step(1, 2)
    pump(12, 10)
    for i in range(3, len(order)):
        all_step(0, i)
        gain_step(i)
        all_step(1, i)
        if i == 3:
            pump(12, 11)
    pump(*([chunks] * (len(mids) + 1)))

    def gains_out(sem):
        copy = pltpu.make_async_copy(S.gain.at[len(order)], O.gains, sem.at[0])
        copy.start()
        copy.wait()

    pl.run_scoped(gains_out, pltpu.SemaphoreType.DMA((1,)))

    def close(c, carry):
        for stage in range(len(mids) + 1):
            grad_send(stage, c).wait_send()
        pair_send(c).wait()
        return carry

    lax.fori_loop(0, chunks, close, 0)
    return_close(0)
    for which in range(2):
        out_hop(which).wait_send()
    for s in range(seqs // 2):
        core_send(1, s).wait_send()
    for i in range(len(order)):
        all_send(0, i).wait_send()
        all_send(1, i).wait_send()
        gain_send(i).wait_send()


def mega(dims, arrays, near):
    outs, sems = mega_plan(*dims)
    in_leaves, in_tree = jax.tree.flatten(dict(arrays, **near))
    inside = {id(value) for value in near.values()}
    out_leaves, out_tree = jax.tree.flatten(outs)
    sem_leaves, sem_tree = jax.tree.flatten(sems)
    results = pl.pallas_call(
        functools.partial(mega_body, dims, in_tree, out_tree, sem_tree),
        in_specs=[WHOLE if id(leaf) in inside else ANY for leaf in in_leaves],
        out_specs=[ANY] * len(out_leaves),
        out_shape=out_leaves,
        scratch_shapes=sem_leaves,
        compiler_params=pltpu.CompilerParams(vmem_limit_bytes=VMEM, collective_id=0, has_side_effects=True),
        name="experts_and_back",
    )(*in_leaves)
    return space(jax.tree.unflatten(out_tree, results))


def shards(
    tokens,
    cotangent,
    gate_logits,
    routes,
    piece_starts,
    piece_kinds,
    q_weight,
    k_weight,
    v_weight,
    o_weight,
    attn_gain,
    moe_gain,
    gate_weight,
    up_weight,
    down_weight,
):
    grp, exp = lax.axis_index(GRP), lax.axis_index(EXP)
    n_grp, n_exp = lax.axis_size(GRP), lax.axis_size(EXP)
    devices = n_grp * n_exp
    length, width = tokens.shape
    local = gate_weight.shape[0] // 2
    q_width, kv_width = q_weight.shape[1], k_weight.shape[1]
    rows_w = q_weight.shape[0]
    dims = (local, 2 * n_exp, length, width, gate_weight.shape[2], n_grp, n_exp, rows_w)

    gates = jax.nn.softmax(gate_logits, axis=-1)
    small = jnp.concatenate([routes.T.astype(F32), gates.T], axis=0)
    gains = jnp.pad(jnp.stack([attn_gain, moe_gain]), ((0, 14), (0, q_width + 2 * kv_width - rows_w)))
    shard = jnp.concatenate([jnp.concatenate([q_weight, k_weight, v_weight], axis=1), gains], axis=0)
    cosine, sine = rope_tables(length)
    tags = piece_tags(piece_starts[0], piece_kinds[0], length)
    tagc, tagr = tags.reshape(length, 1), tags.reshape(1, length)

    a = front(
        dims,
        dict(
            tokens=tokens, dy=cotangent, small=small, wq=shard, wo=o_weight,
            cos=cosine, sin=sine, tagc=tagc, tagr=tagr,
        ),
    )
    r = mega(
        dims,
        dict(
            x=a.x, y=a.y, w_gate=gate_weight, w_up=up_weight, w_down=down_weight, hidden=a.hidden,
            dy=cotangent, wo=a.wo, mixed=a.mixed, q=a.q, k=a.k, v=a.v, wqkv=a.wq, tokens=tokens,
            n1=spread(a.n1, devices), mixed_wide=spread(a.mixed, devices),
        ),
        dict(
            gate=a.gate, choice=a.choice, rank=a.rank, inv_one=a.inv_one, inv_two=a.inv_two, gains=a.gains,
            lse=a.lse.reshape(HEADS, 1, length), cos=cosine, sin=sine, tagc=tagc, tagr=tagr,
        ),
    )
    d_gates = r.d_gates[:, :TOP] + r.d_gates[:, TOP : 2 * TOP]
    logits_grad = gates * (d_gates - jnp.sum(gates * d_gates, axis=-1, keepdims=True))
    share = width // devices
    own = lax.dynamic_slice_in_dim(r.gains, (grp * n_exp + exp) * share, share, 1)
    return (
        r.layer,
        r.d_tokens,
        logits_grad,
        r.qkv_out[:share, :q_width],
        r.qkv_out[:share, q_width : q_width + kv_width],
        r.qkv_out[:share, q_width + kv_width :],
        r.o_out[:share],
        own[0],
        own[1],
        *[r.final[kind].astype(F32) for kind in range(3)],
    )


def solution(mesh):
    rows = P((GRP, EXP), None)
    placed = (rows,) * 6 + (P(GRP, None),) * 4 + (P(GRP),) * 2 + (P(EXP, None, None),) * 3
    outs = (rows,) * 7 + (P((GRP, EXP)),) * 2 + (P(EXP, GRP, None),) * 3
    return jax.shard_map(shards, mesh=mesh, in_specs=placed, out_specs=outs, check_vma=False)
```
